32 devices in a mesh: view: 4 (over y, x), sent: 4 (over z), col: 2 (over core).
Axes of the slice: x: 2, y: 2, z: 4, core: 2. Of those that a mesh axis runs over, the one named last changes fastest.
Arguments:
- sketched: bfloat16 [12, 4096, 2048], P('view', 'sent', 'col')
- widths: int32 [12], P('view'), may hold values from 256 to 2048, as said below
- inv_factor: float32 [12, 2048, 2048], P('view', 'sent', 'col'), as said below
- shared: bfloat16 [4096, 256], P('sent'), may hold values from -6 to 6
Outputs:
- loadings: float32 [12, 2048, 256], P('view', 'col')
- updated: float32 [4096, 256], P('sent')
The draws below stay inside these ranges and needn't reach their ends.
Inputs may be any that keep to these rules, and one draw needn't show every extreme that they name: `widths`: every width is a multiple of 128; in every draw one view has width 2048 and another 2 * 128. Each inv_factor[j] is lower triangular with diagonal entries of 1 to 2.
All inputs are finite; a program needn't handle non-finite values.
Results may differ from the reference program's by a relative error of at most 0.0026.
Values sent between devices are 32-bit elements; how exact they have to be, the bound alone decides.
No kernel may reach another device: no remote copies, remote signals or barrier semaphores. Data moves between devices by JAX's collectives and lax.ppermute only.
A program may use at most 128 MiB of HBM per device.

```python
import math
import jax
import jax.numpy as jnp
from jax import lax

DMAX = 2048
K = 256
ROWS_DEV = 1024
VIEWS = 12
ROWS = 4096
RB = 512
N_SENT = 4


def draw_sketched(key, part):
    first, second = jax.random.split(key, 2)
    values = jnp.clip(jax.random.normal(first, (VIEWS, ROWS, DMAX), jnp.float32), -6.0, 6.0)
    blocks = ROWS // ROWS_DEV
    block_pos = (jnp.arange(ROWS) // ROWS_DEV).astype(jnp.float32)
    rising = jnp.exp(jnp.log(4.0) * block_pos / max(blocks - 1, 1))
    rough = jax.random.uniform(second, (VIEWS, ROWS, 1), jnp.float32, 0.7, 1.4)
    return (values * rough * rising[None, :, None]).astype(jnp.bfloat16)


def draw_widths(key, part):
    step = DMAX // 16
    first, second, third = jax.random.split(key, 3)
    base = jax.random.randint(first, (VIEWS,), 2, 17) * step
    top = jax.random.randint(second, (), 0, VIEWS)
    low = (top + 1 + jax.random.randint(third, (), 0, VIEWS - 1)) % VIEWS
    return base.at[top].set(DMAX).at[low].set(2 * step).astype(jnp.int32)


def draw_inv_factor(key, part):
    first, second = jax.random.split(key, 2)
    diag = jax.random.uniform(first, (VIEWS, DMAX, 1), jnp.float32, 1.0, 2.0)
    off = jax.random.normal(second, (VIEWS, DMAX, DMAX), jnp.float32)
    rowpos = jnp.arange(DMAX)[:, None]
    colpos = jnp.arange(DMAX)[None, :]
    rowscale = 0.5 / jnp.sqrt(rowpos.astype(jnp.float32) + 1.0)
    lower_part = jnp.where(colpos < rowpos, off * rowscale[None], 0.0)
    diagonal = jnp.where(colpos == rowpos, 1.0, 0.0)[None] * diag
    return (lower_part + diagonal).astype(jnp.float32)


def levels(own_key, extent, pieces, low, largest):
    factor_of = 1.0
    for axis_at, parts in pieces:
        steps = jax.random.uniform(jax.random.fold_in(jax.random.fold_in(own_key, 6), axis_at), (parts,), jnp.float32, low / len(pieces), largest / len(pieces))
        factor_of = factor_of * jnp.repeat(jnp.exp(steps), extent[axis_at] // parts).reshape((-1,) + (1,) * (len(extent) - 1 - axis_at))
    return factor_of


def noise(rng, shape, scale, bound, shards=(), held_as=jnp.bfloat16):
    entries = scale * jax.random.normal(rng, shape, jnp.float32)
    if shards:
        entries = entries * levels(rng, shape, shards, -0.22, 0.18)
    return jnp.clip(entries, -bound, bound).astype(held_as)


def setup_inputs(seed: int = 0) -> dict:
    seeds = jax.random.split(jax.random.key(seed), 5)
    return {
        "sketched": draw_sketched(jax.random.fold_in(seeds[4], 71), 0),
        "widths": draw_widths(jax.random.fold_in(seeds[4], 71), 0),
        "inv_factor": draw_inv_factor(jax.random.fold_in(seeds[4], 71), 0),
        "shared": noise(seeds[3], (ROWS, K), 1.0, 6.0, ((0, 4),)),
    }


def reference(sketched, widths, inv_factor, shared):
    scale = 1.0 / math.sqrt(ROWS)
    shared_f = shared.astype(jnp.float32).reshape(N_SENT, ROWS_DEV, K)
    high = lax.Precision.HIGHEST

    def one_view(args):
        feats, width, inverse = args
        keep = (jnp.arange(DMAX) < width).astype(jnp.float32)[:, None]
        blocks = feats.astype(jnp.float32).reshape(N_SENT, ROWS_DEV, DMAX)
        terms = jnp.einsum('srd,srk->sdk', blocks, shared_f) * scale
        proj = lax.optimization_barrier(jnp.sum(terms, axis=0)) * keep
        half = jnp.dot(inverse, proj, precision=high) * keep
        back = jnp.einsum('sid,sik->sdk', inverse.reshape(N_SENT, RB, DMAX), half.reshape(N_SENT, RB, K), precision=high)
        load = lax.optimization_barrier(jnp.sum(back, axis=0)) * keep
        contrib = jnp.dot(feats.astype(jnp.float32), load.astype(jnp.bfloat16).astype(jnp.float32), preferred_element_type=jnp.float32)
        return (load, contrib)
    loadings, contribs = lax.map(one_view, (sketched, widths, inv_factor))
    merged = lax.optimization_barrier(jnp.sum(contribs, axis=0))
    gram = lax.dot_general(merged, merged, (((0,), (0,)), ((), ())), precision=high)
    lower = jnp.linalg.cholesky(gram)
    updated = lax.linalg.triangular_solve(lower, merged, left_side=False, lower=True, transpose_a=True) * math.sqrt(ROWS)
    return (loadings, updated)
```

```python
import math

import jax
import jax.numpy as jnp
from jax import lax
from jax.sharding import PartitionSpec as P

CHUNK = 256


def line_sum(term, first, spread, sent_index, col_index):
    places, cores = 4, len(first)

    def hop(value, pairs):
        perm = [
            (a * cores + c, b * cores + c) for c in range(cores) for a, b in pairs(first[c])
        ]
        return lax.ppermute(value, ("sent", "col"), perm)

    if spread:
        inward = lambda f: [(0, 1)] + ([(3, 2)] if f < 3 else [])
        across = lambda f: [(1, 2)] + ([(2, 1)] if f <= 1 else [])
        outward = lambda f: [(2, 3)] + ([(1, 0)] if f <= 0 else [])
    else:
        inward = lambda f: [(3, 2)] + ([(0, 1)] if f <= 0 else [])
        across = lambda f: [(2, 1)] + ([(1, 2)] if f <= 1 else [])
        outward = lambda f: [(1, 0)] + ([(2, 3)] if f <= 2 else [])
    pair = term + hop(term, inward)
    total = pair + hop(pair, across)
    outer = hop(total, outward)
    at_end = jnp.asarray([f == places - 1 for f in first])[col_index] & (sent_index == places - 1)
    outer = jnp.where(at_end, outer + term, outer)
    is_inner = (sent_index == 1) | (sent_index == 2)
    return jnp.where(is_inner, total, outer)


def shards(sketched, widths, inv_factor, shared):
    view_count, row_count, col_half = sketched.shape
    factor_rows = inv_factor.shape[1]
    sent_size = lax.axis_size("sent")
    view_size = lax.axis_size("view")
    core_count = lax.axis_size("col")
    total_rows = row_count * sent_size
    scale = 1.0 / math.sqrt(total_rows)
    high = lax.Precision.HIGH
    highest = lax.Precision.HIGHEST
    col_index = lax.axis_index("col")
    sent_index = lax.axis_index("sent")
    col_pos = col_index * col_half + jnp.arange(col_half)
    keep_cols = (col_pos[None, :] < widths[:, None]).astype(jnp.float32)[:, :, None]
    row_pos = sent_index * factor_rows + jnp.arange(factor_rows)
    keep_rows = (row_pos[None, :] < widths[:, None]).astype(jnp.float32)[:, :, None]
    use_line = sent_size == 4 and core_count == 2 and col_half % CHUNK == 0

    def sum_sent(term, spread):
        if not use_line:
            return lax.psum(term, "sent")
        parts = []
        for q in range(col_half // CHUNK):
            first = [(c * col_half + q * CHUNK) // factor_rows for c in range(core_count)]
            part = term[q * CHUNK : (q + 1) * CHUNK]
            parts.append(line_sum(part, first, spread, sent_index, col_index))
        return jnp.concatenate(parts, axis=0)

    loads = []
    contrib = jnp.zeros((row_count, shared.shape[1]), jnp.float32)
    for j in range(view_count):
        term = lax.dot_general(
            sketched[j], shared, (((0,), (0,)), ((), ())), preferred_element_type=jnp.float32
        ) * scale
        proj = sum_sent(term, True) * keep_cols[j]
        half_part = jnp.dot(inv_factor[j], proj, precision=high)
        if use_line:
            perm = [
                (s * 2 + c, s * 2 + 1 - c)
                for s in range(sent_size)
                for c in range(2)
                if (s + 1) * factor_rows > col_half
            ]
            half = half_part + lax.ppermute(half_part, ("sent", "col"), perm)
        else:
            half = lax.psum(half_part, "col")
        half = half * keep_rows[j]
        back = lax.dot_general(
            inv_factor[j], half, (((0,), (0,)), ((), ())), precision=high,
            preferred_element_type=jnp.float32,
        )
        load = sum_sent(back, False) * keep_cols[j]
        loads.append(load)
        contrib = contrib + jnp.dot(
            sketched[j], load.astype(jnp.bfloat16), preferred_element_type=jnp.float32
        )
    loadings = jnp.stack(loads)

    if view_size == 4 and core_count == 2:
        part_rows = row_count // 2
        near = lambda bit: [(v, v ^ bit) for v in range(view_size)]
        swap = [(0, 1), (1, 0)]
        mine = lax.dynamic_slice_in_dim(contrib, col_index * part_rows, part_rows)
        other = lax.dynamic_slice_in_dim(contrib, (1 - col_index) * part_rows, part_rows)
        mine = mine + lax.ppermute(other, "col", swap)
        upper, lower_part = mine[: part_rows // 2], mine[part_rows // 2 :]
        upper = upper + lax.ppermute(upper, "view", near(1))
        lower_part = lower_part + lax.ppermute(lower_part, "view", near(2))
        upper = upper + lax.ppermute(upper, "view", near(2))
        lower_part = lower_part + lax.ppermute(lower_part, "view", near(1))
        mine = jnp.concatenate([upper, lower_part])
        other = lax.ppermute(mine, "col", swap)
        merged = jnp.concatenate(
            [jnp.where(col_index == 0, mine, other), jnp.where(col_index == 0, other, mine)]
        )
    else:
        merged = lax.psum(contrib, ("view", "col"))

    if core_count == 2 and sent_size & (sent_size - 1) == 0:
        width = merged.shape[1] // 2
        own = lax.dynamic_slice_in_dim(merged, col_index * width, width, axis=1)
        gram = lax.dot_general(merged, own, (((0,), (0,)), ((), ())), precision=highest)
        bit = 1
        while bit < sent_size:
            gram = gram + lax.ppermute(gram, "sent", [(s, s ^ bit) for s in range(sent_size)])
            bit *= 2
        other = lax.ppermute(gram, "col", [(0, 1), (1, 0)])
        gram = jnp.concatenate(
            [jnp.where(col_index == 0, gram, other), jnp.where(col_index == 0, other, gram)],
            axis=1,
        )
    else:
        gram = lax.dot_general(merged, merged, (((0,), (0,)), ((), ())), precision=highest)
        gram = lax.psum(gram, "sent")
    lower = jnp.linalg.cholesky(gram)
    updated = lax.linalg.triangular_solve(
        lower, merged, left_side=False, lower=True, transpose_a=True
    ) * math.sqrt(total_rows)
    return (loadings, updated)


def solution(mesh):
    return jax.shard_map(
        shards,
        mesh=mesh,
        in_specs=(P("view", "sent", "col"), P("view"), P("view", "sent", "col"), P("sent", None)),
        out_specs=(P("view", "col", None), P("sent", None)),
        check_vma=False,
    )
```

```python
import math

import jax
import jax.numpy as jnp
from jax import lax
from jax.sharding import PartitionSpec as P

CHUNK = 512


def line_chain(terms, firsts, spread, sent_index, col_index):
    count, cores = len(terms), len(firsts[0])
    if spread:
        up_ok = (lambda f: True, lambda f: True, lambda f: True)
        down_ok = (lambda f: f < 3, lambda f: f <= 1, lambda f: f <= 0)
    else:
        up_ok = (lambda f: f <= 0, lambda f: f <= 1, lambda f: f <= 2)
        down_ok = (lambda f: True, lambda f: True, lambda f: True)

    def hop(step, choices, ok, hops):
        present = [i for i in range(3) if 0 <= step - i < count]
        value = choices[present[0]]
        for i in present[1:]:
            value = jnp.where(sent_index == hops[i][0], choices[i], value)
        perm = [
            (hops[i][0] * cores + c, hops[i][1] * cores + c)
            for i in present
            for c in range(cores)
            if ok[i](firsts[step - i][c])
        ]
        return lax.ppermute(value, ("sent", "col"), perm) if perm else jnp.zeros_like(value)

    low = sent_index <= 1
    inner = (sent_index == 1) | (sent_index == 2)
    pairs, totals, finals = {}, {}, []
    for step in range(count + 2):
        choices = [terms[step] if step < count else None, pairs.get(step - 1), totals.get(step - 2)]
        up = hop(step, choices, up_ok, ((0, 1), (1, 2), (2, 3)))
        down = hop(step, choices, down_ok, ((3, 2), (2, 1), (1, 0)))
        near, far = jnp.where(low, up, down), jnp.where(low, down, up)
        if step < count:
            pairs[step] = terms[step] + near
        if 0 <= step - 1 < count:
            totals[step - 1] = pairs[step - 1] + far
        k = step - 2
        if k >= 0:
            at_end = jnp.asarray([f == 3 for f in firsts[k]])[col_index] & (sent_index == 3)
            far = jnp.where(at_end, far + terms[k], far)
            finals.append(jnp.where(inner, totals[k], far))
    return finals


def shards(sketched, widths, inv_factor, shared):
    view_count, row_count, col_half = sketched.shape
    factor_rows = inv_factor.shape[1]
    sent_size = lax.axis_size("sent")
    view_size = lax.axis_size("view")
    core_count = lax.axis_size("col")
    total_rows = row_count * sent_size
    scale = 1.0 / math.sqrt(total_rows)
    high = lax.Precision.HIGH
    highest = lax.Precision.HIGHEST
    col_index = lax.axis_index("col")
    sent_index = lax.axis_index("sent")
    col_pos = col_index * col_half + jnp.arange(col_half)
    keep_cols = (col_pos[None, :] < widths[:, None]).astype(jnp.float32)[:, :, None]
    row_pos = sent_index * factor_rows + jnp.arange(factor_rows)
    keep_rows = (row_pos[None, :] < widths[:, None]).astype(jnp.float32)[:, :, None]
    use_line = sent_size == 4 and core_count == 2 and col_half % CHUNK == 0

    chunk = CHUNK if use_line else col_half
    per_view = col_half // chunk
    slots = [(j, q) for j in range(view_count) for q in range(per_view)]
    firsts = [
        [(c * col_half + q * chunk) // factor_rows for c in range(core_count)] for _, q in slots
    ]

    def sum_sent(terms, spread):
        if use_line:
            return line_chain(terms, firsts, spread, sent_index, col_index)
        return [lax.psum(t, "sent") for t in terms]

    def columns(array, j, q):
        return array[j, :, q * chunk : (q + 1) * chunk]

    def keep_of(j, q):
        return keep_cols[j, q * chunk : (q + 1) * chunk]

    down = (((0,), (0,)), ((), ()))
    terms = [
        lax.dot_general(columns(sketched, j, q), shared, down, preferred_element_type=jnp.float32)
        * scale
        for j, q in slots
    ]
    proj = [p * keep_of(*slot) for p, slot in zip(sum_sent(terms, True), slots)]
    halves = []
    for j in range(view_count):
        half_part = 0.0
        for q in range(per_view):
            half_part += jnp.dot(columns(inv_factor, j, q), proj[j * per_view + q], precision=high)
        if use_line:
            perm = [
                (s * 2 + c, s * 2 + 1 - c)
                for s in range(sent_size)
                for c in range(2)
                if (s + 1) * factor_rows > col_half
            ]
            half = half_part + lax.ppermute(half_part, ("sent", "col"), perm)
        else:
            half = lax.psum(half_part, "col")
        halves.append(half * keep_rows[j])
    backs = [
        lax.dot_general(
            columns(inv_factor, j, q), halves[j], down, precision=high,
            preferred_element_type=jnp.float32,
        )
        for j, q in slots
    ]
    loads = [b * keep_of(*slot) for b, slot in zip(sum_sent(backs, False), slots)]
    contrib = 0.0
    for load, (j, q) in zip(loads, slots):
        contrib += jnp.dot(
            columns(sketched, j, q), load.astype(jnp.bfloat16), preferred_element_type=jnp.float32
        )
    loadings = jnp.concatenate(loads).reshape(view_count, col_half, -1)

    if view_size == 4 and core_count == 2:
        part_rows = row_count // 2
        near = lambda bit: [(v, v ^ bit) for v in range(view_size)]
        swap = [(0, 1), (1, 0)]
        mine = lax.dynamic_slice_in_dim(contrib, col_index * part_rows, part_rows)
        other = lax.dynamic_slice_in_dim(contrib, (1 - col_index) * part_rows, part_rows)
        mine = mine + lax.ppermute(other, "col", swap)
        upper, lower_part = mine[: part_rows // 2], mine[part_rows // 2 :]
        upper = upper + lax.ppermute(upper, "view", near(1))
        lower_part = lower_part + lax.ppermute(lower_part, "view", near(2))
        upper = upper + lax.ppermute(upper, "view", near(2))
        lower_part = lower_part + lax.ppermute(lower_part, "view", near(1))
        mine = jnp.concatenate([upper, lower_part])
        other = lax.ppermute(mine, "col", swap)
        merged = jnp.concatenate(
            [jnp.where(col_index == 0, mine, other), jnp.where(col_index == 0, other, mine)]
        )
    else:
        merged = lax.psum(contrib, ("view", "col"))

    if core_count == 2 and sent_size & (sent_size - 1) == 0:
        width = merged.shape[1] // 2
        own = lax.dynamic_slice_in_dim(merged, col_index * width, width, axis=1)
        gram = lax.dot_general(merged, own, (((0,), (0,)), ((), ())), precision=highest)
        bit = 1
        while bit < sent_size:
            gram = gram + lax.ppermute(gram, "sent", [(s, s ^ bit) for s in range(sent_size)])
            bit *= 2
        other = lax.ppermute(gram, "col", [(0, 1), (1, 0)])
        gram = jnp.concatenate(
            [jnp.where(col_index == 0, gram, other), jnp.where(col_index == 0, other, gram)],
            axis=1,
        )
    else:
        gram = lax.dot_general(merged, merged, (((0,), (0,)), ((), ())), precision=highest)
        gram = lax.psum(gram, "sent")
    lower = jnp.linalg.cholesky(gram)
    updated = lax.linalg.triangular_solve(
        lower, merged, left_side=False, lower=True, transpose_a=True
    ) * math.sqrt(total_rows)
    return (loadings, updated)


def solution(mesh):
    return jax.shard_map(
        shards,
        mesh=mesh,
        in_specs=(P("view", "sent", "col"), P("view"), P("view", "sent", "col"), P("sent", None)),
        out_specs=(P("view", "col", None), P("sent", None)),
        check_vma=False,
    )
```

```python
import math

import jax
import jax.numpy as jnp
from jax import lax
from jax.sharding import PartitionSpec as P

CHUNK = 256
LANES = 2


def line_chain(terms, firsts, spread, sent_index, col_index):
    count, cores = len(terms), len(firsts[0])
    always = lambda f: True
    if spread:
        inward = {(0, 1): always, (3, 2): lambda f: f < 3}
        across = {(1, 2): always, (2, 1): lambda f: f <= 1}
        outward = {(2, 3): always, (1, 0): lambda f: f <= 0}
    else:
        inward = {(3, 2): always, (0, 1): lambda f: f <= 0}
        across = {(2, 1): always, (1, 2): lambda f: f <= 1}
        outward = {(1, 0): always, (2, 3): lambda f: f <= 2}

    def pairs_of(k, hops):
        if not 0 <= k < count:
            return []
        return [
            (a * cores + c, b * cores + c)
            for c in range(cores)
            for (a, b), wanted in hops.items()
            if wanted(firsts[k][c])
        ]

    inner = (sent_index == 1) | (sent_index == 2)
    pairs, totals, finals = {}, {}, []
    for step in range(count + 2):
        if step < 2:
            ends = terms[step] if step < count else jnp.zeros_like(terms[0])
        elif step < count:
            ends = jnp.where(inner, totals[step - 2], terms[step])
        else:
            ends = totals[step - 2]
        perm = pairs_of(step, inward) + pairs_of(step - 2, outward)
        ends_in = lax.ppermute(ends, ("sent", "col"), perm)
        if 0 <= step - 1 < count:
            perm = pairs_of(step - 1, across)
            middle_in = lax.ppermute(pairs[step - 1], ("sent", "col"), perm)
            totals[step - 1] = pairs[step - 1] + middle_in
        if step < count:
            pairs[step] = terms[step] + ends_in
        k = step - 2
        if k >= 0:
            at_end = jnp.asarray([f == 3 for f in firsts[k]])[col_index] & (sent_index == 3)
            outer = jnp.where(at_end, ends_in + terms[k], ends_in)
            finals.append(jnp.where(inner, ends, outer))
    return finals


def shards(sketched, widths, inv_factor, shared):
    view_count, row_count, col_half = sketched.shape
    factor_rows = inv_factor.shape[1]
    sent_size = lax.axis_size("sent")
    view_size = lax.axis_size("view")
    core_count = lax.axis_size("col")
    total_rows = row_count * sent_size
    scale = 1.0 / math.sqrt(total_rows)
    high = lax.Precision.HIGH
    highest = lax.Precision.HIGHEST
    col_index = lax.axis_index("col")
    sent_index = lax.axis_index("sent")
    col_pos = col_index * col_half + jnp.arange(col_half)
    keep_cols = (col_pos[None, :] < widths[:, None]).astype(jnp.float32)[:, :, None]
    row_pos = sent_index * factor_rows + jnp.arange(factor_rows)
    keep_rows = (row_pos[None, :] < widths[:, None]).astype(jnp.float32)[:, :, None]
    use_line = sent_size == 4 and core_count == 2 and col_half % (LANES * CHUNK) == 0

    chunk = CHUNK if use_line else col_half
    per_view = col_half // chunk
    slots = [(j, q) for j in range(view_count) for q in range(per_view)]
    firsts = [
        [(c * col_half + q * chunk) // factor_rows for c in range(core_count)] for _, q in slots
    ]

    def sum_sent(terms, spread):
        if use_line:
            sums = [None] * len(terms)
            for lane in range(LANES):
                sums[lane::LANES] = line_chain(
                    terms[lane::LANES], firsts[lane::LANES], spread, sent_index, col_index
                )
            return sums
        return [lax.psum(t, "sent") for t in terms]

    def columns(array, j, q):
        return array[j, :, q * chunk : (q + 1) * chunk]

    def keep_of(j, q):
        return keep_cols[j, q * chunk : (q + 1) * chunk]

    down = (((0,), (0,)), ((), ()))
    terms = []
    for j in range(view_count):
        whole = scale * lax.dot_general(
            sketched[j], shared, down, preferred_element_type=jnp.float32
        )
        terms += [whole[q * chunk : (q + 1) * chunk] for q in range(per_view)]
    proj = [p * keep_of(*slot) for p, slot in zip(sum_sent(terms, True), slots)]
    halves = []
    for j in range(view_count):
        own = jnp.concatenate(proj[j * per_view : (j + 1) * per_view])
        half_part = jnp.dot(inv_factor[j], own, precision=high)
        if use_line:
            perm = [
                (s * 2 + c, s * 2 + 1 - c)
                for s in range(sent_size)
                for c in range(2)
                if (s + 1) * factor_rows > col_half
            ]
            half = half_part + lax.ppermute(half_part, ("sent", "col"), perm)
        else:
            half = lax.psum(half_part, "col")
        halves.append(half * keep_rows[j])
    backs = []
    for j in range(view_count):
        whole = lax.dot_general(
            inv_factor[j], halves[j], down, precision=high, preferred_element_type=jnp.float32
        )
        backs += [whole[q * chunk : (q + 1) * chunk] for q in range(per_view)]
    loads = [b * keep_of(*slot) for b, slot in zip(sum_sent(backs, False), slots)]
    loadings = jnp.concatenate(loads).reshape(view_count, col_half, -1)
    contrib = 0.0
    for j in range(view_count):
        whole = jnp.concatenate(loads[j * per_view : (j + 1) * per_view]).astype(jnp.bfloat16)
        contrib += jnp.dot(sketched[j], whole, preferred_element_type=jnp.float32)

    if view_size == 4 and core_count == 2:
        part_rows = row_count // 2
        near = lambda bit: [(v, v ^ bit) for v in range(view_size)]
        swap = [(0, 1), (1, 0)]
        mine = lax.dynamic_slice_in_dim(contrib, col_index * part_rows, part_rows)
        other = lax.dynamic_slice_in_dim(contrib, (1 - col_index) * part_rows, part_rows)
        mine = mine + lax.ppermute(other, "col", swap)
        upper, lower_part = mine[: part_rows // 2], mine[part_rows // 2 :]
        upper = upper + lax.ppermute(upper, "view", near(1))
        lower_part = lower_part + lax.ppermute(lower_part, "view", near(2))
        upper = upper + lax.ppermute(upper, "view", near(2))
        lower_part = lower_part + lax.ppermute(lower_part, "view", near(1))
        mine = jnp.concatenate([upper, lower_part])
        other = lax.ppermute(mine, "col", swap)
        merged = jnp.concatenate(
            [jnp.where(col_index == 0, mine, other), jnp.where(col_index == 0, other, mine)]
        )
    else:
        merged = lax.psum(contrib, ("view", "col"))

    if core_count == 2 and sent_size & (sent_size - 1) == 0:
        width = merged.shape[1] // 2
        own = lax.dynamic_slice_in_dim(merged, col_index * width, width, axis=1)
        gram = lax.dot_general(merged, own, (((0,), (0,)), ((), ())), precision=highest)
        bit = 1
        while bit < sent_size:
            gram = gram + lax.ppermute(gram, "sent", [(s, s ^ bit) for s in range(sent_size)])
            bit *= 2
        other = lax.ppermute(gram, "col", [(0, 1), (1, 0)])
        gram = jnp.concatenate(
            [jnp.where(col_index == 0, gram, other), jnp.where(col_index == 0, other, gram)],
            axis=1,
        )
    else:
        gram = lax.dot_general(merged, merged, (((0,), (0,)), ((), ())), precision=highest)
        gram = lax.psum(gram, "sent")
    lower = jnp.linalg.cholesky(gram)
    updated = lax.linalg.triangular_solve(
        lower, merged, left_side=False, lower=True, transpose_a=True
    ) * math.sqrt(total_rows)
    return (loadings, updated)


def solution(mesh):
    return jax.shard_map(
        shards,
        mesh=mesh,
        in_specs=(P("view", "sent", "col"), P("view"), P("view", "sent", "col"), P("sent", None)),
        out_specs=(P("view", "col", None), P("sent", None)),
        check_vma=False,
    )
```

```python
import math

import jax
import jax.numpy as jnp
from jax import lax
from jax.sharding import PartitionSpec as P

CHUNK = 256
LANES = 2


class Line:
    def __init__(self, lanes, sent_index, col_index):
        self.lanes, self.sent_index, self.col_index = lanes, sent_index, col_index
        self.inner = (sent_index == 1) | (sent_index == 2)
        self.slot, self.chunks, self.pairs, self.totals, self.finals = 0, {}, {}, {}, {}

    def pairs_of(self, k, stage):
        if k not in self.chunks:
            return []
        _, first, spread = self.chunks[k]
        always = lambda f: True
        if spread:
            hops = (
                {(0, 1): always, (3, 2): lambda f: f < 3},
                {(1, 2): always, (2, 1): lambda f: f <= 1},
                {(2, 3): always, (1, 0): lambda f: f <= 0},
            )
        else:
            hops = (
                {(3, 2): always, (0, 1): lambda f: f <= 0},
                {(2, 1): always, (1, 2): lambda f: f <= 1},
                {(1, 0): always, (2, 3): lambda f: f <= 2},
            )
        cores = len(first)
        return [
            (a * cores + c, b * cores + c)
            for c in range(cores)
            for (a, b), wanted in hops[stage].items()
            if wanted(first[c])
        ]

    def step(self, term=None, first=None, spread=None):
        k = self.slot
        self.slot += 1
        middle, last = k - self.lanes, k - 2 * self.lanes
        if term is not None:
            self.chunks[k] = (term, first, spread)
        ends = term
        if last in self.totals:
            total = self.totals[last]
            ends = total if term is None else jnp.where(self.inner, total, term)
        pair = self.pairs.get(middle)
        if ends is not None and pair is not None:
            ends, pair = lax.optimization_barrier((ends, pair))
        axes = ("sent", "col")
        if ends is not None:
            perm = self.pairs_of(k, 0) + self.pairs_of(last, 2)
            ends_in = lax.ppermute(ends, axes, perm)
        if pair is not None:
            self.totals[middle] = pair + lax.ppermute(pair, axes, self.pairs_of(middle, 1))
        if term is not None:
            self.pairs[k] = term + ends_in
        if last in self.totals:
            old, first, _ = self.chunks[last]
            alone = jnp.asarray([f == 3 for f in first])[self.col_index] & (self.sent_index == 3)
            outer = jnp.where(alone, ends_in + old, ends_in)
            self.finals[last] = jnp.where(self.inner, ends, outer)


def shards(sketched, widths, inv_factor, shared):
    view_count, row_count, col_half = sketched.shape
    factor_rows = inv_factor.shape[1]
    sent_size = lax.axis_size("sent")
    view_size = lax.axis_size("view")
    core_count = lax.axis_size("col")
    total_rows = row_count * sent_size
    scale = 1.0 / math.sqrt(total_rows)
    high = lax.Precision.HIGH
    highest = lax.Precision.HIGHEST
    col_index = lax.axis_index("col")
    sent_index = lax.axis_index("sent")
    col_pos = col_index * col_half + jnp.arange(col_half)
    keep_cols = (col_pos[None, :] < widths[:, None]).astype(jnp.float32)[:, :, None]
    row_pos = sent_index * factor_rows + jnp.arange(factor_rows)
    keep_rows = (row_pos[None, :] < widths[:, None]).astype(jnp.float32)[:, :, None]
    use_line = sent_size == 4 and core_count == 2 and col_half % (LANES * CHUNK) == 0

    chunk = CHUNK if use_line else col_half
    per_view = col_half // chunk
    slots = [(j, q) for j in range(view_count) for q in range(per_view)]
    firsts = [
        [(c * col_half + q * chunk) // factor_rows for c in range(core_count)] for _, q in slots
    ]

    def keep_of(j, q):
        return keep_cols[j, q * chunk : (q + 1) * chunk]

    down = (((0,), (0,)), ((), ()))
    def first_half(proj, j):
        half_part = jnp.dot(inv_factor[j], jnp.concatenate(proj), precision=high)
        if use_line:
            perm = [
                (s * 2 + c, s * 2 + 1 - c)
                for s in range(sent_size)
                for c in range(2)
                if (s + 1) * factor_rows > col_half
            ]
            half = half_part + lax.ppermute(half_part, ("sent", "col"), perm)
        else:
            half = lax.psum(half_part, "col")
        return half * keep_rows[j]

    def cut(whole):
        return [whole[q * chunk : (q + 1) * chunk] for q in range(per_view)]

    terms = []
    for j in range(view_count):
        terms += cut(
            scale
            * lax.dot_general(sketched[j], shared, down, preferred_element_type=jnp.float32)
        )

    def back_terms(proj, j):
        return cut(
            lax.dot_general(
                inv_factor[j], first_half(proj, j), down, precision=high,
                preferred_element_type=jnp.float32,
            )
        )

    if use_line:
        line = Line(LANES, sent_index, col_index)
        for term, first in zip(terms, firsts):
            line.step(term, first, True)
        done = 0
        while done < len(slots):
            while done + per_view - 1 not in line.finals:
                line.step()
            proj = [line.finals[done + q] * keep_of(*slots[done + q]) for q in range(per_view)]
            for q, term in enumerate(back_terms(proj, slots[done][0])):
                line.step(term, firsts[q], False)
            done += per_view
        begin = line.slot - len(slots)
        for _ in range(2 * LANES):
            line.step()
        sums = [line.finals[begin + k] for k in range(len(slots))]
    else:
        sums = []
        for j in range(view_count):
            proj = [lax.psum(terms[j], "sent") * keep_of(j, 0)]
            sums += [lax.psum(t, "sent") for t in back_terms(proj, j)]
    loads = [total * keep_of(*slot) for total, slot in zip(sums, slots)]
    loadings = jnp.concatenate(loads).reshape(view_count, col_half, -1)
    contrib = 0.0
    for j in range(view_count):
        whole = jnp.concatenate(loads[j * per_view : (j + 1) * per_view]).astype(jnp.bfloat16)
        contrib += jnp.dot(sketched[j], whole, preferred_element_type=jnp.float32)

    if view_size == 4 and core_count == 2:
        part_rows = row_count // 2
        near = lambda bit: [(v, v ^ bit) for v in range(view_size)]
        swap = [(0, 1), (1, 0)]
        mine = lax.dynamic_slice_in_dim(contrib, col_index * part_rows, part_rows)
        other = lax.dynamic_slice_in_dim(contrib, (1 - col_index) * part_rows, part_rows)
        mine = mine + lax.ppermute(other, "col", swap)
        upper, lower_part = mine[: part_rows // 2], mine[part_rows // 2 :]
        upper = upper + lax.ppermute(upper, "view", near(1))
        lower_part = lower_part + lax.ppermute(lower_part, "view", near(2))
        upper = upper + lax.ppermute(upper, "view", near(2))
        lower_part = lower_part + lax.ppermute(lower_part, "view", near(1))
        mine = jnp.concatenate([upper, lower_part])
        other = lax.ppermute(mine, "col", swap)
        merged = jnp.concatenate(
            [jnp.where(col_index == 0, mine, other), jnp.where(col_index == 0, other, mine)]
        )
    else:
        merged = lax.psum(contrib, ("view", "col"))

    if core_count == 2 and sent_size & (sent_size - 1) == 0:
        width = merged.shape[1] // 2
        own = lax.dynamic_slice_in_dim(merged, col_index * width, width, axis=1)
        gram = lax.dot_general(merged, own, (((0,), (0,)), ((), ())), precision=highest)
        bit = 1
        while bit < sent_size:
            gram = gram + lax.ppermute(gram, "sent", [(s, s ^ bit) for s in range(sent_size)])
            bit *= 2
        other = lax.ppermute(gram, "col", [(0, 1), (1, 0)])
        gram = jnp.concatenate(
            [jnp.where(col_index == 0, gram, other), jnp.where(col_index == 0, other, gram)],
            axis=1,
        )
    else:
        gram = lax.dot_general(merged, merged, (((0,), (0,)), ((), ())), precision=highest)
        gram = lax.psum(gram, "sent")
    lower = jnp.linalg.cholesky(gram)
    updated = lax.linalg.triangular_solve(
        lower, merged, left_side=False, lower=True, transpose_a=True
    ) * math.sqrt(total_rows)
    return (loadings, updated)


def solution(mesh):
    return jax.shard_map(
        shards,
        mesh=mesh,
        in_specs=(P("view", "sent", "col"), P("view"), P("view", "sent", "col"), P("sent", None)),
        out_specs=(P("view", "col", None), P("sent", None)),
        check_vma=False,
    )
```

```python
import math

import jax
import jax.numpy as jnp
from jax import lax
from jax.sharding import PartitionSpec as P

CHUNK = 512
LANES = 2


class Line:
    def __init__(self, lanes, sent_index, col_index):
        self.lanes, self.sent_index, self.col_index = lanes, sent_index, col_index
        self.inner = (sent_index == 1) | (sent_index == 2)
        self.slot, self.chunks, self.pairs, self.totals, self.finals = 0, {}, {}, {}, {}

    def pairs_of(self, k, stage):
        if k not in self.chunks:
            return []
        _, first, spread = self.chunks[k]
        always = lambda f: True
        if spread:
            hops = (
                {(0, 1): always, (3, 2): lambda f: f < 3},
                {(1, 2): always, (2, 1): lambda f: f <= 1},
                {(2, 3): always, (1, 0): lambda f: f <= 0},
            )
        else:
            hops = (
                {(3, 2): always, (0, 1): lambda f: f <= 0},
                {(2, 1): always, (1, 2): lambda f: f <= 1},
                {(1, 0): always, (2, 3): lambda f: f <= 2},
            )
        cores = len(first)
        return [
            (a * cores + c, b * cores + c)
            for c in range(cores)
            for (a, b), wanted in hops[stage].items()
            if wanted(first[c])
        ]

    def step(self, term=None, first=None, spread=None):
        k = self.slot
        self.slot += 1
        middle, last = k - self.lanes, k - 2 * self.lanes
        if term is not None:
            self.chunks[k] = (term, first, spread)
        ends = term
        if last in self.totals:
            total = self.totals[last]
            ends = total if term is None else jnp.where(self.inner, total, term)
        pair = self.pairs.get(middle)
        if ends is not None and pair is not None:
            ends, pair = lax.optimization_barrier((ends, pair))
        axes = ("sent", "col")
        if ends is not None:
            perm = self.pairs_of(k, 0) + self.pairs_of(last, 2)
            ends_in = lax.ppermute(ends, axes, perm)
        if pair is not None:
            self.totals[middle] = pair + lax.ppermute(pair, axes, self.pairs_of(middle, 1))
        if term is not None:
            self.pairs[k] = term + ends_in
        if last in self.totals:
            old, first, _ = self.chunks[last]
            alone = jnp.asarray([f == 3 for f in first])[self.col_index] & (self.sent_index == 3)
            outer = jnp.where(alone, ends_in + old, ends_in)
            self.finals[last] = jnp.where(self.inner, ends, outer)


def shards(sketched, widths, inv_factor, shared):
    view_count, row_count, col_half = sketched.shape
    factor_rows = inv_factor.shape[1]
    sent_size = lax.axis_size("sent")
    view_size = lax.axis_size("view")
    core_count = lax.axis_size("col")
    total_rows = row_count * sent_size
    scale = 1.0 / math.sqrt(total_rows)
    high = lax.Precision.HIGH
    highest = lax.Precision.HIGHEST
    col_index = lax.axis_index("col")
    sent_index = lax.axis_index("sent")
    col_pos = col_index * col_half + jnp.arange(col_half)
    keep_cols = (col_pos[None, :] < widths[:, None]).astype(jnp.float32)[:, :, None]
    row_pos = sent_index * factor_rows + jnp.arange(factor_rows)
    keep_rows = (row_pos[None, :] < widths[:, None]).astype(jnp.float32)[:, :, None]
    use_line = sent_size == 4 and core_count == 2 and col_half % (LANES * CHUNK) == 0

    chunk = CHUNK if use_line else col_half
    per_view = col_half // chunk
    slots = [(j, q) for j in range(view_count) for q in range(per_view)]
    firsts = [
        [(c * col_half + q * chunk) // factor_rows for c in range(core_count)] for _, q in slots
    ]

    def keep_of(j, q):
        return keep_cols[j, q * chunk : (q + 1) * chunk]

    down = (((0,), (0,)), ((), ()))
    def first_half(proj, j):
        half_part = jnp.dot(inv_factor[j], jnp.concatenate(proj), precision=high)
        if use_line:
            perm = [
                (s * 2 + c, s * 2 + 1 - c)
                for s in range(sent_size)
                for c in range(2)
                if (s + 1) * factor_rows > col_half
            ]
            half = half_part + lax.ppermute(half_part, ("sent", "col"), perm)
        else:
            half = lax.psum(half_part, "col")
        return half * keep_rows[j]

    def cut(whole):
        return [whole[q * chunk : (q + 1) * chunk] for q in range(per_view)]

    terms = []
    for j in range(view_count):
        terms += cut(
            scale
            * lax.dot_general(sketched[j], shared, down, preferred_element_type=jnp.float32)
        )

    def back_terms(proj, j):
        return cut(
            lax.dot_general(
                inv_factor[j], first_half(proj, j), down, precision=high,
                preferred_element_type=jnp.float32,
            )
        )

    if use_line:
        line = Line(LANES, sent_index, col_index)
        for term, first in zip(terms, firsts):
            line.step(term, first, True)
        done = 0
        while done < len(slots):
            while done + per_view - 1 not in line.finals:
                line.step()
            proj = [line.finals[done + q] * keep_of(*slots[done + q]) for q in range(per_view)]
            for q, term in enumerate(back_terms(proj, slots[done][0])):
                line.step(term, firsts[q], False)
            done += per_view
        begin = line.slot - len(slots)
        for _ in range(2 * LANES):
            line.step()
        sums = [line.finals[begin + k] for k in range(len(slots))]
    else:
        sums = []
        for j in range(view_count):
            proj = [lax.psum(terms[j], "sent") * keep_of(j, 0)]
            sums += [lax.psum(t, "sent") for t in back_terms(proj, j)]
    loads = [total * keep_of(*slot) for total, slot in zip(sums, slots)]
    loadings = jnp.concatenate(loads).reshape(view_count, col_half, -1)
    contrib = 0.0
    for j in range(view_count):
        whole = jnp.concatenate(loads[j * per_view : (j + 1) * per_view]).astype(jnp.bfloat16)
        contrib += jnp.dot(sketched[j], whole, preferred_element_type=jnp.float32)

    if view_size == 4 and core_count == 2:
        part_rows = row_count // 2
        near = lambda bit: [(v, v ^ bit) for v in range(view_size)]
        swap = [(0, 1), (1, 0)]
        mine = lax.dynamic_slice_in_dim(contrib, col_index * part_rows, part_rows)
        other = lax.dynamic_slice_in_dim(contrib, (1 - col_index) * part_rows, part_rows)
        mine = mine + lax.ppermute(other, "col", swap)
        upper, lower_part = mine[: part_rows // 2], mine[part_rows // 2 :]
        upper = upper + lax.ppermute(upper, "view", near(1))
        lower_part = lower_part + lax.ppermute(lower_part, "view", near(2))
        upper = upper + lax.ppermute(upper, "view", near(2))
        lower_part = lower_part + lax.ppermute(lower_part, "view", near(1))
        mine = jnp.concatenate([upper, lower_part])
        other = lax.ppermute(mine, "col", swap)
        merged = jnp.concatenate(
            [jnp.where(col_index == 0, mine, other), jnp.where(col_index == 0, other, mine)]
        )
    else:
        merged = lax.psum(contrib, ("view", "col"))

    if core_count == 2 and sent_size & (sent_size - 1) == 0:
        width = merged.shape[1] // 2
        own = lax.dynamic_slice_in_dim(merged, col_index * width, width, axis=1)
        gram = lax.dot_general(merged, own, (((0,), (0,)), ((), ())), precision=highest)
        bit = 1
        while bit < sent_size:
            gram = gram + lax.ppermute(gram, "sent", [(s, s ^ bit) for s in range(sent_size)])
            bit *= 2
        other = lax.ppermute(gram, "col", [(0, 1), (1, 0)])
        gram = jnp.concatenate(
            [jnp.where(col_index == 0, gram, other), jnp.where(col_index == 0, other, gram)],
            axis=1,
        )
    else:
        gram = lax.dot_general(merged, merged, (((0,), (0,)), ((), ())), precision=highest)
        gram = lax.psum(gram, "sent")
    lower = jnp.linalg.cholesky(gram)
    updated = lax.linalg.triangular_solve(
        lower, merged, left_side=False, lower=True, transpose_a=True
    ) * math.sqrt(total_rows)
    return (loadings, updated)


def solution(mesh):
    return jax.shard_map(
        shards,
        mesh=mesh,
        in_specs=(P("view", "sent", "col"), P("view"), P("view", "sent", "col"), P("sent", None)),
        out_specs=(P("view", "col", None), P("sent", None)),
        check_vma=False,
    )
```

```python
import math

import jax
import jax.numpy as jnp
from jax import lax
from jax.sharding import PartitionSpec as P

CHUNK = 512
LANES = 1
WHOLE_VIEWS = 1


class Line:
    def __init__(self, lanes, sent_index, col_index):
        self.lanes, self.sent_index, self.col_index = lanes, sent_index, col_index
        self.inner = (sent_index == 1) | (sent_index == 2)
        self.slot, self.chunks, self.pairs, self.totals, self.finals = 0, {}, {}, {}, {}

    def pairs_of(self, k, stage):
        if k not in self.chunks:
            return []
        _, first, spread = self.chunks[k]
        always = lambda f: True
        if spread:
            hops = (
                {(0, 1): always, (3, 2): lambda f: f < 3},
                {(1, 2): always, (2, 1): lambda f: f <= 1},
                {(2, 3): always, (1, 0): lambda f: f <= 0},
            )
        else:
            hops = (
                {(3, 2): always, (0, 1): lambda f: f <= 0},
                {(2, 1): always, (1, 2): lambda f: f <= 1},
                {(1, 0): always, (2, 3): lambda f: f <= 2},
            )
        cores = len(first)
        return [
            (a * cores + c, b * cores + c)
            for c in range(cores)
            for (a, b), wanted in hops[stage].items()
            if wanted(first[c])
        ]

    def meet(self, value):
        last = self.slot - self.lanes - 1
        value, self.totals[last] = lax.optimization_barrier((value, self.totals[last]))
        return value

    def step(self, term=None, first=None, spread=None):
        k = self.slot
        self.slot += 1
        middle, last = k - self.lanes, k - 2 * self.lanes
        if term is not None:
            self.chunks[k] = (term, first, spread)
        ends = term
        if last in self.totals:
            total = self.totals[last]
            ends = total if term is None else jnp.where(self.inner, total, term)
        pair = self.pairs.get(middle)
        if ends is not None and pair is not None:
            ends, pair = lax.optimization_barrier((ends, pair))
        axes = ("sent", "col")
        if ends is not None:
            perm = self.pairs_of(k, 0) + self.pairs_of(last, 2)
            ends_in = lax.ppermute(ends, axes, perm)
        if pair is not None:
            self.totals[middle] = pair + lax.ppermute(pair, axes, self.pairs_of(middle, 1))
        if term is not None:
            self.pairs[k] = term + ends_in
        if last in self.totals:
            old, first, _ = self.chunks[last]
            alone = jnp.asarray([f == 3 for f in first])[self.col_index] & (self.sent_index == 3)
            outer = jnp.where(alone, ends_in + old, ends_in)
            self.finals[last] = jnp.where(self.inner, ends, outer)


def shards(sketched, widths, inv_factor, shared):
    view_count, row_count, col_half = sketched.shape
    factor_rows = inv_factor.shape[1]
    sent_size = lax.axis_size("sent")
    view_size = lax.axis_size("view")
    core_count = lax.axis_size("col")
    total_rows = row_count * sent_size
    scale = 1.0 / math.sqrt(total_rows)
    high = lax.Precision.HIGH
    highest = lax.Precision.HIGHEST
    col_index = lax.axis_index("col")
    sent_index = lax.axis_index("sent")
    col_pos = col_index * col_half + jnp.arange(col_half)
    keep_cols = (col_pos[None, :] < widths[:, None]).astype(jnp.float32)[:, :, None]
    row_pos = sent_index * factor_rows + jnp.arange(factor_rows)
    keep_rows = (row_pos[None, :] < widths[:, None]).astype(jnp.float32)[:, :, None]
    use_line = sent_size == 4 and core_count == 2 and col_half % (LANES * CHUNK) == 0

    chunk = CHUNK if use_line else col_half
    per_view = col_half // chunk
    slots = [(j, q) for j in range(view_count) for q in range(per_view)]
    firsts = [
        [(c * col_half + q * chunk) // factor_rows for c in range(core_count)] for _, q in slots
    ]

    def keep_of(j, q):
        return keep_cols[j, q * chunk : (q + 1) * chunk]

    down = (((0,), (0,)), ((), ()))
    def first_half(proj, j):
        half_part = jnp.dot(inv_factor[j], jnp.concatenate(proj), precision=high)
        if use_line:
            perm = [
                (s * 2 + c, s * 2 + 1 - c)
                for s in range(sent_size)
                for c in range(2)
                if (s + 1) * factor_rows > col_half
            ]
            half = half_part + lax.ppermute(half_part, ("sent", "col"), perm)
        else:
            half = lax.psum(half_part, "col")
        return half * keep_rows[j]

    def cut(whole):
        return [whole[q * chunk : (q + 1) * chunk] for q in range(per_view)]

    def cut_all(whole):
        return [whole[k * chunk : (k + 1) * chunk] for k in range(whole.shape[0] // chunk)]

    terms = []
    for j in range(view_count):
        terms += cut(
            scale
            * lax.dot_general(sketched[j], shared, down, preferred_element_type=jnp.float32)
        )

    def back_terms(proj, j):
        return cut(
            lax.dot_general(
                inv_factor[j], first_half(proj, j), down, precision=high,
                preferred_element_type=jnp.float32,
            )
        )

    if use_line:
        line_views = view_count - WHOLE_VIEWS
        sums = [None] * len(slots)
        chunks = line_views * per_view
        apart = jnp.concatenate(terms[chunks:])
        apart, terms[0] = lax.optimization_barrier((apart, terms[0]))
        apart = lax.psum(apart, "sent")
        spread, gather = Line(LANES, sent_index, col_index), Line(LANES, sent_index, col_index)
        for k in range(chunks):
            spread.step(terms[k], firsts[k], True)
        apart = spread.meet(apart)
        for _ in range(2 * LANES):
            spread.step()
        projs = [spread.finals[k] * keep_of(*slots[k]) for k in range(chunks)]
        projs += [p * keep_of(*slots[chunks + k]) for k, p in enumerate(cut_all(apart))]
        views = [back_terms(projs[j * per_view : (j + 1) * per_view], j) for j in range(view_count)]
        apart = jnp.concatenate(sum(views[line_views:], []))
        apart, views[1][0] = lax.optimization_barrier((apart, views[1][0]))
        apart = lax.psum(apart, "sent")
        for k, term in enumerate(sum(views[:line_views], [])):
            gather.step(term, firsts[k], False)
        gather.step()
        apart = gather.meet(apart)
        gather.step()
        sums[chunks:] = cut_all(apart)
        for k in range(chunks):
            sums[k] = gather.finals[k]
    else:
        sums = []
        for j in range(view_count):
            proj = [lax.psum(terms[j], "sent") * keep_of(j, 0)]
            sums += [lax.psum(t, "sent") for t in back_terms(proj, j)]
    loads = [total * keep_of(*slot) for total, slot in zip(sums, slots)]
    loadings = jnp.concatenate(loads).reshape(view_count, col_half, -1)
    contrib = 0.0
    for j in range(view_count):
        whole = jnp.concatenate(loads[j * per_view : (j + 1) * per_view]).astype(jnp.bfloat16)
        contrib += jnp.dot(sketched[j], whole, preferred_element_type=jnp.float32)

    if view_size == 4 and core_count == 2:
        part_rows = row_count // 2
        near = lambda bit: [(v, v ^ bit) for v in range(view_size)]
        swap = [(0, 1), (1, 0)]
        mine = lax.dynamic_slice_in_dim(contrib, col_index * part_rows, part_rows)
        other = lax.dynamic_slice_in_dim(contrib, (1 - col_index) * part_rows, part_rows)
        mine = mine + lax.ppermute(other, "col", swap)
        upper, lower_part = mine[: part_rows // 2], mine[part_rows // 2 :]
        upper = upper + lax.ppermute(upper, "view", near(1))
        lower_part = lower_part + lax.ppermute(lower_part, "view", near(2))
        upper = upper + lax.ppermute(upper, "view", near(2))
        lower_part = lower_part + lax.ppermute(lower_part, "view", near(1))
        mine = jnp.concatenate([upper, lower_part])
        other = lax.ppermute(mine, "col", swap)
        merged = jnp.concatenate(
            [jnp.where(col_index == 0, mine, other), jnp.where(col_index == 0, other, mine)]
        )
    else:
        merged = lax.psum(contrib, ("view", "col"))

    if core_count == 2 and sent_size & (sent_size - 1) == 0:
        width = merged.shape[1] // 2
        own = lax.dynamic_slice_in_dim(merged, col_index * width, width, axis=1)
        gram = lax.dot_general(merged, own, (((0,), (0,)), ((), ())), precision=highest)
        bit = 1
        while bit < sent_size:
            gram = gram + lax.ppermute(gram, "sent", [(s, s ^ bit) for s in range(sent_size)])
            bit *= 2
        other = lax.ppermute(gram, "col", [(0, 1), (1, 0)])
        gram = jnp.concatenate(
            [jnp.where(col_index == 0, gram, other), jnp.where(col_index == 0, other, gram)],
            axis=1,
        )
    else:
        gram = lax.dot_general(merged, merged, (((0,), (0,)), ((), ())), precision=highest)
        gram = lax.psum(gram, "sent")
    lower = jnp.linalg.cholesky(gram)
    updated = lax.linalg.triangular_solve(
        lower, merged, left_side=False, lower=True, transpose_a=True
    ) * math.sqrt(total_rows)
    return (loadings, updated)


def solution(mesh):
    return jax.shard_map(
        shards,
        mesh=mesh,
        in_specs=(P("view", "sent", "col"), P("view"), P("view", "sent", "col"), P("sent", None)),
        out_specs=(P("view", "col", None), P("sent", None)),
        check_vma=False,
    )
```

```python
import functools
import math

import jax
import jax.numpy as jnp
from jax import lax
from jax.experimental import pallas as pl
from jax.experimental.pallas import tpu as pltpu
from jax.sharding import PartitionSpec as P

CHUNK = 512
PANEL = 32


def line_chain(terms, firsts, spread, sent_index, col_index):
    count, cores = len(terms), len(firsts[0])
    if spread:
        up_ok = (lambda f: True, lambda f: True, lambda f: True)
        down_ok = (lambda f: f < 3, lambda f: f <= 1, lambda f: f <= 0)
    else:
        up_ok = (lambda f: f <= 0, lambda f: f <= 1, lambda f: f <= 2)
        down_ok = (lambda f: True, lambda f: True, lambda f: True)

    def hop(step, choices, ok, hops):
        present = [i for i in range(3) if 0 <= step - i < count]
        value = choices[present[0]]
        for i in present[1:]:
            value = jnp.where(sent_index == hops[i][0], choices[i], value)
        perm = [
            (hops[i][0] * cores + c, hops[i][1] * cores + c)
            for i in present
            for c in range(cores)
            if ok[i](firsts[step - i][c])
        ]
        return lax.ppermute(value, ("sent", "col"), perm) if perm else jnp.zeros_like(value)

    low = sent_index <= 1
    inner = (sent_index == 1) | (sent_index == 2)
    pairs, totals, finals = {}, {}, []
    for step in range(count + 2):
        choices = [terms[step] if step < count else None, pairs.get(step - 1), totals.get(step - 2)]
        up = hop(step, choices, up_ok, ((0, 1), (1, 2), (2, 3)))
        down = hop(step, choices, down_ok, ((3, 2), (2, 1), (1, 0)))
        near, far = jnp.where(low, up, down), jnp.where(low, down, up)
        if step < count:
            pairs[step] = terms[step] + near
        if 0 <= step - 1 < count:
            totals[step - 1] = pairs[step - 1] + far
        k = step - 2
        if k >= 0:
            at_end = jnp.asarray([f == 3 for f in firsts[k]])[col_index] & (sent_index == 3)
            far = jnp.where(at_end, far + terms[k], far)
            finals.append(jnp.where(inner, totals[k], far))
    return finals


def pieces(x):
    high = x.astype(jnp.bfloat16)
    rest = x - high.astype(jnp.float32)
    middle = rest.astype(jnp.bfloat16)
    return high, middle, (rest - middle.astype(jnp.float32)).astype(jnp.bfloat16)


def whiten_kernel(scale, gram_ref, merged_ref, out_ref, work):
    size = gram_ref.shape[0]
    tile = (8, 128)
    work[:, :size] = gram_ref[...]
    rows = lax.broadcasted_iota(jnp.int32, (size, size), 0)
    work[:, size:] = (rows == lax.broadcasted_iota(jnp.int32, (size, size), 1)).astype(jnp.float32)
    sublane = lax.broadcasted_iota(jnp.int32, tile, 0)
    for panel in range(0, size, PANEL):
        end = panel + PANEL
        start = panel // 128 * 128
        stop = size + start + 128
        for block in range(panel, end, 8):
            lanes = range(start, stop, 128)
            cols = [
                [
                    jnp.broadcast_to(
                        work[t : t + 8, start : start + 128][:, block - start + k][:, None], tile
                    )
                    for k in range(8)
                ]
                for t in range(block, end, 8)
            ]
            low = [
                [jnp.broadcast_to(cols[0][k][i : i + 1], tile) for k in range(i + 1)]
                for i in range(8)
            ]
            inverse = []
            for k in range(8):
                pivot = low[k][k]
                root = lax.rsqrt(pivot)
                root = root * (1.5 - 0.5 * pivot * root * root)
                inverse.append(root)
                for i in range(k + 1, 8):
                    low[i][k] = low[i][k] * root
                for i in range(k + 1, 8):
                    for m in range(k + 1, i + 1):
                        low[i][m] = low[i][m] - low[i][k] * low[m][k]
            for t in range(1, len(cols)):
                for k in range(8):
                    value = cols[t][k]
                    for m in range(k):
                        value = value - low[k][m] * cols[t][m]
                    cols[t][k] = value * inverse[k]
            for lane in lanes:
                here = slice(lane, lane + 128)
                old = work[block : block + 8, here]
                done, new = [], old
                for k in range(8):
                    value = jnp.broadcast_to(old[k : k + 1], tile)
                    for m in range(k):
                        value = value - low[k][m] * done[m]
                    done.append(value * inverse[k])
                    new = jnp.where(sublane == k, done[k], new)
                work[block : block + 8, here] = new
                for t in range(1, len(cols)):
                    at = slice(block + 8 * t, block + 8 * t + 8)
                    value = work[at, here]
                    for k in range(8):
                        value = value - cols[t][k] * done[k]
                    work[at, here] = value
        if end < size:
            first = end // 128 * 128
            upper = pieces(work[panel:end, first:size])
            right = pieces(work[panel:end, first:stop])
            a = jnp.concatenate([upper[i] for i in (0, 0, 1, 1, 0, 2)])
            b = jnp.concatenate([right[i] for i in (0, 1, 0, 1, 2, 0)])
            update = lax.dot_general(
                a, b, (((0,), (0,)), ((), ())), preferred_element_type=jnp.float32
            )
            work[end:, first:stop] -= update[end - first :]
    a = pieces(merged_ref[...])
    b = pieces(work[:, size:] * scale)
    total = 0.0
    for i, j in ((1, 1), (0, 2), (2, 0), (0, 1), (1, 0), (0, 0)):
        total += lax.dot_general(
            a[i], b[j], (((1,), (1,)), ((), ())), preferred_element_type=jnp.float32
        )
    out_ref[...] = total


def whiten(gram, merged, scale):
    size = gram.shape[0]
    return pl.pallas_call(
        functools.partial(whiten_kernel, scale),
        out_shape=jax.ShapeDtypeStruct(merged.shape, jnp.float32),
        in_specs=[pl.BlockSpec(memory_space=pltpu.VMEM)] * 2,
        out_specs=pl.BlockSpec(memory_space=pltpu.VMEM),
        scratch_shapes=[pltpu.VMEM((size, 2 * size), jnp.float32)],
        compiler_params=pltpu.CompilerParams(vmem_limit_bytes=32 * 2**20),
        name="whiten",
    )(gram, merged)


def shards(sketched, widths, inv_factor, shared):
    view_count, row_count, col_half = sketched.shape
    factor_rows = inv_factor.shape[1]
    sent_size = lax.axis_size("sent")
    view_size = lax.axis_size("view")
    core_count = lax.axis_size("col")
    total_rows = row_count * sent_size
    scale = 1.0 / math.sqrt(total_rows)
    high = lax.Precision.HIGH
    highest = lax.Precision.HIGHEST
    col_index = lax.axis_index("col")
    sent_index = lax.axis_index("sent")
    col_pos = col_index * col_half + jnp.arange(col_half)
    keep_cols = (col_pos[None, :] < widths[:, None]).astype(jnp.float32)[:, :, None]
    row_pos = sent_index * factor_rows + jnp.arange(factor_rows)
    keep_rows = (row_pos[None, :] < widths[:, None]).astype(jnp.float32)[:, :, None]
    use_line = sent_size == 4 and core_count == 2 and col_half % CHUNK == 0

    chunk = CHUNK if use_line else col_half
    per_view = col_half // chunk
    slots = [(j, q) for j in range(view_count) for q in range(per_view)]
    firsts = [
        [(c * col_half + q * chunk) // factor_rows for c in range(core_count)] for _, q in slots
    ]

    def sum_sent(terms, spread):
        if use_line:
            return line_chain(terms, firsts, spread, sent_index, col_index)
        return [lax.psum(t, "sent") for t in terms]

    def columns(array, j, q):
        return array[j, :, q * chunk : (q + 1) * chunk]

    def keep_of(j, q):
        return keep_cols[j, q * chunk : (q + 1) * chunk]

    down = (((0,), (0,)), ((), ()))
    terms = [
        lax.dot_general(columns(sketched, j, q), shared, down, preferred_element_type=jnp.float32)
        * scale
        for j, q in slots
    ]
    proj = [p * keep_of(*slot) for p, slot in zip(sum_sent(terms, True), slots)]
    halves = []
    for j in range(view_count):
        half_part = 0.0
        for q in range(per_view):
            half_part += jnp.dot(columns(inv_factor, j, q), proj[j * per_view + q], precision=high)
        if use_line:
            perm = [
                (s * 2 + c, s * 2 + 1 - c)
                for s in range(sent_size)
                for c in range(2)
                if (s + 1) * factor_rows > col_half
            ]
            half = half_part + lax.ppermute(half_part, ("sent", "col"), perm)
        else:
            half = lax.psum(half_part, "col")
        halves.append(half * keep_rows[j])
    backs = [
        lax.dot_general(
            columns(inv_factor, j, q), halves[j], down, precision=high,
            preferred_element_type=jnp.float32,
        )
        for j, q in slots
    ]
    loads = [b * keep_of(*slot) for b, slot in zip(sum_sent(backs, False), slots)]
    contrib = 0.0
    for load, (j, q) in zip(loads, slots):
        contrib += jnp.dot(
            columns(sketched, j, q), load.astype(jnp.bfloat16), preferred_element_type=jnp.float32
        )
    loadings = jnp.concatenate(loads).reshape(view_count, col_half, -1)

    if view_size == 4 and core_count == 2:
        part_rows = row_count // 2
        near = lambda bit: [(v, v ^ bit) for v in range(view_size)]
        swap = [(0, 1), (1, 0)]
        mine = lax.dynamic_slice_in_dim(contrib, col_index * part_rows, part_rows)
        other = lax.dynamic_slice_in_dim(contrib, (1 - col_index) * part_rows, part_rows)
        mine = mine + lax.ppermute(other, "col", swap)
        upper, lower_part = mine[: part_rows // 2], mine[part_rows // 2 :]
        upper = upper + lax.ppermute(upper, "view", near(1))
        lower_part = lower_part + lax.ppermute(lower_part, "view", near(2))
        upper = upper + lax.ppermute(upper, "view", near(2))
        lower_part = lower_part + lax.ppermute(lower_part, "view", near(1))
        mine = jnp.concatenate([upper, lower_part])
        other = lax.ppermute(mine, "col", swap)
        merged = jnp.concatenate(
            [jnp.where(col_index == 0, mine, other), jnp.where(col_index == 0, other, mine)]
        )
    else:
        merged = lax.psum(contrib, ("view", "col"))

    if core_count == 2 and sent_size & (sent_size - 1) == 0:
        width = merged.shape[1] // 2
        own = lax.dynamic_slice_in_dim(merged, col_index * width, width, axis=1)
        gram = lax.dot_general(merged, own, (((0,), (0,)), ((), ())), precision=highest)
        bit = 1
        while bit < sent_size:
            gram = gram + lax.ppermute(gram, "sent", [(s, s ^ bit) for s in range(sent_size)])
            bit *= 2
        other = lax.ppermute(gram, "col", [(0, 1), (1, 0)])
        gram = jnp.concatenate(
            [jnp.where(col_index == 0, gram, other), jnp.where(col_index == 0, other, gram)],
            axis=1,
        )
    else:
        gram = lax.dot_general(merged, merged, (((0,), (0,)), ((), ())), precision=highest)
        gram = lax.psum(gram, "sent")
    updated = whiten(gram, merged, math.sqrt(total_rows))
    return (loadings, updated)


def solution(mesh):
    return jax.shard_map(
        shards,
        mesh=mesh,
        in_specs=(P("view", "sent", "col"), P("view"), P("view", "sent", "col"), P("sent", None)),
        out_specs=(P("view", "col", None), P("sent", None)),
        check_vma=False,
    )
```

```python
import functools
import math

import jax
import jax.numpy as jnp
from jax import lax
from jax.experimental import pallas as pl
from jax.experimental.pallas import tpu as pltpu
from jax.sharding import PartitionSpec as P

CHUNK = 256
LANES = 2
PANEL = 32


class Line:
    def __init__(self, lanes, sent_index, col_index):
        self.lanes, self.sent_index, self.col_index = lanes, sent_index, col_index
        self.inner = (sent_index == 1) | (sent_index == 2)
        self.slot, self.chunks, self.pairs, self.totals, self.finals = 0, {}, {}, {}, {}
        self.arrived = {}

    def pairs_of(self, k, stage):
        if k not in self.chunks:
            return []
        _, first, spread = self.chunks[k]
        always = lambda f: True
        if spread:
            hops = (
                {(0, 1): always, (3, 2): lambda f: f < 3},
                {(1, 2): always, (2, 1): lambda f: f <= 1},
                {(2, 3): always, (1, 0): lambda f: f <= 0},
            )
        else:
            hops = (
                {(3, 2): always, (0, 1): lambda f: f <= 0},
                {(2, 1): always, (1, 2): lambda f: f <= 1},
                {(1, 0): always, (2, 3): lambda f: f <= 2},
            )
        cores = len(first)
        return [
            (a * cores + c, b * cores + c)
            for c in range(cores)
            for (a, b), wanted in hops[stage].items()
            if wanted(first[c])
        ]

    def step(self, term=None, first=None, spread=None):
        k = self.slot
        self.slot += 1
        self.collect(k - self.lanes)
        middle, last = k - self.lanes, k - 2 * self.lanes
        if term is not None:
            self.chunks[k] = (term, first, spread)
        ends, pair = term, self.pairs.get(middle)
        if last in self.totals:
            total = self.totals[last]
            ends = total if term is None else jnp.where(self.inner, total, term)
        if ends is not None and pair is not None:
            ends, pair = lax.optimization_barrier((ends, pair))
        axes, ends_in, pair_in = ("sent", "col"), None, None
        if ends is not None:
            perm = self.pairs_of(k, 0) + self.pairs_of(last, 2)
            ends_in = lax.ppermute(ends, axes, perm)
        if pair is not None:
            pair_in = lax.ppermute(pair, axes, self.pairs_of(middle, 1))
        self.arrived[k] = (ends, ends_in, pair_in)

    def collect(self, k):
        if k not in self.arrived:
            return
        ends, ends_in, pair_in = self.arrived.pop(k)
        middle, last = k - self.lanes, k - 2 * self.lanes
        following = self.arrived.get(k + 1, (None,))[0] if self.lanes > 1 else None
        tied = [v for v in (following, ends_in, pair_in) if v is not None]
        tied = list(lax.optimization_barrier(tuple(tied)))
        if following is not None:
            del tied[0]
        if ends_in is not None:
            ends_in = tied.pop(0)
        if pair_in is not None:
            self.totals[middle] = self.pairs[middle] + tied.pop(0)
        if k in self.chunks:
            self.pairs[k] = self.chunks[k][0] + ends_in
        if last in self.totals:
            old, first, _ = self.chunks[last]
            alone = (self.sent_index == 3) & (self.col_index >= [f == 3 for f in first].index(True)) \
                if 3 in first else None
            outer = ends_in if alone is None else jnp.where(alone, ends_in + old, ends_in)
            self.finals[last] = jnp.where(self.inner, ends, outer)


def pieces(x):
    high = x.astype(jnp.bfloat16)
    rest = x - high.astype(jnp.float32)
    middle = rest.astype(jnp.bfloat16)
    return high, middle, (rest - middle.astype(jnp.float32)).astype(jnp.bfloat16)


def whiten_kernel(scale, gram_ref, merged_ref, out_ref, work):
    size = gram_ref.shape[0]
    tile = (8, 128)
    work[:, :size] = gram_ref[...]
    rows = lax.broadcasted_iota(jnp.int32, (size, size), 0)
    work[:, size:] = (rows == lax.broadcasted_iota(jnp.int32, (size, size), 1)).astype(jnp.float32)
    sublane = lax.broadcasted_iota(jnp.int32, tile, 0)
    for panel in range(0, size, PANEL):
        end = panel + PANEL
        start = panel // 128 * 128
        stop = size + start + 128
        for block in range(panel, end, 8):
            lanes = range(start, stop, 128)
            cols = [
                [
                    jnp.broadcast_to(
                        work[t : t + 8, start : start + 128][:, block - start + k][:, None], tile
                    )
                    for k in range(8)
                ]
                for t in range(block, end, 8)
            ]
            low = [
                [jnp.broadcast_to(cols[0][k][i : i + 1], tile) for k in range(i + 1)]
                for i in range(8)
            ]
            inverse = []
            for k in range(8):
                pivot = low[k][k]
                root = lax.rsqrt(pivot)
                root = root * (1.5 - 0.5 * pivot * root * root)
                inverse.append(root)
                for i in range(k + 1, 8):
                    low[i][k] = low[i][k] * root
                for i in range(k + 1, 8):
                    for m in range(k + 1, i + 1):
                        low[i][m] = low[i][m] - low[i][k] * low[m][k]
            for t in range(1, len(cols)):
                for k in range(8):
                    value = cols[t][k]
                    for m in range(k):
                        value = value - low[k][m] * cols[t][m]
                    cols[t][k] = value * inverse[k]
            for lane in lanes:
                here = slice(lane, lane + 128)
                old = work[block : block + 8, here]
                done, new = [], old
                for k in range(8):
                    value = jnp.broadcast_to(old[k : k + 1], tile)
                    for m in range(k):
                        value = value - low[k][m] * done[m]
                    done.append(value * inverse[k])
                    new = jnp.where(sublane == k, done[k], new)
                work[block : block + 8, here] = new
                for t in range(1, len(cols)):
                    at = slice(block + 8 * t, block + 8 * t + 8)
                    value = work[at, here]
                    for k in range(8):
                        value = value - cols[t][k] * done[k]
                    work[at, here] = value
        if end < size:
            first = end // 128 * 128
            upper = pieces(work[panel:end, first:size])
            right = pieces(work[panel:end, first:stop])
            a = jnp.concatenate([upper[i] for i in (0, 0, 1, 1, 0, 2)])
            b = jnp.concatenate([right[i] for i in (0, 1, 0, 1, 2, 0)])
            update = lax.dot_general(
                a, b, (((0,), (0,)), ((), ())), preferred_element_type=jnp.float32
            )
            work[end:, first:stop] -= update[end - first :]
    a = pieces(merged_ref[...])
    b = pieces(work[:, size:] * scale)
    total = 0.0
    for i, j in ((1, 1), (0, 2), (2, 0), (0, 1), (1, 0), (0, 0)):
        total += lax.dot_general(
            a[i], b[j], (((1,), (1,)), ((), ())), preferred_element_type=jnp.float32
        )
    out_ref[...] = total


def whiten(gram, merged, scale):
    size = gram.shape[0]
    return pl.pallas_call(
        functools.partial(whiten_kernel, scale),
        out_shape=jax.ShapeDtypeStruct(merged.shape, jnp.float32),
        in_specs=[pl.BlockSpec(memory_space=pltpu.VMEM)] * 2,
        out_specs=pl.BlockSpec(memory_space=pltpu.VMEM),
        scratch_shapes=[pltpu.VMEM((size, 2 * size), jnp.float32)],
        compiler_params=pltpu.CompilerParams(vmem_limit_bytes=32 * 2**20),
        name="whiten",
    )(gram, merged)


def shards(sketched, widths, inv_factor, shared):
    view_count, row_count, col_half = sketched.shape
    factor_rows = inv_factor.shape[1]
    sent_size = lax.axis_size("sent")
    view_size = lax.axis_size("view")
    core_count = lax.axis_size("col")
    total_rows = row_count * sent_size
    scale = 1.0 / math.sqrt(total_rows)
    high = lax.Precision.HIGH
    highest = lax.Precision.HIGHEST
    col_index = lax.axis_index("col")
    sent_index = lax.axis_index("sent")
    col_pos = col_index * col_half + jnp.arange(col_half)
    keep_cols = (col_pos[None, :] < widths[:, None]).astype(jnp.float32)[:, :, None]
    row_pos = sent_index * factor_rows + jnp.arange(factor_rows)
    keep_rows = (row_pos[None, :] < widths[:, None]).astype(jnp.float32)[:, :, None]
    use_line = sent_size == 4 and core_count == 2 and col_half % CHUNK == 0

    chunk = CHUNK if use_line else col_half
    per_view = col_half // chunk
    slots = [(j, q) for j in range(view_count) for q in range(per_view)]
    firsts = [
        [(c * col_half + q * chunk) // factor_rows for c in range(core_count)] for _, q in slots
    ]

    def keep_of(j, q):
        return keep_cols[j, q * chunk : (q + 1) * chunk]

    down = (((0,), (0,)), ((), ()))
    def first_half(proj, j):
        half_part = jnp.dot(inv_factor[j], jnp.concatenate(proj), precision=high)
        if use_line:
            perm = [
                (s * 2 + c, s * 2 + 1 - c)
                for s in range(sent_size)
                for c in range(2)
                if (s + 1) * factor_rows > col_half
            ]
            half = half_part + lax.ppermute(half_part, ("sent", "col"), perm)
        else:
            half = lax.psum(half_part, "col")
        return half * keep_rows[j]

    def cut(whole):
        return [whole[q * chunk : (q + 1) * chunk] for q in range(per_view)]

    terms = []
    for j in range(view_count):
        terms += cut(
            scale
            * lax.dot_general(sketched[j], shared, down, preferred_element_type=jnp.float32)
        )

    def back_terms(proj, j):
        return cut(
            lax.dot_general(
                inv_factor[j], first_half(proj, j), down, precision=high,
                preferred_element_type=jnp.float32,
            )
        )

    if use_line:
        line = Line(LANES, sent_index, col_index)
        for term, first in zip(terms, firsts):
            line.step(term, first, True)
        done = 0
        while done < len(slots):
            while done + per_view - 1 not in line.finals:
                line.step()
            proj = [line.finals[done + q] * keep_of(*slots[done + q]) for q in range(per_view)]
            for q, term in enumerate(back_terms(proj, slots[done][0])):
                line.step(term, firsts[q], False)
            done += per_view
        begin = line.slot - len(slots)
        for _ in range(3 * LANES):
            line.step()
        sums = [line.finals[begin + k] for k in range(len(slots))]
    else:
        sums = []
        for j in range(view_count):
            proj = [lax.psum(terms[j], "sent") * keep_of(j, 0)]
            sums += [lax.psum(t, "sent") for t in back_terms(proj, j)]
    loads = [total * keep_of(*slot) for total, slot in zip(sums, slots)]
    loadings = jnp.concatenate(loads).reshape(view_count, col_half, -1)
    contrib = 0.0
    for j in range(view_count):
        whole = jnp.concatenate(loads[j * per_view : (j + 1) * per_view]).astype(jnp.bfloat16)
        contrib += jnp.dot(sketched[j], whole, preferred_element_type=jnp.float32)

    if view_size == 4 and core_count == 2:
        part_rows = row_count // 2
        near = lambda bit: [(v, v ^ bit) for v in range(view_size)]
        swap = [(0, 1), (1, 0)]
        mine = lax.dynamic_slice_in_dim(contrib, col_index * part_rows, part_rows)
        other = lax.dynamic_slice_in_dim(contrib, (1 - col_index) * part_rows, part_rows)
        mine = mine + lax.ppermute(other, "col", swap)
        upper, lower_part = mine[: part_rows // 2], mine[part_rows // 2 :]
        upper = upper + lax.ppermute(upper, "view", near(1))
        lower_part = lower_part + lax.ppermute(lower_part, "view", near(2))
        upper = upper + lax.ppermute(upper, "view", near(2))
        lower_part = lower_part + lax.ppermute(lower_part, "view", near(1))
        mine = jnp.concatenate([upper, lower_part])
        other = lax.ppermute(mine, "col", swap)
        merged = jnp.concatenate(
            [jnp.where(col_index == 0, mine, other), jnp.where(col_index == 0, other, mine)]
        )
    else:
        merged = lax.psum(contrib, ("view", "col"))

    if core_count == 2 and sent_size & (sent_size - 1) == 0:
        width = merged.shape[1] // 2
        own = lax.dynamic_slice_in_dim(merged, col_index * width, width, axis=1)
        gram = lax.dot_general(merged, own, (((0,), (0,)), ((), ())), precision=highest)
        bit = 1
        while bit < sent_size:
            gram = gram + lax.ppermute(gram, "sent", [(s, s ^ bit) for s in range(sent_size)])
            bit *= 2
        other = lax.ppermute(gram, "col", [(0, 1), (1, 0)])
        gram = jnp.concatenate(
            [jnp.where(col_index == 0, gram, other), jnp.where(col_index == 0, other, gram)],
            axis=1,
        )
    else:
        gram = lax.dot_general(merged, merged, (((0,), (0,)), ((), ())), precision=highest)
        gram = lax.psum(gram, "sent")
    updated = whiten(gram, merged, math.sqrt(total_rows))
    return (loadings, updated)


def solution(mesh):
    return jax.shard_map(
        shards,
        mesh=mesh,
        in_specs=(P("view", "sent", "col"), P("view"), P("view", "sent", "col"), P("sent", None)),
        out_specs=(P("view", "col", None), P("sent", None)),
        check_vma=False,
    )
```

```python
import functools
import math

import jax
import jax.numpy as jnp
from jax import lax
from jax.experimental import pallas as pl
from jax.experimental.pallas import tpu as pltpu
from jax.sharding import PartitionSpec as P

CHUNK = 256
LANES = 2
PANEL = 32


class Line:
    def __init__(self, lanes, sent_index, col_index):
        self.lanes, self.sent_index, self.col_index = lanes, sent_index, col_index
        self.inner = (sent_index == 1) | (sent_index == 2)
        self.slot, self.chunks, self.pairs, self.totals, self.finals = 0, {}, {}, {}, {}
        self.arrived = {}

    def pairs_of(self, k, stage):
        if k not in self.chunks:
            return []
        _, first, spread = self.chunks[k]
        always = lambda f: True
        if spread:
            hops = (
                {(0, 1): always, (3, 2): lambda f: f < 3},
                {(1, 2): always, (2, 1): lambda f: f <= 1},
                {(2, 3): always, (1, 0): lambda f: f <= 0},
            )
        else:
            hops = (
                {(3, 2): always, (0, 1): lambda f: f <= 0},
                {(2, 1): always, (1, 2): lambda f: f <= 1},
                {(1, 0): always, (2, 3): lambda f: f <= 2},
            )
        cores = len(first)
        return [
            (a * cores + c, b * cores + c)
            for c in range(cores)
            for (a, b), wanted in hops[stage].items()
            if wanted(first[c])
        ]

    def step(self, term=None, first=None, spread=None):
        k = self.slot
        self.slot += 1
        self.collect(k - self.lanes)
        middle, last = k - self.lanes, k - 2 * self.lanes
        if term is not None:
            self.chunks[k] = (term, first, spread)
        ends, pair = term, self.pairs.get(middle)
        if last in self.totals:
            total = self.totals[last]
            ends = total if term is None else jnp.where(self.inner, total, term)
        if ends is not None and pair is not None:
            ends, pair = lax.optimization_barrier((ends, pair))
        axes, ends_in, pair_in = ("sent", "col"), None, None
        if ends is not None:
            perm = self.pairs_of(k, 0) + self.pairs_of(last, 2)
            ends_in = lax.ppermute(ends, axes, perm)
        if pair is not None:
            pair_in = lax.ppermute(pair, axes, self.pairs_of(middle, 1))
        self.arrived[k] = (ends, ends_in, pair_in)

    def collect(self, k):
        if k not in self.arrived:
            return
        ends, ends_in, pair_in = self.arrived.pop(k)
        middle, last = k - self.lanes, k - 2 * self.lanes
        following = self.arrived.get(k + 1, (None,))[0] if self.lanes > 1 else None
        tied = [v for v in (following, ends_in, pair_in) if v is not None]
        tied = list(lax.optimization_barrier(tuple(tied)))
        if following is not None:
            del tied[0]
        if ends_in is not None:
            ends_in = tied.pop(0)
        if pair_in is not None:
            self.totals[middle] = self.pairs[middle] + tied.pop(0)
        if k in self.chunks:
            self.pairs[k] = self.chunks[k][0] + ends_in
        if last in self.totals:
            old, first, _ = self.chunks[last]
            alone = (self.sent_index == 3) & (self.col_index >= [f == 3 for f in first].index(True)) \
                if 3 in first else None
            outer = ends_in if alone is None else jnp.where(alone, ends_in + old, ends_in)
            self.finals[last] = jnp.where(self.inner, ends, outer)


def pieces(x):
    high = x.astype(jnp.bfloat16)
    rest = x - high.astype(jnp.float32)
    middle = rest.astype(jnp.bfloat16)
    return high, middle, (rest - middle.astype(jnp.float32)).astype(jnp.bfloat16)


def whiten_kernel(scale, gram_ref, merged_ref, out_ref, work):
    size = gram_ref.shape[0]
    tile = (8, 128)
    work[:, :size] = gram_ref[...]
    rows = lax.broadcasted_iota(jnp.int32, (size, size), 0)
    work[:, size:] = (rows == lax.broadcasted_iota(jnp.int32, (size, size), 1)).astype(jnp.float32)
    sublane = lax.broadcasted_iota(jnp.int32, tile, 0)
    for panel in range(0, size, PANEL):
        end = panel + PANEL
        start = panel // 128 * 128
        stop = size + start + 128
        for block in range(panel, end, 8):
            lanes = range(start, stop, 128)
            cols = [
                [
                    jnp.broadcast_to(
                        work[t : t + 8, start : start + 128][:, block - start + k][:, None], tile
                    )
                    for k in range(8)
                ]
                for t in range(block, end, 8)
            ]
            low = [
                [jnp.broadcast_to(cols[0][k][i : i + 1], tile) for k in range(i + 1)]
                for i in range(8)
            ]
            inverse = []
            for k in range(8):
                pivot = low[k][k]
                root = lax.rsqrt(pivot)
                root = root * (1.5 - 0.5 * pivot * root * root)
                inverse.append(root)
                for i in range(k + 1, 8):
                    low[i][k] = low[i][k] * root
                for i in range(k + 1, 8):
                    for m in range(k + 1, i + 1):
                        low[i][m] = low[i][m] - low[i][k] * low[m][k]
            for t in range(1, len(cols)):
                for k in range(8):
                    value = cols[t][k]
                    for m in range(k):
                        value = value - low[k][m] * cols[t][m]
                    cols[t][k] = value * inverse[k]
            for lane in lanes:
                here = slice(lane, lane + 128)
                old = work[block : block + 8, here]
                done, new = [], old
                for k in range(8):
                    value = jnp.broadcast_to(old[k : k + 1], tile)
                    for m in range(k):
                        value = value - low[k][m] * done[m]
                    done.append(value * inverse[k])
                    new = jnp.where(sublane == k, done[k], new)
                work[block : block + 8, here] = new
                for t in range(1, len(cols)):
                    at = slice(block + 8 * t, block + 8 * t + 8)
                    value = work[at, here]
                    for k in range(8):
                        value = value - cols[t][k] * done[k]
                    work[at, here] = value
        if end < size:
            first = end // 128 * 128
            upper = pieces(work[panel:end, first:size])
            right = pieces(work[panel:end, first:stop])
            a = jnp.concatenate([upper[i] for i in (0, 0, 1, 1, 0, 2)])
            b = jnp.concatenate([right[i] for i in (0, 1, 0, 1, 2, 0)])
            update = lax.dot_general(
                a, b, (((0,), (0,)), ((), ())), preferred_element_type=jnp.float32
            )
            work[end:, first:stop] -= update[end - first :]
    a = pieces(merged_ref[...])
    b = pieces(work[:, size:] * scale)
    total = 0.0
    for i, j in ((1, 1), (0, 2), (2, 0), (0, 1), (1, 0), (0, 0)):
        total += lax.dot_general(
            a[i], b[j], (((1,), (1,)), ((), ())), preferred_element_type=jnp.float32
        )
    out_ref[...] = total


def whiten(gram, merged, scale):
    size = gram.shape[0]
    return pl.pallas_call(
        functools.partial(whiten_kernel, scale),
        out_shape=jax.ShapeDtypeStruct(merged.shape, jnp.float32),
        in_specs=[pl.BlockSpec(memory_space=pltpu.VMEM)] * 2,
        out_specs=pl.BlockSpec(memory_space=pltpu.VMEM),
        scratch_shapes=[pltpu.VMEM((size, 2 * size), jnp.float32)],
        compiler_params=pltpu.CompilerParams(vmem_limit_bytes=32 * 2**20),
        name="whiten",
    )(gram, merged)


def shards(sketched, widths, inv_factor, shared):
    view_count, row_count, col_half = sketched.shape
    factor_rows = inv_factor.shape[1]
    sent_size = lax.axis_size("sent")
    view_size = lax.axis_size("view")
    core_count = lax.axis_size("col")
    total_rows = row_count * sent_size
    scale = 1.0 / math.sqrt(total_rows)
    high = lax.Precision.HIGH
    highest = lax.Precision.HIGHEST
    col_index = lax.axis_index("col")
    sent_index = lax.axis_index("sent")
    col_pos = col_index * col_half + jnp.arange(col_half)
    keep_cols = (col_pos[None, :] < widths[:, None]).astype(jnp.float32)[:, :, None]
    row_pos = sent_index * factor_rows + jnp.arange(factor_rows)
    keep_rows = (row_pos[None, :] < widths[:, None]).astype(jnp.float32)[:, :, None]
    use_line = sent_size == 4 and core_count == 2 and col_half % CHUNK == 0

    chunk = CHUNK if use_line else col_half
    per_view = col_half // chunk
    slots = [(j, q) for j in range(view_count) for q in range(per_view)]
    firsts = [
        [(c * col_half + q * chunk) // factor_rows for c in range(core_count)] for _, q in slots
    ]

    def columns(array, j, q):
        return array[j, :, q * chunk : (q + 1) * chunk]

    def keep_of(j, q):
        return keep_cols[j, q * chunk : (q + 1) * chunk]

    down = (((0,), (0,)), ((), ()))
    def first_half(proj, j):
        half_part = jnp.dot(inv_factor[j], jnp.concatenate(proj), precision=high)
        if use_line:
            perm = [
                (s * 2 + c, s * 2 + 1 - c)
                for s in range(sent_size)
                for c in range(2)
                if (s + 1) * factor_rows > col_half
            ]
            half = half_part + lax.ppermute(half_part, ("sent", "col"), perm)
        else:
            half = lax.psum(half_part, "col")
        return half * keep_rows[j]

    def cut(whole):
        return [whole[q * chunk : (q + 1) * chunk] for q in range(per_view)]

    def term_of(features):
        return scale * lax.dot_general(features, shared, down, preferred_element_type=jnp.float32)

    terms = [term_of(columns(sketched, 0, q)) for q in range(per_view)]
    for j in range(1, view_count):
        terms += cut(term_of(sketched[j]))

    def back_terms(proj, j):
        return cut(
            lax.dot_general(
                inv_factor[j], first_half(proj, j), down, precision=high,
                preferred_element_type=jnp.float32,
            )
        )

    if use_line:
        line = Line(LANES, sent_index, col_index)
        for term, first in zip(terms, firsts):
            line.step(term, first, True)
        done = 0
        while done < len(slots):
            while done + per_view - 1 not in line.finals:
                line.step()
            proj = [line.finals[done + q] * keep_of(*slots[done + q]) for q in range(per_view)]
            for q, term in enumerate(back_terms(proj, slots[done][0])):
                line.step(term, firsts[q], False)
            done += per_view
        begin = line.slot - len(slots)
        for _ in range(3 * LANES):
            line.step()
        sums = [line.finals[begin + k] for k in range(len(slots))]
    else:
        sums = []
        for j in range(view_count):
            proj = [lax.psum(terms[j], "sent") * keep_of(j, 0)]
            sums += [lax.psum(t, "sent") for t in back_terms(proj, j)]
    loads = [total * keep_of(*slot) for total, slot in zip(sums, slots)]
    loadings = jnp.concatenate(loads).reshape(view_count, col_half, -1)
    contrib = 0.0
    for j in range(view_count):
        whole = jnp.concatenate(loads[j * per_view : (j + 1) * per_view]).astype(jnp.bfloat16)
        contrib += jnp.dot(sketched[j], whole, preferred_element_type=jnp.float32)

    if view_size == 4 and core_count == 2:
        part_rows = row_count // 2
        near = lambda bit: [(v, v ^ bit) for v in range(view_size)]
        swap = [(0, 1), (1, 0)]
        mine = lax.dynamic_slice_in_dim(contrib, col_index * part_rows, part_rows)
        other = lax.dynamic_slice_in_dim(contrib, (1 - col_index) * part_rows, part_rows)
        mine = mine + lax.ppermute(other, "col", swap)
        upper, lower_part = mine[: part_rows // 2], mine[part_rows // 2 :]
        upper = upper + lax.ppermute(upper, "view", near(1))
        lower_part = lower_part + lax.ppermute(lower_part, "view", near(2))
        upper = upper + lax.ppermute(upper, "view", near(2))
        lower_part = lower_part + lax.ppermute(lower_part, "view", near(1))
        mine = jnp.concatenate([upper, lower_part])
        other = lax.ppermute(mine, "col", swap)
        merged = jnp.concatenate(
            [jnp.where(col_index == 0, mine, other), jnp.where(col_index == 0, other, mine)]
        )
        width = mine.shape[1] // 2
        gram = lax.dot_general(mine, mine, (((0,), (0,)), ((), ())), precision=highest)
        left, right = gram[:, :width], gram[:, width:]
        gram = jnp.where(col_index == 0, left, right)
        gram = gram + lax.ppermute(jnp.where(col_index == 0, right, left), "col", swap)
    else:
        merged = lax.psum(contrib, ("view", "col"))
        gram = lax.dot_general(merged, merged, (((0,), (0,)), ((), ())), precision=highest)
        width = gram.shape[1] // core_count
        gram = lax.dynamic_slice_in_dim(gram, col_index * width, width, axis=1)

    if sent_size & (sent_size - 1) == 0:
        bit = 1
        while bit < sent_size:
            gram = gram + lax.ppermute(gram, "sent", [(s, s ^ bit) for s in range(sent_size)])
            bit *= 2
    else:
        gram = lax.psum(gram, "sent")
    if core_count == 2:
        other = lax.ppermute(gram, "col", [(0, 1), (1, 0)])
        gram = jnp.concatenate(
            [jnp.where(col_index == 0, gram, other), jnp.where(col_index == 0, other, gram)],
            axis=1,
        )
    else:
        gram = lax.all_gather(gram, "col", axis=1, tiled=True)
    updated = whiten(gram, merged, math.sqrt(total_rows))
    return (loadings, updated)


def solution(mesh):
    return jax.shard_map(
        shards,
        mesh=mesh,
        in_specs=(P("view", "sent", "col"), P("view"), P("view", "sent", "col"), P("sent", None)),
        out_specs=(P("view", "col", None), P("sent", None)),
        check_vma=False,
    )
```

```python
import functools
import math

import jax
import jax.numpy as jnp
from jax import lax
from jax.experimental import pallas as pl
from jax.experimental.pallas import tpu as pltpu
from jax.sharding import PartitionSpec as P

CHUNK = 512
LANES = 2
PANEL = 32


class Line:
    def __init__(self, lanes, sent_index, col_index):
        self.lanes, self.sent_index, self.col_index = lanes, sent_index, col_index
        self.inner = (sent_index == 1) | (sent_index == 2)
        self.slot, self.chunks, self.pairs, self.totals, self.finals = 0, {}, {}, {}, {}
        self.arrived = {}

    def pairs_of(self, k, stage):
        if k not in self.chunks:
            return []
        _, first, spread = self.chunks[k]
        always = lambda f: True
        if spread:
            hops = (
                {(0, 1): always, (3, 2): lambda f: f < 3},
                {(1, 2): always, (2, 1): lambda f: f <= 1},
                {(2, 3): always, (1, 0): lambda f: f <= 0},
            )
        else:
            hops = (
                {(3, 2): always, (0, 1): lambda f: f <= 0},
                {(2, 1): always, (1, 2): lambda f: f <= 1},
                {(1, 0): always, (2, 3): lambda f: f <= 2},
            )
        cores = len(first)
        return [
            (a * cores + c, b * cores + c)
            for c in range(cores)
            for (a, b), wanted in hops[stage].items()
            if wanted(first[c])
        ]

    def step(self, term=None, first=None, spread=None):
        k = self.slot
        self.slot += 1
        self.collect(k - self.lanes)
        middle, last = k - self.lanes, k - 2 * self.lanes
        if term is not None:
            self.chunks[k] = (term, first, spread)
        ends, pair = term, self.pairs.get(middle)
        if last in self.totals:
            total = self.totals[last]
            ends = total if term is None else jnp.where(self.inner, total, term)
        if ends is not None and pair is not None:
            ends, pair = lax.optimization_barrier((ends, pair))
        axes, ends_in, pair_in = ("sent", "col"), None, None
        if ends is not None:
            perm = self.pairs_of(k, 0) + self.pairs_of(last, 2)
            ends_in = lax.ppermute(ends, axes, perm)
        if pair is not None:
            pair_in = lax.ppermute(pair, axes, self.pairs_of(middle, 1))
        self.arrived[k] = (ends, ends_in, pair_in)

    def collect(self, k):
        if k not in self.arrived:
            return
        ends, ends_in, pair_in = self.arrived.pop(k)
        middle, last = k - self.lanes, k - 2 * self.lanes
        following = self.arrived.get(k + 1, (None,))[0] if self.lanes > 1 else None
        tied = [v for v in (following, ends_in, pair_in) if v is not None]
        tied = list(lax.optimization_barrier(tuple(tied)))
        if following is not None:
            del tied[0]
        if ends_in is not None:
            ends_in = tied.pop(0)
        if pair_in is not None:
            self.totals[middle] = self.pairs[middle] + tied.pop(0)
        if k in self.chunks:
            self.pairs[k] = self.chunks[k][0] + ends_in
        if last in self.totals:
            old, first, _ = self.chunks[last]
            alone = (self.sent_index == 3) & (self.col_index >= [f == 3 for f in first].index(True)) \
                if 3 in first else None
            outer = ends_in if alone is None else jnp.where(alone, ends_in + old, ends_in)
            self.finals[last] = jnp.where(self.inner, ends, outer)


def pieces(x):
    high = x.astype(jnp.bfloat16)
    rest = x - high.astype(jnp.float32)
    middle = rest.astype(jnp.bfloat16)
    return high, middle, (rest - middle.astype(jnp.float32)).astype(jnp.bfloat16)


def whiten_kernel(scale, gram_ref, merged_ref, out_ref, work):
    size = gram_ref.shape[0]
    tile = (8, 128)
    work[:, :size] = gram_ref[...]
    rows = lax.broadcasted_iota(jnp.int32, (size, size), 0)
    work[:, size:] = (rows == lax.broadcasted_iota(jnp.int32, (size, size), 1)).astype(jnp.float32)
    sublane = lax.broadcasted_iota(jnp.int32, tile, 0)
    for panel in range(0, size, PANEL):
        end = panel + PANEL
        start = panel // 128 * 128
        stop = size + start + 128
        for block in range(panel, end, 8):
            lanes = range(start, stop, 128)
            cols = [
                [
                    jnp.broadcast_to(
                        work[t : t + 8, start : start + 128][:, block - start + k][:, None], tile
                    )
                    for k in range(8)
                ]
                for t in range(block, end, 8)
            ]
            low = [
                [jnp.broadcast_to(cols[0][k][i : i + 1], tile) for k in range(i + 1)]
                for i in range(8)
            ]
            inverse = []
            for k in range(8):
                pivot = low[k][k]
                root = lax.rsqrt(pivot)
                root = root * (1.5 - 0.5 * pivot * root * root)
                inverse.append(root)
                for i in range(k + 1, 8):
                    low[i][k] = low[i][k] * root
                for i in range(k + 1, 8):
                    for m in range(k + 1, i + 1):
                        low[i][m] = low[i][m] - low[i][k] * low[m][k]
            for t in range(1, len(cols)):
                for k in range(8):
                    value = cols[t][k]
                    for m in range(k):
                        value = value - low[k][m] * cols[t][m]
                    cols[t][k] = value * inverse[k]
            for lane in lanes:
                here = slice(lane, lane + 128)
                old = work[block : block + 8, here]
                done, new = [], old
                for k in range(8):
                    value = jnp.broadcast_to(old[k : k + 1], tile)
                    for m in range(k):
                        value = value - low[k][m] * done[m]
                    done.append(value * inverse[k])
                    new = jnp.where(sublane == k, done[k], new)
                work[block : block + 8, here] = new
                for t in range(1, len(cols)):
                    at = slice(block + 8 * t, block + 8 * t + 8)
                    value = work[at, here]
                    for k in range(8):
                        value = value - cols[t][k] * done[k]
                    work[at, here] = value
        if end < size:
            first = end // 128 * 128
            upper = pieces(work[panel:end, first:size])
            right = pieces(work[panel:end, first:stop])
            a = jnp.concatenate([upper[i] for i in (0, 0, 1, 1, 0, 2)])
            b = jnp.concatenate([right[i] for i in (0, 1, 0, 1, 2, 0)])
            update = lax.dot_general(
                a, b, (((0,), (0,)), ((), ())), preferred_element_type=jnp.float32
            )
            work[end:, first:stop] -= update[end - first :]
    a = pieces(merged_ref[...])
    b = pieces(work[:, size:] * scale)
    total = 0.0
    for i, j in ((1, 1), (0, 2), (2, 0), (0, 1), (1, 0), (0, 0)):
        total += lax.dot_general(
            a[i], b[j], (((1,), (1,)), ((), ())), preferred_element_type=jnp.float32
        )
    out_ref[...] = total


def whiten(gram, merged, scale):
    size = gram.shape[0]
    return pl.pallas_call(
        functools.partial(whiten_kernel, scale),
        out_shape=jax.ShapeDtypeStruct(merged.shape, jnp.float32),
        in_specs=[pl.BlockSpec(memory_space=pltpu.VMEM)] * 2,
        out_specs=pl.BlockSpec(memory_space=pltpu.VMEM),
        scratch_shapes=[pltpu.VMEM((size, 2 * size), jnp.float32)],
        compiler_params=pltpu.CompilerParams(vmem_limit_bytes=32 * 2**20),
        name="whiten",
    )(gram, merged)


def shards(sketched, widths, inv_factor, shared):
    view_count, row_count, col_half = sketched.shape
    factor_rows = inv_factor.shape[1]
    sent_size = lax.axis_size("sent")
    view_size = lax.axis_size("view")
    core_count = lax.axis_size("col")
    total_rows = row_count * sent_size
    scale = 1.0 / math.sqrt(total_rows)
    high = lax.Precision.HIGH
    highest = lax.Precision.HIGHEST
    col_index = lax.axis_index("col")
    sent_index = lax.axis_index("sent")
    col_pos = col_index * col_half + jnp.arange(col_half)
    keep_cols = (col_pos[None, :] < widths[:, None]).astype(jnp.float32)[:, :, None]
    row_pos = sent_index * factor_rows + jnp.arange(factor_rows)
    keep_rows = (row_pos[None, :] < widths[:, None]).astype(jnp.float32)[:, :, None]
    use_line = sent_size == 4 and core_count == 2 and col_half % CHUNK == 0

    chunk = CHUNK if use_line else col_half
    per_view = col_half // chunk
    slots = [(j, q) for j in range(view_count) for q in range(per_view)]
    firsts = [
        [(c * col_half + q * chunk) // factor_rows for c in range(core_count)] for _, q in slots
    ]

    def keep_of(j, q):
        return keep_cols[j, q * chunk : (q + 1) * chunk]

    down = (((0,), (0,)), ((), ()))
    def first_half(proj, j):
        half_part = jnp.dot(inv_factor[j], jnp.concatenate(proj), precision=high)
        if use_line:
            perm = [
                (s * 2 + c, s * 2 + 1 - c)
                for s in range(sent_size)
                for c in range(2)
                if (s + 1) * factor_rows > col_half
            ]
            half = half_part + lax.ppermute(half_part, ("sent", "col"), perm)
        else:
            half = lax.psum(half_part, "col")
        return half * keep_rows[j]

    def cut(whole):
        return [whole[q * chunk : (q + 1) * chunk] for q in range(per_view)]

    def term_of(features):
        return scale * lax.dot_general(features, shared, down, preferred_element_type=jnp.float32)

    terms = []
    for j in range(view_count):
        terms += cut(term_of(sketched[j]))

    def back_terms(proj, j):
        return cut(
            lax.dot_general(
                inv_factor[j], first_half(proj, j), down, precision=high,
                preferred_element_type=jnp.float32,
            )
        )

    if use_line:
        line = Line(LANES, sent_index, col_index)
        for term, first in zip(terms, firsts):
            line.step(term, first, True)
        done = 0
        while done < len(slots):
            while done + per_view - 1 not in line.finals:
                line.step()
            proj = [line.finals[done + q] * keep_of(*slots[done + q]) for q in range(per_view)]
            for q, term in enumerate(back_terms(proj, slots[done][0])):
                line.step(term, firsts[q], False)
            done += per_view
        begin = line.slot - len(slots)
        for _ in range(3 * LANES):
            line.step()
        sums = [line.finals[begin + k] for k in range(len(slots))]
    else:
        sums = []
        for j in range(view_count):
            proj = [lax.psum(terms[j], "sent") * keep_of(j, 0)]
            sums += [lax.psum(t, "sent") for t in back_terms(proj, j)]
    loads = [total * keep_of(*slot) for total, slot in zip(sums, slots)]
    loadings = jnp.concatenate(loads).reshape(view_count, col_half, -1)
    contrib = 0.0
    for j in range(view_count):
        whole = jnp.concatenate(loads[j * per_view : (j + 1) * per_view]).astype(jnp.bfloat16)
        contrib += jnp.dot(sketched[j], whole, preferred_element_type=jnp.float32)

    if view_size == 4 and core_count == 2:
        part_rows = row_count // 2
        near = lambda bit: [(v, v ^ bit) for v in range(view_size)]
        swap = [(0, 1), (1, 0)]
        mine = lax.dynamic_slice_in_dim(contrib, col_index * part_rows, part_rows)
        other = lax.dynamic_slice_in_dim(contrib, (1 - col_index) * part_rows, part_rows)
        mine = mine + lax.ppermute(other, "col", swap)
        upper, lower_part = mine[: part_rows // 2], mine[part_rows // 2 :]
        upper = upper + lax.ppermute(upper, "view", near(1))
        lower_part = lower_part + lax.ppermute(lower_part, "view", near(2))
        upper = upper + lax.ppermute(upper, "view", near(2))
        lower_part = lower_part + lax.ppermute(lower_part, "view", near(1))
        mine = jnp.concatenate([upper, lower_part])
        other = lax.ppermute(mine, "col", swap)
        merged = jnp.concatenate(
            [jnp.where(col_index == 0, mine, other), jnp.where(col_index == 0, other, mine)]
        )
        width = mine.shape[1] // 2
        gram = lax.dot_general(mine, mine, (((0,), (0,)), ((), ())), precision=highest)
        left, right = gram[:, :width], gram[:, width:]
        gram = jnp.where(col_index == 0, left, right)
        gram = gram + lax.ppermute(jnp.where(col_index == 0, right, left), "col", swap)
    else:
        merged = lax.psum(contrib, ("view", "col"))
        gram = lax.dot_general(merged, merged, (((0,), (0,)), ((), ())), precision=highest)
        width = gram.shape[1] // core_count
        gram = lax.dynamic_slice_in_dim(gram, col_index * width, width, axis=1)

    if sent_size & (sent_size - 1) == 0:
        bit = 1
        while bit < sent_size:
            gram = gram + lax.ppermute(gram, "sent", [(s, s ^ bit) for s in range(sent_size)])
            bit *= 2
    else:
        gram = lax.psum(gram, "sent")
    if core_count == 2:
        other = lax.ppermute(gram, "col", [(0, 1), (1, 0)])
        gram = jnp.concatenate(
            [jnp.where(col_index == 0, gram, other), jnp.where(col_index == 0, other, gram)],
            axis=1,
        )
    else:
        gram = lax.all_gather(gram, "col", axis=1, tiled=True)
    updated = whiten(gram, merged, math.sqrt(total_rows))
    return (loadings, updated)


def solution(mesh):
    return jax.shard_map(
        shards,
        mesh=mesh,
        in_specs=(P("view", "sent", "col"), P("view"), P("view", "sent", "col"), P("sent", None)),
        out_specs=(P("view", "col", None), P("sent", None)),
        check_vma=False,
    )
```

```python
import functools
import math

import jax
import jax.numpy as jnp
from jax import lax
from jax.experimental import pallas as pl
from jax.experimental.pallas import tpu as pltpu
from jax.sharding import PartitionSpec as P

CHUNK = 512
LANES = 2
PANEL = 32


class Line:
    def __init__(self, lanes, count, sent_index, col_index):
        self.lanes, self.sent_index, self.col_index = lanes, sent_index, col_index
        self.inner = (sent_index == 1) | (sent_index == 2)
        self.slots = lanes * (2 * (count // lanes) + 2)
        self.chunks, self.sums, self.arrived, self.half, self.finals = [], {}, {}, {}, {}

    def hops(self, k, core, stage):
        if not 0 <= k < len(self.chunks):
            return []
        _, first, spread = self.chunks[k]
        f = first[core]
        if spread:
            wanted = (
                {(0, 1): True, (3, 2): f < 3},
                {(1, 2): True, (2, 1): f <= 1},
                {(2, 3): True, (1, 0): f <= 0},
            )
        else:
            wanted = (
                {(3, 2): True, (0, 1): f <= 0},
                {(2, 1): True, (1, 2): f <= 1},
                {(1, 0): True, (2, 3): f <= 2},
            )
        return [(a * 2 + core, b * 2 + core) for (a, b), yes in wanted[stage].items() if yes]

    def due(self, slot):
        lane, turn = slot % self.lanes, slot // self.lanes
        k = turn // 2 * self.lanes + lane
        return lane, turn % 2, k, k - self.lanes

    def step(self, slot):
        self.collect(slot - self.lanes)
        lane, core, k, last = self.due(slot)
        term = self.chunks[k][0] if k < len(self.chunks) else None
        held = self.sums.get(lane)
        if term is None or held is None:
            payload = held if term is None else term
        else:
            payload = jnp.where((self.col_index == core) & ~self.inner, term, held)
        perm = self.hops(k, core, 0) + self.hops(last, core, 2)
        perm += self.hops(k if core else last, 1 - core, 1)
        self.arrived[slot] = (payload, lax.ppermute(payload, ("sent", "col"), perm))

    def collect(self, slot):
        if slot not in self.arrived:
            return
        payload, brought = self.arrived.pop(slot)
        if slot + 1 in self.arrived:
            following = self.arrived[slot + 1][0]
            _, brought = lax.optimization_barrier((following, brought))
        lane, core, k, last = self.due(slot)
        held = self.sums.get(lane)
        base = held
        if k < len(self.chunks):
            term = self.chunks[k][0]
            base = term if held is None else jnp.where(self.col_index == core, term, held)
        self.sums[lane] = base + brought
        if last >= 0:
            old, first, _ = self.chunks[last]
            outer = brought
            if first[core] == 3:
                outer = jnp.where(self.sent_index == 3, brought + old, brought)
            final = jnp.where(self.inner, payload, outer)
            if core == 0:
                self.half[last] = final
            else:
                self.finals[last] = jnp.where(self.col_index == 0, self.half.pop(last), final)


def pieces(x):
    high = x.astype(jnp.bfloat16)
    rest = x - high.astype(jnp.float32)
    middle = rest.astype(jnp.bfloat16)
    return high, middle, (rest - middle.astype(jnp.float32)).astype(jnp.bfloat16)


def whiten_kernel(scale, gram_ref, merged_ref, out_ref, work):
    size = gram_ref.shape[0]
    tile = (8, 128)
    work[:, :size] = gram_ref[...]
    rows = lax.broadcasted_iota(jnp.int32, (size, size), 0)
    work[:, size:] = (rows == lax.broadcasted_iota(jnp.int32, (size, size), 1)).astype(jnp.float32)
    sublane = lax.broadcasted_iota(jnp.int32, tile, 0)
    for panel in range(0, size, PANEL):
        end = panel + PANEL
        start = panel // 128 * 128
        stop = size + start + 128
        for block in range(panel, end, 8):
            lanes = range(start, stop, 128)
            cols = [
                [
                    jnp.broadcast_to(
                        work[t : t + 8, start : start + 128][:, block - start + k][:, None], tile
                    )
                    for k in range(8)
                ]
                for t in range(block, end, 8)
            ]
            low = [
                [jnp.broadcast_to(cols[0][k][i : i + 1], tile) for k in range(i + 1)]
                for i in range(8)
            ]
            inverse = []
            for k in range(8):
                pivot = low[k][k]
                root = lax.rsqrt(pivot)
                root = root * (1.5 - 0.5 * pivot * root * root)
                inverse.append(root)
                for i in range(k + 1, 8):
                    low[i][k] = low[i][k] * root
                for i in range(k + 1, 8):
                    for m in range(k + 1, i + 1):
                        low[i][m] = low[i][m] - low[i][k] * low[m][k]
            for t in range(1, len(cols)):
                for k in range(8):
                    value = cols[t][k]
                    for m in range(k):
                        value = value - low[k][m] * cols[t][m]
                    cols[t][k] = value * inverse[k]
            for lane in lanes:
                here = slice(lane, lane + 128)
                old = work[block : block + 8, here]
                done, new = [], old
                for k in range(8):
                    value = jnp.broadcast_to(old[k : k + 1], tile)
                    for m in range(k):
                        value = value - low[k][m] * done[m]
                    done.append(value * inverse[k])
                    new = jnp.where(sublane == k, done[k], new)
                work[block : block + 8, here] = new
                for t in range(1, len(cols)):
                    at = slice(block + 8 * t, block + 8 * t + 8)
                    value = work[at, here]
                    for k in range(8):
                        value = value - cols[t][k] * done[k]
                    work[at, here] = value
        if end < size:
            first = end // 128 * 128
            upper = pieces(work[panel:end, first:size])
            right = pieces(work[panel:end, first:stop])
            a = jnp.concatenate([upper[i] for i in (0, 0, 1, 1, 0, 2)])
            b = jnp.concatenate([right[i] for i in (0, 1, 0, 1, 2, 0)])
            update = lax.dot_general(
                a, b, (((0,), (0,)), ((), ())), preferred_element_type=jnp.float32
            )
            work[end:, first:stop] -= update[end - first :]
    a = pieces(merged_ref[...])
    b = pieces(work[:, size:] * scale)
    total = 0.0
    for i, j in ((1, 1), (0, 2), (2, 0), (0, 1), (1, 0), (0, 0)):
        total += lax.dot_general(
            a[i], b[j], (((1,), (1,)), ((), ())), preferred_element_type=jnp.float32
        )
    out_ref[...] = total


def whiten(gram, merged, scale):
    size = gram.shape[0]
    return pl.pallas_call(
        functools.partial(whiten_kernel, scale),
        out_shape=jax.ShapeDtypeStruct(merged.shape, jnp.float32),
        in_specs=[pl.BlockSpec(memory_space=pltpu.VMEM)] * 2,
        out_specs=pl.BlockSpec(memory_space=pltpu.VMEM),
        scratch_shapes=[pltpu.VMEM((size, 2 * size), jnp.float32)],
        compiler_params=pltpu.CompilerParams(vmem_limit_bytes=32 * 2**20),
        name="whiten",
    )(gram, merged)


def shards(sketched, widths, inv_factor, shared):
    view_count, row_count, col_half = sketched.shape
    factor_rows = inv_factor.shape[1]
    sent_size = lax.axis_size("sent")
    view_size = lax.axis_size("view")
    core_count = lax.axis_size("col")
    total_rows = row_count * sent_size
    scale = 1.0 / math.sqrt(total_rows)
    high = lax.Precision.HIGH
    highest = lax.Precision.HIGHEST
    col_index = lax.axis_index("col")
    sent_index = lax.axis_index("sent")
    col_pos = col_index * col_half + jnp.arange(col_half)
    keep_cols = (col_pos[None, :] < widths[:, None]).astype(jnp.float32)[:, :, None]
    row_pos = sent_index * factor_rows + jnp.arange(factor_rows)
    keep_rows = (row_pos[None, :] < widths[:, None]).astype(jnp.float32)[:, :, None]
    use_line = sent_size == 4 and core_count == 2 and col_half % (LANES * CHUNK) == 0

    chunk = CHUNK if use_line else col_half
    per_view = col_half // chunk
    slots = [(j, q) for j in range(view_count) for q in range(per_view)]
    firsts = [
        [(c * col_half + q * chunk) // factor_rows for c in range(core_count)] for _, q in slots
    ]

    def keep_of(j, q):
        return keep_cols[j, q * chunk : (q + 1) * chunk]

    down = (((0,), (0,)), ((), ()))
    def first_half(proj, j):
        half_part = jnp.dot(inv_factor[j], jnp.concatenate(proj), precision=high)
        if use_line:
            perm = [
                (s * 2 + c, s * 2 + 1 - c)
                for s in range(sent_size)
                for c in range(2)
                if (s + 1) * factor_rows > col_half
            ]
            half = half_part + lax.ppermute(half_part, ("sent", "col"), perm)
        else:
            half = lax.psum(half_part, "col")
        return half * keep_rows[j]

    def cut(whole):
        return [whole[q * chunk : (q + 1) * chunk] for q in range(per_view)]

    def term_of(features):
        return scale * lax.dot_general(features, shared, down, preferred_element_type=jnp.float32)

    terms = []
    for j in range(view_count):
        terms += cut(term_of(sketched[j]))

    def back_terms(proj, j):
        return cut(
            lax.dot_general(
                inv_factor[j], first_half(proj, j), down, precision=high,
                preferred_element_type=jnp.float32,
            )
        )

    if use_line:
        line = Line(LANES, 2 * len(slots), sent_index, col_index)
        for term, first in zip(terms, firsts):
            line.chunks.append((term, first, True))
        for slot in range(line.slots + LANES):
            done = len(line.chunks) - len(slots)
            if slot < line.slots and line.due(slot)[2] == len(slots) + done and done < len(slots):
                j = slots[done][0]
                proj = [line.finals[done + q] * keep_of(j, q) for q in range(per_view)]
                for q, term in enumerate(back_terms(proj, j)):
                    line.chunks.append((term, firsts[q], False))
            if slot < line.slots:
                line.step(slot)
            else:
                line.collect(slot - LANES)
        sums = [line.finals[len(slots) + k] for k in range(len(slots))]
    else:
        sums = []
        for j in range(view_count):
            proj = [lax.psum(terms[j], "sent") * keep_of(j, 0)]
            sums += [lax.psum(t, "sent") for t in back_terms(proj, j)]
    loads = [total * keep_of(*slot) for total, slot in zip(sums, slots)]
    loadings = jnp.concatenate(loads).reshape(view_count, col_half, -1)
    contrib = 0.0
    for j in range(view_count):
        whole = jnp.concatenate(loads[j * per_view : (j + 1) * per_view]).astype(jnp.bfloat16)
        contrib += jnp.dot(sketched[j], whole, preferred_element_type=jnp.float32)

    if view_size == 4 and core_count == 2:
        part_rows = row_count // 2
        near = lambda bit: [(v, v ^ bit) for v in range(view_size)]
        swap = [(0, 1), (1, 0)]
        mine = lax.dynamic_slice_in_dim(contrib, col_index * part_rows, part_rows)
        other = lax.dynamic_slice_in_dim(contrib, (1 - col_index) * part_rows, part_rows)
        mine = mine + lax.ppermute(other, "col", swap)
        upper, lower_part = mine[: part_rows // 2], mine[part_rows // 2 :]
        upper = upper + lax.ppermute(upper, "view", near(1))
        lower_part = lower_part + lax.ppermute(lower_part, "view", near(2))
        upper = upper + lax.ppermute(upper, "view", near(2))
        lower_part = lower_part + lax.ppermute(lower_part, "view", near(1))
        mine = jnp.concatenate([upper, lower_part])
        other = lax.ppermute(mine, "col", swap)
        merged = jnp.concatenate(
            [jnp.where(col_index == 0, mine, other), jnp.where(col_index == 0, other, mine)]
        )
        width = mine.shape[1] // 2
        gram = lax.dot_general(mine, mine, (((0,), (0,)), ((), ())), precision=highest)
        left, right = gram[:, :width], gram[:, width:]
        gram = jnp.where(col_index == 0, left, right)
        gram = gram + lax.ppermute(jnp.where(col_index == 0, right, left), "col", swap)
    else:
        merged = lax.psum(contrib, ("view", "col"))
        gram = lax.dot_general(merged, merged, (((0,), (0,)), ((), ())), precision=highest)
        width = gram.shape[1] // core_count
        gram = lax.dynamic_slice_in_dim(gram, col_index * width, width, axis=1)

    if sent_size & (sent_size - 1) == 0:
        bit = 1
        while bit < sent_size:
            gram = gram + lax.ppermute(gram, "sent", [(s, s ^ bit) for s in range(sent_size)])
            bit *= 2
    else:
        gram = lax.psum(gram, "sent")
    if core_count == 2:
        other = lax.ppermute(gram, "col", [(0, 1), (1, 0)])
        gram = jnp.concatenate(
            [jnp.where(col_index == 0, gram, other), jnp.where(col_index == 0, other, gram)],
            axis=1,
        )
    else:
        gram = lax.all_gather(gram, "col", axis=1, tiled=True)
    updated = whiten(gram, merged, math.sqrt(total_rows))
    return (loadings, updated)


def solution(mesh):
    return jax.shard_map(
        shards,
        mesh=mesh,
        in_specs=(P("view", "sent", "col"), P("view"), P("view", "sent", "col"), P("sent", None)),
        out_specs=(P("view", "col", None), P("sent", None)),
        check_vma=False,
    )
```

```python
import functools
import math

import jax
import jax.numpy as jnp
from jax import lax
from jax.experimental import pallas as pl
from jax.experimental.pallas import tpu as pltpu
from jax.sharding import PartitionSpec as P

CHUNK = 256
LANES = 2
PANEL = 32


class Line:
    def __init__(self, lanes, sent_index, col_index):
        self.lanes, self.sent_index, self.col_index = lanes, sent_index, col_index
        self.inner = (sent_index == 1) | (sent_index == 2)
        self.slot, self.chunks, self.pairs, self.totals, self.finals = 0, {}, {}, {}, {}
        self.arrived = {}

    def pairs_of(self, k, stage):
        if k not in self.chunks:
            return []
        _, first, spread = self.chunks[k]
        always = lambda f: True
        if spread:
            hops = (
                {(0, 1): always, (3, 2): lambda f: f < 3},
                {(1, 2): always, (2, 1): lambda f: f <= 1},
                {(2, 3): always, (1, 0): lambda f: f <= 0},
            )
        else:
            hops = (
                {(3, 2): always, (0, 1): lambda f: f <= 0},
                {(2, 1): always, (1, 2): lambda f: f <= 1},
                {(1, 0): always, (2, 3): lambda f: f <= 2},
            )
        cores = len(first)
        return [
            (a * cores + c, b * cores + c)
            for c in range(cores)
            for (a, b), wanted in hops[stage].items()
            if wanted(first[c])
        ]

    def step(self, term=None, first=None, spread=None):
        k = self.slot
        self.slot += 1
        self.collect(k - self.lanes)
        middle, last = k - self.lanes, k - 2 * self.lanes
        if term is not None:
            self.chunks[k] = (term, first, spread)
        ends, pair = term, self.pairs.get(middle)
        if last in self.totals:
            total = self.totals[last]
            ends = total if term is None else jnp.where(self.inner, total, term)
        axes, ends_in, pair_in = ("sent", "col"), None, None
        if ends is not None:
            perm = self.pairs_of(k, 0) + self.pairs_of(last, 2)
            ends_in = lax.ppermute(ends, axes, perm)
        if pair is not None:
            pair_in = lax.ppermute(pair, axes, self.pairs_of(middle, 1))
        self.arrived[k] = (ends, ends_in, pair_in)

    def collect(self, k):
        if k not in self.arrived:
            return
        ends, ends_in, pair_in = self.arrived.pop(k)
        middle, last = k - self.lanes, k - 2 * self.lanes
        following = self.arrived.get(k + 1, (None,))[0] if self.lanes > 1 else None
        tied = [v for v in (following, ends_in, pair_in) if v is not None]
        tied = list(lax.optimization_barrier(tuple(tied)))
        if following is not None:
            del tied[0]
        if ends_in is not None:
            ends_in = tied.pop(0)
        if pair_in is not None:
            self.totals[middle] = self.pairs[middle] + tied.pop(0)
        if k in self.chunks:
            self.pairs[k] = self.chunks[k][0] + ends_in
        if last in self.totals:
            old, first, _ = self.chunks[last]
            alone = (self.sent_index == 3) & (self.col_index >= [f == 3 for f in first].index(True)) \
                if 3 in first else None
            outer = ends_in if alone is None else jnp.where(alone, ends_in + old, ends_in)
            self.finals[last] = jnp.where(self.inner, ends, outer)


def pieces(x):
    high = x.astype(jnp.bfloat16)
    rest = x - high.astype(jnp.float32)
    middle = rest.astype(jnp.bfloat16)
    return high, middle, (rest - middle.astype(jnp.float32)).astype(jnp.bfloat16)


def whiten_kernel(scale, gram_ref, merged_ref, out_ref, work):
    size = gram_ref.shape[0]
    tile = (8, 128)
    work[:, :size] = gram_ref[...]
    rows = lax.broadcasted_iota(jnp.int32, (size, size), 0)
    work[:, size:] = (rows == lax.broadcasted_iota(jnp.int32, (size, size), 1)).astype(jnp.float32)
    sublane = lax.broadcasted_iota(jnp.int32, tile, 0)
    for panel in range(0, size, PANEL):
        end = panel + PANEL
        start = panel // 128 * 128
        stop = size + start + 128
        for block in range(panel, end, 8):
            lanes = range(start, stop, 128)
            cols = [
                [
                    jnp.broadcast_to(
                        work[t : t + 8, start : start + 128][:, block - start + k][:, None], tile
                    )
                    for k in range(8)
                ]
                for t in range(block, end, 8)
            ]
            low = [
                [jnp.broadcast_to(cols[0][k][i : i + 1], tile) for k in range(i + 1)]
                for i in range(8)
            ]
            inverse = []
            for k in range(8):
                pivot = low[k][k]
                root = lax.rsqrt(pivot)
                root = root * (1.5 - 0.5 * pivot * root * root)
                inverse.append(root)
                for i in range(k + 1, 8):
                    low[i][k] = low[i][k] * root
                for i in range(k + 1, 8):
                    for m in range(k + 1, i + 1):
                        low[i][m] = low[i][m] - low[i][k] * low[m][k]
            for t in range(1, len(cols)):
                for k in range(8):
                    value = cols[t][k]
                    for m in range(k):
                        value = value - low[k][m] * cols[t][m]
                    cols[t][k] = value * inverse[k]
            for lane in lanes:
                here = slice(lane, lane + 128)
                old = work[block : block + 8, here]
                done, new = [], old
                for k in range(8):
                    value = jnp.broadcast_to(old[k : k + 1], tile)
                    for m in range(k):
                        value = value - low[k][m] * done[m]
                    done.append(value * inverse[k])
                    new = jnp.where(sublane == k, done[k], new)
                work[block : block + 8, here] = new
                for t in range(1, len(cols)):
                    at = slice(block + 8 * t, block + 8 * t + 8)
                    value = work[at, here]
                    for k in range(8):
                        value = value - cols[t][k] * done[k]
                    work[at, here] = value
        if end < size:
            first = end // 128 * 128
            upper = pieces(work[panel:end, first:size])
            right = pieces(work[panel:end, first:stop])
            a = jnp.concatenate([upper[i] for i in (0, 0, 1, 1, 0, 2)])
            b = jnp.concatenate([right[i] for i in (0, 1, 0, 1, 2, 0)])
            update = lax.dot_general(
                a, b, (((0,), (0,)), ((), ())), preferred_element_type=jnp.float32
            )
            work[end:, first:stop] -= update[end - first :]
    a = pieces(merged_ref[...])
    b = pieces(work[:, size:] * scale)
    total = 0.0
    for i, j in ((1, 1), (0, 2), (2, 0), (0, 1), (1, 0), (0, 0)):
        total += lax.dot_general(
            a[i], b[j], (((1,), (1,)), ((), ())), preferred_element_type=jnp.float32
        )
    out_ref[...] = total


def whiten(gram, merged, scale):
    size = gram.shape[0]
    return pl.pallas_call(
        functools.partial(whiten_kernel, scale),
        out_shape=jax.ShapeDtypeStruct(merged.shape, jnp.float32),
        in_specs=[pl.BlockSpec(memory_space=pltpu.VMEM)] * 2,
        out_specs=pl.BlockSpec(memory_space=pltpu.VMEM),
        scratch_shapes=[pltpu.VMEM((size, 2 * size), jnp.float32)],
        compiler_params=pltpu.CompilerParams(vmem_limit_bytes=32 * 2**20),
        name="whiten",
    )(gram, merged)


def shards(sketched, widths, inv_factor, shared):
    view_count, row_count, col_half = sketched.shape
    factor_rows = inv_factor.shape[1]
    sent_size = lax.axis_size("sent")
    view_size = lax.axis_size("view")
    core_count = lax.axis_size("col")
    total_rows = row_count * sent_size
    scale = 1.0 / math.sqrt(total_rows)
    high = lax.Precision.HIGH
    highest = lax.Precision.HIGHEST
    col_index = lax.axis_index("col")
    sent_index = lax.axis_index("sent")
    col_pos = col_index * col_half + jnp.arange(col_half)
    keep_cols = (col_pos[None, :] < widths[:, None]).astype(jnp.float32)[:, :, None]
    row_pos = sent_index * factor_rows + jnp.arange(factor_rows)
    keep_rows = (row_pos[None, :] < widths[:, None]).astype(jnp.float32)[:, :, None]
    use_line = sent_size == 4 and core_count == 2 and col_half % CHUNK == 0

    chunk = CHUNK if use_line else col_half
    per_view = col_half // chunk
    slots = [(j, q) for j in range(view_count) for q in range(per_view)]
    firsts = [
        [(c * col_half + q * chunk) // factor_rows for c in range(core_count)] for _, q in slots
    ]

    def keep_of(j, q):
        return keep_cols[j, q * chunk : (q + 1) * chunk]

    down = (((0,), (0,)), ((), ()))
    def first_half(proj, j):
        half_part = jnp.dot(inv_factor[j], jnp.concatenate(proj), precision=high)
        if use_line:
            perm = [
                (s * 2 + c, s * 2 + 1 - c)
                for s in range(sent_size)
                for c in range(2)
                if (s + 1) * factor_rows > col_half
            ]
            half = half_part + lax.ppermute(half_part, ("sent", "col"), perm)
        else:
            half = lax.psum(half_part, "col")
        return half * keep_rows[j]

    def cut(whole):
        return [whole[q * chunk : (q + 1) * chunk] for q in range(per_view)]

    def term_of(features):
        return scale * lax.dot_general(features, shared, down, preferred_element_type=jnp.float32)

    terms = []
    for j in range(view_count):
        terms += cut(term_of(sketched[j]))

    def back_terms(proj, j):
        return cut(
            lax.dot_general(
                inv_factor[j], first_half(proj, j), down, precision=high,
                preferred_element_type=jnp.float32,
            )
        )

    if use_line:
        line = Line(LANES, sent_index, col_index)
        for term, first in zip(terms, firsts):
            line.step(term, first, True)
        done = 0
        while done < len(slots):
            while done + per_view - 1 not in line.finals:
                line.step()
            proj = [line.finals[done + q] * keep_of(*slots[done + q]) for q in range(per_view)]
            for q, term in enumerate(back_terms(proj, slots[done][0])):
                line.step(term, firsts[q], False)
            done += per_view
        begin = line.slot - len(slots)
        for _ in range(3 * LANES):
            line.step()
        sums = [line.finals[begin + k] for k in range(len(slots))]
    else:
        sums = []
        for j in range(view_count):
            proj = [lax.psum(terms[j], "sent") * keep_of(j, 0)]
            sums += [lax.psum(t, "sent") for t in back_terms(proj, j)]
    loads = [total * keep_of(*slot) for total, slot in zip(sums, slots)]
    loadings = jnp.concatenate(loads).reshape(view_count, col_half, -1)
    contrib = 0.0
    for j in range(view_count):
        whole = jnp.concatenate(loads[j * per_view : (j + 1) * per_view]).astype(jnp.bfloat16)
        contrib += jnp.dot(sketched[j], whole, preferred_element_type=jnp.float32)

    if view_size == 4 and core_count == 2:
        part_rows = row_count // 2
        near = lambda bit: [(v, v ^ bit) for v in range(view_size)]
        swap = [(0, 1), (1, 0)]
        mine = lax.dynamic_slice_in_dim(contrib, col_index * part_rows, part_rows)
        other = lax.dynamic_slice_in_dim(contrib, (1 - col_index) * part_rows, part_rows)
        mine = mine + lax.ppermute(other, "col", swap)
        upper, lower_part = mine[: part_rows // 2], mine[part_rows // 2 :]
        upper = upper + lax.ppermute(upper, "view", near(1))
        lower_part = lower_part + lax.ppermute(lower_part, "view", near(2))
        upper = upper + lax.ppermute(upper, "view", near(2))
        lower_part = lower_part + lax.ppermute(lower_part, "view", near(1))
        mine = jnp.concatenate([upper, lower_part])
        other = lax.ppermute(mine, "col", swap)
        merged = jnp.concatenate(
            [jnp.where(col_index == 0, mine, other), jnp.where(col_index == 0, other, mine)]
        )
        width = mine.shape[1] // 2
        gram = lax.dot_general(mine, mine, (((0,), (0,)), ((), ())), precision=highest)
        left, right = gram[:, :width], gram[:, width:]
        gram = jnp.where(col_index == 0, left, right)
        gram = gram + lax.ppermute(jnp.where(col_index == 0, right, left), "col", swap)
    else:
        merged = lax.psum(contrib, ("view", "col"))
        gram = lax.dot_general(merged, merged, (((0,), (0,)), ((), ())), precision=highest)
        width = gram.shape[1] // core_count
        gram = lax.dynamic_slice_in_dim(gram, col_index * width, width, axis=1)

    if sent_size & (sent_size - 1) == 0:
        bit = 1
        while bit < sent_size:
            gram = gram + lax.ppermute(gram, "sent", [(s, s ^ bit) for s in range(sent_size)])
            bit *= 2
    else:
        gram = lax.psum(gram, "sent")
    if core_count == 2:
        other = lax.ppermute(gram, "col", [(0, 1), (1, 0)])
        gram = jnp.concatenate(
            [jnp.where(col_index == 0, gram, other), jnp.where(col_index == 0, other, gram)],
            axis=1,
        )
    else:
        gram = lax.all_gather(gram, "col", axis=1, tiled=True)
    updated = whiten(gram, merged, math.sqrt(total_rows))
    return (loadings, updated)


def solution(mesh):
    return jax.shard_map(
        shards,
        mesh=mesh,
        in_specs=(P("view", "sent", "col"), P("view"), P("view", "sent", "col"), P("sent", None)),
        out_specs=(P("view", "col", None), P("sent", None)),
        check_vma=False,
    )
```

```python
import functools
import math

import jax
import jax.numpy as jnp
from jax import lax
from jax.experimental import pallas as pl
from jax.experimental.pallas import tpu as pltpu
from jax.sharding import PartitionSpec as P

CHUNK = 256
LANES = 3
PANEL = 32


class Line:
    def __init__(self, lanes, count, sent_index, col_index):
        self.lanes, self.sent_index, self.col_index = lanes, sent_index, col_index
        self.inner = (sent_index == 1) | (sent_index == 2)
        self.slots = lanes * (2 * (count // lanes) + 2)
        self.chunks, self.sums, self.arrived, self.half, self.finals = [], {}, {}, {}, {}
        self.payloads = {}

    def hops(self, k, core, stage):
        if not 0 <= k < len(self.chunks):
            return []
        _, first, spread = self.chunks[k]
        f = first[core]
        if spread:
            wanted = (
                {(0, 1): True, (3, 2): f < 3},
                {(1, 2): True, (2, 1): f <= 1},
                {(2, 3): True, (1, 0): f <= 0},
            )
        else:
            wanted = (
                {(3, 2): True, (0, 1): f <= 0},
                {(2, 1): True, (1, 2): f <= 1},
                {(1, 0): True, (2, 3): f <= 2},
            )
        return [(a * 2 + core, b * 2 + core) for (a, b), yes in wanted[stage].items() if yes]

    def due(self, slot):
        lane, turn = slot % self.lanes, slot // self.lanes
        k = turn // 2 * self.lanes + lane
        return lane, turn % 2, k, k - self.lanes

    def step(self, slot):
        self.collect(slot - self.lanes)
        lane, core, k, last = self.due(slot)
        term = self.chunks[k][0] if k < len(self.chunks) else None
        held = self.sums.get(lane)
        if term is None or held is None:
            payload = held if term is None else term
        else:
            payload = jnp.where((self.col_index == core) & ~self.inner, term, held)
        perm = self.hops(k, core, 0) + self.hops(last, core, 2)
        perm += self.hops(k if core else last, 1 - core, 1)
        self.payloads[slot] = payload
        self.arrived[slot] = (payload, lax.ppermute(payload, ("sent", "col"), perm))

    def collect(self, slot):
        if slot not in self.arrived:
            return
        payload, brought = self.arrived.pop(slot)
        if slot + self.lanes - 1 in self.arrived:
            following = self.arrived[slot + self.lanes - 1][0]
            _, brought = lax.optimization_barrier((following, brought))
        lane, core, k, last = self.due(slot)
        held = self.sums.get(lane)
        base = held
        if k < len(self.chunks):
            term = self.chunks[k][0]
            base = term if held is None else jnp.where(self.col_index == core, term, held)
        self.sums[lane] = base + brought
        if last >= 0:
            old, first, _ = self.chunks[last]
            outer = brought
            if first[core] == 3:
                outer = jnp.where(self.sent_index == 3, brought + old, brought)
            final = jnp.where(self.inner, payload, outer)
            if core == 0:
                self.half[last] = final
            else:
                self.finals[last] = jnp.where(self.col_index == 0, self.half.pop(last), final)


def pieces(x):
    high = x.astype(jnp.bfloat16)
    rest = x - high.astype(jnp.float32)
    middle = rest.astype(jnp.bfloat16)
    return high, middle, (rest - middle.astype(jnp.float32)).astype(jnp.bfloat16)


def whiten_kernel(scale, gram_ref, merged_ref, out_ref, work):
    size = gram_ref.shape[0]
    tile = (8, 128)
    work[:, :size] = gram_ref[...]
    rows = lax.broadcasted_iota(jnp.int32, (size, size), 0)
    work[:, size:] = (rows == lax.broadcasted_iota(jnp.int32, (size, size), 1)).astype(jnp.float32)
    sublane = lax.broadcasted_iota(jnp.int32, tile, 0)
    for panel in range(0, size, PANEL):
        end = panel + PANEL
        start = panel // 128 * 128
        stop = size + start + 128
        for block in range(panel, end, 8):
            lanes = range(start, stop, 128)
            cols = [
                [
                    jnp.broadcast_to(
                        work[t : t + 8, start : start + 128][:, block - start + k][:, None], tile
                    )
                    for k in range(8)
                ]
                for t in range(block, end, 8)
            ]
            low = [
                [jnp.broadcast_to(cols[0][k][i : i + 1], tile) for k in range(i + 1)]
                for i in range(8)
            ]
            inverse = []
            for k in range(8):
                pivot = low[k][k]
                root = lax.rsqrt(pivot)
                root = root * (1.5 - 0.5 * pivot * root * root)
                inverse.append(root)
                for i in range(k + 1, 8):
                    low[i][k] = low[i][k] * root
                for i in range(k + 1, 8):
                    for m in range(k + 1, i + 1):
                        low[i][m] = low[i][m] - low[i][k] * low[m][k]
            for t in range(1, len(cols)):
                for k in range(8):
                    value = cols[t][k]
                    for m in range(k):
                        value = value - low[k][m] * cols[t][m]
                    cols[t][k] = value * inverse[k]
            for lane in lanes:
                here = slice(lane, lane + 128)
                old = work[block : block + 8, here]
                done, new = [], old
                for k in range(8):
                    value = jnp.broadcast_to(old[k : k + 1], tile)
                    for m in range(k):
                        value = value - low[k][m] * done[m]
                    done.append(value * inverse[k])
                    new = jnp.where(sublane == k, done[k], new)
                work[block : block + 8, here] = new
                for t in range(1, len(cols)):
                    at = slice(block + 8 * t, block + 8 * t + 8)
                    value = work[at, here]
                    for k in range(8):
                        value = value - cols[t][k] * done[k]
                    work[at, here] = value
        if end < size:
            first = end // 128 * 128
            upper = pieces(work[panel:end, first:size])
            right = pieces(work[panel:end, first:stop])
            a = jnp.concatenate([upper[i] for i in (0, 0, 1, 1, 0, 2)])
            b = jnp.concatenate([right[i] for i in (0, 1, 0, 1, 2, 0)])
            update = lax.dot_general(
                a, b, (((0,), (0,)), ((), ())), preferred_element_type=jnp.float32
            )
            work[end:, first:stop] -= update[end - first :]
    a = pieces(merged_ref[...])
    b = pieces(work[:, size:] * scale)
    total = 0.0
    for i, j in ((1, 1), (0, 2), (2, 0), (0, 1), (1, 0), (0, 0)):
        total += lax.dot_general(
            a[i], b[j], (((1,), (1,)), ((), ())), preferred_element_type=jnp.float32
        )
    out_ref[...] = total


def whiten(gram, merged, scale):
    size = gram.shape[0]
    return pl.pallas_call(
        functools.partial(whiten_kernel, scale),
        out_shape=jax.ShapeDtypeStruct(merged.shape, jnp.float32),
        in_specs=[pl.BlockSpec(memory_space=pltpu.VMEM)] * 2,
        out_specs=pl.BlockSpec(memory_space=pltpu.VMEM),
        scratch_shapes=[pltpu.VMEM((size, 2 * size), jnp.float32)],
        compiler_params=pltpu.CompilerParams(vmem_limit_bytes=32 * 2**20),
        name="whiten",
    )(gram, merged)


def shards(sketched, widths, inv_factor, shared):
    view_count, row_count, col_half = sketched.shape
    factor_rows = inv_factor.shape[1]
    sent_size = lax.axis_size("sent")
    view_size = lax.axis_size("view")
    core_count = lax.axis_size("col")
    total_rows = row_count * sent_size
    scale = 1.0 / math.sqrt(total_rows)
    high = lax.Precision.HIGH
    highest = lax.Precision.HIGHEST
    col_index = lax.axis_index("col")
    sent_index = lax.axis_index("sent")
    col_pos = col_index * col_half + jnp.arange(col_half)
    keep_cols = (col_pos[None, :] < widths[:, None]).astype(jnp.float32)[:, :, None]
    row_pos = sent_index * factor_rows + jnp.arange(factor_rows)
    keep_rows = (row_pos[None, :] < widths[:, None]).astype(jnp.float32)[:, :, None]
    use_line = sent_size == 4 and core_count == 2 and col_half % CHUNK == 0
    use_line = use_line and view_count * (col_half // CHUNK) % LANES == 0

    chunk = CHUNK if use_line else col_half
    per_view = col_half // chunk
    slots = [(j, q) for j in range(view_count) for q in range(per_view)]
    firsts = [
        [(c * col_half + q * chunk) // factor_rows for c in range(core_count)] for _, q in slots
    ]

    def keep_of(j, q):
        return keep_cols[j, q * chunk : (q + 1) * chunk]

    down = (((0,), (0,)), ((), ()))
    def first_half(proj, j):
        half_part = jnp.dot(inv_factor[j], jnp.concatenate(proj), precision=high)
        if use_line:
            perm = [
                (s * 2 + c, s * 2 + 1 - c)
                for s in range(sent_size)
                for c in range(2)
                if (s + 1) * factor_rows > col_half
            ]
            half = half_part + lax.ppermute(half_part, ("sent", "col"), perm)
        else:
            half = lax.psum(half_part, "col")
        return half * keep_rows[j]

    def cut(whole):
        return [whole[q * chunk : (q + 1) * chunk] for q in range(per_view)]

    def spread_terms(j, after=None):
        directions = shared
        if after is not None:
            directions, _ = lax.optimization_barrier((shared, after))
        return cut(
            scale
            * lax.dot_general(sketched[j], directions, down, preferred_element_type=jnp.float32)
        )

    def back_terms(proj, j):
        return cut(
            lax.dot_general(
                inv_factor[j], first_half(proj, j), down, precision=high,
                preferred_element_type=jnp.float32,
            )
        )

    if use_line:
        line = Line(LANES, 2 * len(slots), sent_index, col_index)
        for slot in range(line.slots + LANES):
            made = len(line.chunks)
            if slot < line.slots and line.due(slot)[2] == made and made < 2 * len(slots):
                done = made % len(slots)
                j = slots[done][0]
                if made < len(slots):
                    new = spread_terms(j, line.payloads.get(slot - 2 * LANES + 1))
                else:
                    new = [line.finals[done + q] * keep_of(j, q) for q in range(per_view)]
                    new = back_terms(new, j)
                for q, term in enumerate(new):
                    line.chunks.append((term, firsts[q], made < len(slots)))
            if slot < line.slots:
                line.step(slot)
            else:
                line.collect(slot - LANES)
        sums = [line.finals[len(slots) + k] for k in range(len(slots))]
    else:
        sums = []
        for j in range(view_count):
            proj = [lax.psum(spread_terms(j)[0], "sent") * keep_of(j, 0)]
            sums += [lax.psum(t, "sent") for t in back_terms(proj, j)]
    loads = [total * keep_of(*slot) for total, slot in zip(sums, slots)]
    loadings = jnp.concatenate(loads).reshape(view_count, col_half, -1)
    contrib = 0.0
    for j in range(view_count):
        whole = jnp.concatenate(loads[j * per_view : (j + 1) * per_view]).astype(jnp.bfloat16)
        contrib += jnp.dot(sketched[j], whole, preferred_element_type=jnp.float32)

    if view_size == 4 and core_count == 2:
        part_rows = row_count // 2
        near = lambda bit: [(v, v ^ bit) for v in range(view_size)]
        swap = [(0, 1), (1, 0)]
        mine = lax.dynamic_slice_in_dim(contrib, col_index * part_rows, part_rows)
        other = lax.dynamic_slice_in_dim(contrib, (1 - col_index) * part_rows, part_rows)
        mine = mine + lax.ppermute(other, "col", swap)
        upper, lower_part = mine[: part_rows // 2], mine[part_rows // 2 :]
        upper = upper + lax.ppermute(upper, "view", near(1))
        lower_part = lower_part + lax.ppermute(lower_part, "view", near(2))
        upper = upper + lax.ppermute(upper, "view", near(2))
        lower_part = lower_part + lax.ppermute(lower_part, "view", near(1))
        mine = jnp.concatenate([upper, lower_part])
        other = lax.ppermute(mine, "col", swap)
        merged = jnp.concatenate(
            [jnp.where(col_index == 0, mine, other), jnp.where(col_index == 0, other, mine)]
        )
        width = mine.shape[1] // 2
        gram = lax.dot_general(mine, mine, (((0,), (0,)), ((), ())), precision=highest)
        left, right = gram[:, :width], gram[:, width:]
        gram = jnp.where(col_index == 0, left, right)
        gram = gram + lax.ppermute(jnp.where(col_index == 0, right, left), "col", swap)
    else:
        merged = lax.psum(contrib, ("view", "col"))
        gram = lax.dot_general(merged, merged, (((0,), (0,)), ((), ())), precision=highest)
        width = gram.shape[1] // core_count
        gram = lax.dynamic_slice_in_dim(gram, col_index * width, width, axis=1)

    if sent_size & (sent_size - 1) == 0:
        bit = 1
        while bit < sent_size:
            gram = gram + lax.ppermute(gram, "sent", [(s, s ^ bit) for s in range(sent_size)])
            bit *= 2
    else:
        gram = lax.psum(gram, "sent")
    if core_count == 2:
        other = lax.ppermute(gram, "col", [(0, 1), (1, 0)])
        gram = jnp.concatenate(
            [jnp.where(col_index == 0, gram, other), jnp.where(col_index == 0, other, gram)],
            axis=1,
        )
    else:
        gram = lax.all_gather(gram, "col", axis=1, tiled=True)
    updated = whiten(gram, merged, math.sqrt(total_rows))
    return (loadings, updated)


def solution(mesh):
    return jax.shard_map(
        shards,
        mesh=mesh,
        in_specs=(P("view", "sent", "col"), P("view"), P("view", "sent", "col"), P("sent", None)),
        out_specs=(P("view", "col", None), P("sent", None)),
        check_vma=False,
    )
```

```python
import functools
import math

import jax
import jax.numpy as jnp
from jax import lax
from jax.experimental import pallas as pl
from jax.experimental.pallas import tpu as pltpu
from jax.sharding import PartitionSpec as P

CHUNK = 512
LANES = 2
PANEL = 32


class Line:
    def __init__(self, lanes, count, sent_index, col_index):
        self.lanes, self.sent_index, self.col_index = lanes, sent_index, col_index
        self.inner = (sent_index == 1) | (sent_index == 2)
        self.slots = lanes * (2 * (count // lanes) + 2)
        self.chunks, self.sums, self.arrived, self.half, self.finals = [], {}, {}, {}, {}
        self.payloads = {}

    def hops(self, k, core, stage):
        if not 0 <= k < len(self.chunks):
            return []
        _, first, spread = self.chunks[k]
        f = first[core]
        if spread:
            wanted = (
                {(0, 1): True, (3, 2): f < 3},
                {(1, 2): True, (2, 1): f <= 1},
                {(2, 3): True, (1, 0): f <= 0},
            )
        else:
            wanted = (
                {(3, 2): True, (0, 1): f <= 0},
                {(2, 1): True, (1, 2): f <= 1},
                {(1, 0): True, (2, 3): f <= 2},
            )
        return [(a * 2 + core, b * 2 + core) for (a, b), yes in wanted[stage].items() if yes]

    def due(self, slot):
        lane, turn = slot % self.lanes, slot // self.lanes
        k = turn // 2 * self.lanes + lane
        return lane, turn % 2, k, k - self.lanes

    def step(self, slot):
        self.collect(slot - self.lanes)
        lane, core, k, last = self.due(slot)
        term = self.chunks[k][0] if k < len(self.chunks) else None
        held = self.sums.get(lane)
        if term is None or held is None:
            payload = held if term is None else term
        else:
            payload = jnp.where((self.col_index == core) & ~self.inner, term, held)
        perm = self.hops(k, core, 0) + self.hops(last, core, 2)
        perm += self.hops(k if core else last, 1 - core, 1)
        self.payloads[slot] = payload
        self.arrived[slot] = (payload, lax.ppermute(payload, ("sent", "col"), perm))

    def collect(self, slot):
        if slot not in self.arrived:
            return
        payload, brought = self.arrived.pop(slot)
        if slot + self.lanes - 1 in self.arrived:
            following = self.arrived[slot + self.lanes - 1][0]
            _, brought = lax.optimization_barrier((following, brought))
        lane, core, k, last = self.due(slot)
        held = self.sums.get(lane)
        base = held
        if k < len(self.chunks):
            term = self.chunks[k][0]
            base = term if held is None else jnp.where(self.col_index == core, term, held)
        self.sums[lane] = base + brought
        if last >= 0:
            old, first, _ = self.chunks[last]
            outer = brought
            if first[core] == 3:
                outer = jnp.where(self.sent_index == 3, brought + old, brought)
            final = jnp.where(self.inner, payload, outer)
            if core == 0:
                self.half[last] = final
            else:
                self.finals[last] = jnp.where(self.col_index == 0, self.half.pop(last), final)


def pieces(x):
    high = x.astype(jnp.bfloat16)
    rest = x - high.astype(jnp.float32)
    middle = rest.astype(jnp.bfloat16)
    return high, middle, (rest - middle.astype(jnp.float32)).astype(jnp.bfloat16)


def whiten_kernel(scale, gram_ref, merged_ref, out_ref, work):
    size = gram_ref.shape[0]
    tile = (8, 128)
    work[:, :size] = gram_ref[...]
    rows = lax.broadcasted_iota(jnp.int32, (size, size), 0)
    work[:, size:] = (rows == lax.broadcasted_iota(jnp.int32, (size, size), 1)).astype(jnp.float32)
    sublane = lax.broadcasted_iota(jnp.int32, tile, 0)
    for panel in range(0, size, PANEL):
        end = panel + PANEL
        start = panel // 128 * 128
        stop = size + start + 128
        for block in range(panel, end, 8):
            lanes = range(start, stop, 128)
            cols = [
                [
                    jnp.broadcast_to(
                        work[t : t + 8, start : start + 128][:, block - start + k][:, None], tile
                    )
                    for k in range(8)
                ]
                for t in range(block, end, 8)
            ]
            low = [
                [jnp.broadcast_to(cols[0][k][i : i + 1], tile) for k in range(i + 1)]
                for i in range(8)
            ]
            inverse = []
            for k in range(8):
                pivot = low[k][k]
                root = lax.rsqrt(pivot)
                root = root * (1.5 - 0.5 * pivot * root * root)
                inverse.append(root)
                for i in range(k + 1, 8):
                    low[i][k] = low[i][k] * root
                for i in range(k + 1, 8):
                    for m in range(k + 1, i + 1):
                        low[i][m] = low[i][m] - low[i][k] * low[m][k]
            for t in range(1, len(cols)):
                for k in range(8):
                    value = cols[t][k]
                    for m in range(k):
                        value = value - low[k][m] * cols[t][m]
                    cols[t][k] = value * inverse[k]
            for lane in lanes:
                here = slice(lane, lane + 128)
                old = work[block : block + 8, here]
                done, new = [], old
                for k in range(8):
                    value = jnp.broadcast_to(old[k : k + 1], tile)
                    for m in range(k):
                        value = value - low[k][m] * done[m]
                    done.append(value * inverse[k])
                    new = jnp.where(sublane == k, done[k], new)
                work[block : block + 8, here] = new
                for t in range(1, len(cols)):
                    at = slice(block + 8 * t, block + 8 * t + 8)
                    value = work[at, here]
                    for k in range(8):
                        value = value - cols[t][k] * done[k]
                    work[at, here] = value
        if end < size:
            first = end // 128 * 128
            upper = pieces(work[panel:end, first:size])
            right = pieces(work[panel:end, first:stop])
            a = jnp.concatenate([upper[i] for i in (0, 0, 1, 1, 0, 2)])
            b = jnp.concatenate([right[i] for i in (0, 1, 0, 1, 2, 0)])
            update = lax.dot_general(
                a, b, (((0,), (0,)), ((), ())), preferred_element_type=jnp.float32
            )
            work[end:, first:stop] -= update[end - first :]
    a = pieces(merged_ref[...])
    b = pieces(work[:, size:] * scale)
    total = 0.0
    for i, j in ((1, 1), (0, 2), (2, 0), (0, 1), (1, 0), (0, 0)):
        total += lax.dot_general(
            a[i], b[j], (((1,), (1,)), ((), ())), preferred_element_type=jnp.float32
        )
    out_ref[...] = total


def whiten(gram, merged, scale):
    size = gram.shape[0]
    return pl.pallas_call(
        functools.partial(whiten_kernel, scale),
        out_shape=jax.ShapeDtypeStruct(merged.shape, jnp.float32),
        in_specs=[pl.BlockSpec(memory_space=pltpu.VMEM)] * 2,
        out_specs=pl.BlockSpec(memory_space=pltpu.VMEM),
        scratch_shapes=[pltpu.VMEM((size, 2 * size), jnp.float32)],
        compiler_params=pltpu.CompilerParams(vmem_limit_bytes=32 * 2**20),
        name="whiten",
    )(gram, merged)


def shards(sketched, widths, inv_factor, shared):
    view_count, row_count, col_half = sketched.shape
    factor_rows = inv_factor.shape[1]
    sent_size = lax.axis_size("sent")
    view_size = lax.axis_size("view")
    core_count = lax.axis_size("col")
    total_rows = row_count * sent_size
    scale = 1.0 / math.sqrt(total_rows)
    high = lax.Precision.HIGH
    highest = lax.Precision.HIGHEST
    col_index = lax.axis_index("col")
    sent_index = lax.axis_index("sent")
    col_pos = col_index * col_half + jnp.arange(col_half)
    keep_cols = (col_pos[None, :] < widths[:, None]).astype(jnp.float32)[:, :, None]
    row_pos = sent_index * factor_rows + jnp.arange(factor_rows)
    keep_rows = (row_pos[None, :] < widths[:, None]).astype(jnp.float32)[:, :, None]
    use_line = sent_size == 4 and core_count == 2 and col_half % CHUNK == 0
    use_line = use_line and view_count * (col_half // CHUNK) % LANES == 0

    chunk = CHUNK if use_line else col_half
    per_view = col_half // chunk
    slots = [(j, q) for j in range(view_count) for q in range(per_view)]
    firsts = [
        [(c * col_half + q * chunk) // factor_rows for c in range(core_count)] for _, q in slots
    ]

    def keep_of(j, q):
        return keep_cols[j, q * chunk : (q + 1) * chunk]

    down = (((0,), (0,)), ((), ()))
    def first_half(proj, j):
        half_part = jnp.dot(inv_factor[j], jnp.concatenate(proj), precision=high)
        if use_line:
            perm = [
                (s * 2 + c, s * 2 + 1 - c)
                for s in range(sent_size)
                for c in range(2)
                if (s + 1) * factor_rows > col_half
            ]
            half = half_part + lax.ppermute(half_part, ("sent", "col"), perm)
        else:
            half = lax.psum(half_part, "col")
        return half * keep_rows[j]

    def cut(whole):
        return [whole[q * chunk : (q + 1) * chunk] for q in range(per_view)]

    def spread_terms(j, after=None):
        directions = shared
        if after is not None:
            directions, _ = lax.optimization_barrier((shared, after))
        return cut(
            scale
            * lax.dot_general(sketched[j], directions, down, preferred_element_type=jnp.float32)
        )

    def back_terms(proj, j):
        return cut(
            lax.dot_general(
                inv_factor[j], first_half(proj, j), down, precision=high,
                preferred_element_type=jnp.float32,
            )
        )

    if use_line:
        line = Line(LANES, 2 * len(slots), sent_index, col_index)
        for slot in range(line.slots + LANES):
            made = len(line.chunks)
            if slot < line.slots and line.due(slot)[2] == made and made < 2 * len(slots):
                done = made % len(slots)
                j = slots[done][0]
                if made < len(slots):
                    new = spread_terms(j, line.payloads.get(slot - 2 * LANES + 1))
                else:
                    new = [line.finals[done + q] * keep_of(j, q) for q in range(per_view)]
                    new = back_terms(new, j)
                for q, term in enumerate(new):
                    line.chunks.append((term, firsts[q], made < len(slots)))
            if slot < line.slots:
                line.step(slot)
            else:
                line.collect(slot - LANES)
        sums = [line.finals[len(slots) + k] for k in range(len(slots))]
    else:
        sums = []
        for j in range(view_count):
            proj = [lax.psum(spread_terms(j)[0], "sent") * keep_of(j, 0)]
            sums += [lax.psum(t, "sent") for t in back_terms(proj, j)]
    loads = [total * keep_of(*slot) for total, slot in zip(sums, slots)]
    loadings = jnp.concatenate(loads).reshape(view_count, col_half, -1)
    contrib = 0.0
    for j in range(view_count):
        whole = jnp.concatenate(loads[j * per_view : (j + 1) * per_view]).astype(jnp.bfloat16)
        contrib += jnp.dot(sketched[j], whole, preferred_element_type=jnp.float32)

    if view_size == 4 and core_count == 2:
        part_rows = row_count // 2
        near = lambda bit: [(v, v ^ bit) for v in range(view_size)]
        swap = [(0, 1), (1, 0)]
        mine = lax.dynamic_slice_in_dim(contrib, col_index * part_rows, part_rows)
        other = lax.dynamic_slice_in_dim(contrib, (1 - col_index) * part_rows, part_rows)
        mine = mine + lax.ppermute(other, "col", swap)
        upper, lower_part = mine[: part_rows // 2], mine[part_rows // 2 :]
        upper = upper + lax.ppermute(upper, "view", near(1))
        lower_part = lower_part + lax.ppermute(lower_part, "view", near(2))
        upper = upper + lax.ppermute(upper, "view", near(2))
        lower_part = lower_part + lax.ppermute(lower_part, "view", near(1))
        mine = jnp.concatenate([upper, lower_part])
        other = lax.ppermute(mine, "col", swap)
        merged = jnp.concatenate(
            [jnp.where(col_index == 0, mine, other), jnp.where(col_index == 0, other, mine)]
        )
        width = mine.shape[1] // 2
        gram = lax.dot_general(mine, mine, (((0,), (0,)), ((), ())), precision=highest)
        left, right = gram[:, :width], gram[:, width:]
        gram = jnp.where(col_index == 0, left, right)
        gram = gram + lax.ppermute(jnp.where(col_index == 0, right, left), "col", swap)
    else:
        merged = lax.psum(contrib, ("view", "col"))
        gram = lax.dot_general(merged, merged, (((0,), (0,)), ((), ())), precision=highest)
        width = gram.shape[1] // core_count
        gram = lax.dynamic_slice_in_dim(gram, col_index * width, width, axis=1)

    if sent_size & (sent_size - 1) == 0:
        bit = 1
        while bit < sent_size:
            gram = gram + lax.ppermute(gram, "sent", [(s, s ^ bit) for s in range(sent_size)])
            bit *= 2
    else:
        gram = lax.psum(gram, "sent")
    if core_count == 2:
        other = lax.ppermute(gram, "col", [(0, 1), (1, 0)])
        gram = jnp.concatenate(
            [jnp.where(col_index == 0, gram, other), jnp.where(col_index == 0, other, gram)],
            axis=1,
        )
    else:
        gram = lax.all_gather(gram, "col", axis=1, tiled=True)
    updated = whiten(gram, merged, math.sqrt(total_rows))
    return (loadings, updated)


def solution(mesh):
    return jax.shard_map(
        shards,
        mesh=mesh,
        in_specs=(P("view", "sent", "col"), P("view"), P("view", "sent", "col"), P("sent", None)),
        out_specs=(P("view", "col", None), P("sent", None)),
        check_vma=False,
    )
```

```python
import functools
import math

import jax
import jax.numpy as jnp
from jax import lax
from jax.experimental import pallas as pl
from jax.experimental.pallas import tpu as pltpu
from jax.sharding import PartitionSpec as P

CHUNK = 512
LANES = 2
PANEL = 32


class Line:
    def __init__(self, lanes, count, sent_index, col_index):
        self.lanes, self.sent_index, self.col_index = lanes, sent_index, col_index
        self.inner = (sent_index == 1) | (sent_index == 2)
        self.slots = lanes * (2 * (count // lanes) + 2)
        self.chunks, self.sums, self.arrived, self.half, self.finals = [], {}, {}, {}, {}
        self.payloads = {}

    def hops(self, k, core, stage):
        if not 0 <= k < len(self.chunks):
            return []
        _, first, spread = self.chunks[k]
        f = first[core]
        if spread:
            wanted = (
                {(0, 1): True, (3, 2): f < 3},
                {(1, 2): True, (2, 1): f <= 1},
                {(2, 3): True, (1, 0): f <= 0},
            )
        else:
            wanted = (
                {(3, 2): True, (0, 1): f <= 0},
                {(2, 1): True, (1, 2): f <= 1},
                {(1, 0): True, (2, 3): f <= 2},
            )
        return [(a * 2 + core, b * 2 + core) for (a, b), yes in wanted[stage].items() if yes]

    def due(self, slot):
        lane, turn = slot % self.lanes, slot // self.lanes
        k = turn // 2 * self.lanes + lane
        return lane, turn % 2, (turn + lane) % 2, k, k - self.lanes

    def step(self, slot):
        self.collect(slot - self.lanes)
        lane, late, core, k, last = self.due(slot)
        term = self.chunks[k][0] if k < len(self.chunks) else None
        held = self.sums.get(lane)
        if term is None or held is None:
            payload = held if term is None else term
        else:
            payload = jnp.where((self.col_index == core) & ~self.inner, term, held)
        perm = self.hops(k, core, 0) + self.hops(last, core, 2)
        perm += self.hops(k if late else last, 1 - core, 1)
        self.payloads[slot] = payload
        self.arrived[slot] = (payload, lax.ppermute(payload, ("sent", "col"), perm))

    def collect(self, slot):
        if slot not in self.arrived:
            return
        payload, brought = self.arrived.pop(slot)
        if slot + self.lanes - 1 in self.arrived:
            following = self.arrived[slot + self.lanes - 1][0]
            _, brought = lax.optimization_barrier((following, brought))
        lane, late, core, k, last = self.due(slot)
        held = self.sums.get(lane)
        base = held
        if k < len(self.chunks):
            term = self.chunks[k][0]
            base = term if held is None else jnp.where(self.col_index == core, term, held)
        self.sums[lane] = base + brought
        if last >= 0:
            old, first, _ = self.chunks[last]
            outer = brought
            if first[core] == 3:
                outer = jnp.where(self.sent_index == 3, brought + old, brought)
            final = jnp.where(self.inner, payload, outer)
            if not late:
                self.half[last] = final
            else:
                self.finals[last] = jnp.where(self.col_index == core, final, self.half.pop(last))


def pieces(x):
    high = x.astype(jnp.bfloat16)
    rest = x - high.astype(jnp.float32)
    middle = rest.astype(jnp.bfloat16)
    return high, middle, (rest - middle.astype(jnp.float32)).astype(jnp.bfloat16)


def whiten_kernel(scale, gram_ref, merged_ref, out_ref, work):
    size = gram_ref.shape[0]
    tile = (8, 128)
    work[:, :size] = gram_ref[...]
    rows = lax.broadcasted_iota(jnp.int32, (size, size), 0)
    work[:, size:] = (rows == lax.broadcasted_iota(jnp.int32, (size, size), 1)).astype(jnp.float32)
    sublane = lax.broadcasted_iota(jnp.int32, tile, 0)
    for panel in range(0, size, PANEL):
        end = panel + PANEL
        start = panel // 128 * 128
        stop = size + start + 128
        for block in range(panel, end, 8):
            lanes = range(start, stop, 128)
            cols = [
                [
                    jnp.broadcast_to(
                        work[t : t + 8, start : start + 128][:, block - start + k][:, None], tile
                    )
                    for k in range(8)
                ]
                for t in range(block, end, 8)
            ]
            low = [
                [jnp.broadcast_to(cols[0][k][i : i + 1], tile) for k in range(i + 1)]
                for i in range(8)
            ]
            inverse = []
            for k in range(8):
                pivot = low[k][k]
                root = lax.rsqrt(pivot)
                root = root * (1.5 - 0.5 * pivot * root * root)
                inverse.append(root)
                for i in range(k + 1, 8):
                    low[i][k] = low[i][k] * root
                for i in range(k + 1, 8):
                    for m in range(k + 1, i + 1):
                        low[i][m] = low[i][m] - low[i][k] * low[m][k]
            for t in range(1, len(cols)):
                for k in range(8):
                    value = cols[t][k]
                    for m in range(k):
                        value = value - low[k][m] * cols[t][m]
                    cols[t][k] = value * inverse[k]
            for lane in lanes:
                here = slice(lane, lane + 128)
                old = work[block : block + 8, here]
                done, new = [], old
                for k in range(8):
                    value = jnp.broadcast_to(old[k : k + 1], tile)
                    for m in range(k):
                        value = value - low[k][m] * done[m]
                    done.append(value * inverse[k])
                    new = jnp.where(sublane == k, done[k], new)
                work[block : block + 8, here] = new
                for t in range(1, len(cols)):
                    at = slice(block + 8 * t, block + 8 * t + 8)
                    value = work[at, here]
                    for k in range(8):
                        value = value - cols[t][k] * done[k]
                    work[at, here] = value
        if end < size:
            first = end // 128 * 128
            upper = pieces(work[panel:end, first:size])
            right = pieces(work[panel:end, first:stop])
            a = jnp.concatenate([upper[i] for i in (0, 0, 1, 1, 0, 2)])
            b = jnp.concatenate([right[i] for i in (0, 1, 0, 1, 2, 0)])
            update = lax.dot_general(
                a, b, (((0,), (0,)), ((), ())), preferred_element_type=jnp.float32
            )
            work[end:, first:stop] -= update[end - first :]
    a = pieces(merged_ref[...])
    b = pieces(work[:, size:] * scale)
    total = 0.0
    for i, j in ((1, 1), (0, 2), (2, 0), (0, 1), (1, 0), (0, 0)):
        total += lax.dot_general(
            a[i], b[j], (((1,), (1,)), ((), ())), preferred_element_type=jnp.float32
        )
    out_ref[...] = total


def whiten(gram, merged, scale):
    size = gram.shape[0]
    return pl.pallas_call(
        functools.partial(whiten_kernel, scale),
        out_shape=jax.ShapeDtypeStruct(merged.shape, jnp.float32),
        in_specs=[pl.BlockSpec(memory_space=pltpu.VMEM)] * 2,
        out_specs=pl.BlockSpec(memory_space=pltpu.VMEM),
        scratch_shapes=[pltpu.VMEM((size, 2 * size), jnp.float32)],
        compiler_params=pltpu.CompilerParams(vmem_limit_bytes=32 * 2**20),
        name="whiten",
    )(gram, merged)


def shards(sketched, widths, inv_factor, shared):
    view_count, row_count, col_half = sketched.shape
    factor_rows = inv_factor.shape[1]
    sent_size = lax.axis_size("sent")
    view_size = lax.axis_size("view")
    core_count = lax.axis_size("col")
    total_rows = row_count * sent_size
    scale = 1.0 / math.sqrt(total_rows)
    high = lax.Precision.HIGH
    highest = lax.Precision.HIGHEST
    col_index = lax.axis_index("col")
    sent_index = lax.axis_index("sent")
    col_pos = col_index * col_half + jnp.arange(col_half)
    keep_cols = (col_pos[None, :] < widths[:, None]).astype(jnp.float32)[:, :, None]
    row_pos = sent_index * factor_rows + jnp.arange(factor_rows)
    keep_rows = (row_pos[None, :] < widths[:, None]).astype(jnp.float32)[:, :, None]
    use_line = sent_size == 4 and core_count == 2 and col_half % CHUNK == 0
    use_line = use_line and view_count * (col_half // CHUNK) % LANES == 0

    chunk = CHUNK if use_line else col_half
    per_view = col_half // chunk
    slots = [(j, q) for j in range(view_count) for q in range(per_view)]
    firsts = [
        [(c * col_half + q * chunk) // factor_rows for c in range(core_count)] for _, q in slots
    ]

    def keep_of(j, q):
        return keep_cols[j, q * chunk : (q + 1) * chunk]

    down = (((0,), (0,)), ((), ()))
    def first_half(proj, j):
        half_part = jnp.dot(inv_factor[j], jnp.concatenate(proj), precision=high)
        if use_line:
            perm = [
                (s * 2 + c, s * 2 + 1 - c)
                for s in range(sent_size)
                for c in range(2)
                if (s + 1) * factor_rows > col_half
            ]
            half = half_part + lax.ppermute(half_part, ("sent", "col"), perm)
        else:
            half = lax.psum(half_part, "col")
        return half * keep_rows[j]

    def cut(whole):
        return [whole[q * chunk : (q + 1) * chunk] for q in range(per_view)]

    def spread_terms(j, after=None):
        directions = shared
        if after is not None:
            directions, _ = lax.optimization_barrier((shared, after))
        return cut(
            scale
            * lax.dot_general(sketched[j], directions, down, preferred_element_type=jnp.float32)
        )

    def back_terms(proj, j):
        return cut(
            lax.dot_general(
                inv_factor[j], first_half(proj, j), down, precision=high,
                preferred_element_type=jnp.float32,
            )
        )

    if use_line:
        line = Line(LANES, 2 * len(slots), sent_index, col_index)
        for slot in range(line.slots + LANES):
            made = len(line.chunks)
            if slot < line.slots and line.due(slot)[3] == made and made < 2 * len(slots):
                done = made % len(slots)
                j = slots[done][0]
                if made < len(slots):
                    new = spread_terms(j, line.payloads.get(slot - 2 * LANES + 1))
                else:
                    new = [line.finals[done + q] * keep_of(j, q) for q in range(per_view)]
                    new = back_terms(new, j)
                for q, term in enumerate(new):
                    line.chunks.append((term, firsts[q], made < len(slots)))
            if slot < line.slots:
                line.step(slot)
            else:
                line.collect(slot - LANES)
        sums = [line.finals[len(slots) + k] for k in range(len(slots))]
    else:
        sums = []
        for j in range(view_count):
            proj = [lax.psum(spread_terms(j)[0], "sent") * keep_of(j, 0)]
            sums += [lax.psum(t, "sent") for t in back_terms(proj, j)]
    loads = [total * keep_of(*slot) for total, slot in zip(sums, slots)]
    loadings = jnp.concatenate(loads).reshape(view_count, col_half, -1)
    contrib = 0.0
    for j in range(view_count):
        whole = jnp.concatenate(loads[j * per_view : (j + 1) * per_view]).astype(jnp.bfloat16)
        contrib += jnp.dot(sketched[j], whole, preferred_element_type=jnp.float32)

    if view_size == 4 and core_count == 2:
        part_rows = row_count // 2
        near = lambda bit: [(v, v ^ bit) for v in range(view_size)]
        swap = [(0, 1), (1, 0)]
        mine = lax.dynamic_slice_in_dim(contrib, col_index * part_rows, part_rows)
        other = lax.dynamic_slice_in_dim(contrib, (1 - col_index) * part_rows, part_rows)
        mine = mine + lax.ppermute(other, "col", swap)
        upper, lower_part = mine[: part_rows // 2], mine[part_rows // 2 :]
        upper = upper + lax.ppermute(upper, "view", near(1))
        lower_part = lower_part + lax.ppermute(lower_part, "view", near(2))
        upper = upper + lax.ppermute(upper, "view", near(2))
        lower_part = lower_part + lax.ppermute(lower_part, "view", near(1))
        mine = jnp.concatenate([upper, lower_part])
        other = lax.ppermute(mine, "col", swap)
        merged = jnp.concatenate(
            [jnp.where(col_index == 0, mine, other), jnp.where(col_index == 0, other, mine)]
        )
        width = mine.shape[1] // 2
        gram = lax.dot_general(mine, mine, (((0,), (0,)), ((), ())), precision=highest)
        left, right = gram[:, :width], gram[:, width:]
        gram = jnp.where(col_index == 0, left, right)
        gram = gram + lax.ppermute(jnp.where(col_index == 0, right, left), "col", swap)
    else:
        merged = lax.psum(contrib, ("view", "col"))
        gram = lax.dot_general(merged, merged, (((0,), (0,)), ((), ())), precision=highest)
        width = gram.shape[1] // core_count
        gram = lax.dynamic_slice_in_dim(gram, col_index * width, width, axis=1)

    if sent_size & (sent_size - 1) == 0:
        bit = 1
        while bit < sent_size:
            gram = gram + lax.ppermute(gram, "sent", [(s, s ^ bit) for s in range(sent_size)])
            bit *= 2
    else:
        gram = lax.psum(gram, "sent")
    if core_count == 2:
        other = lax.ppermute(gram, "col", [(0, 1), (1, 0)])
        gram = jnp.concatenate(
            [jnp.where(col_index == 0, gram, other), jnp.where(col_index == 0, other, gram)],
            axis=1,
        )
    else:
        gram = lax.all_gather(gram, "col", axis=1, tiled=True)
    updated = whiten(gram, merged, math.sqrt(total_rows))
    return (loadings, updated)


def solution(mesh):
    return jax.shard_map(
        shards,
        mesh=mesh,
        in_specs=(P("view", "sent", "col"), P("view"), P("view", "sent", "col"), P("sent", None)),
        out_specs=(P("view", "col", None), P("sent", None)),
        check_vma=False,
    )
```

```python
import functools
import math

import jax
import jax.numpy as jnp
from jax import lax
from jax.experimental import pallas as pl
from jax.experimental.pallas import tpu as pltpu
from jax.sharding import PartitionSpec as P

CHUNK = 256
LANES = 2
PANEL = 32


class Line:
    def __init__(self, lanes, sent_index, col_index):
        self.lanes, self.sent_index, self.col_index = lanes, sent_index, col_index
        self.inner = (sent_index == 1) | (sent_index == 2)
        self.slot, self.chunks, self.pairs, self.totals, self.finals = 0, {}, {}, {}, {}
        self.arrived = {}

    def pairs_of(self, k, stage):
        if k not in self.chunks:
            return []
        _, first, spread = self.chunks[k]
        always = lambda f: True
        if spread:
            hops = (
                {(0, 1): always, (3, 2): lambda f: f < 3},
                {(1, 2): always, (2, 1): lambda f: f <= 1},
                {(2, 3): always, (1, 0): lambda f: f <= 0},
            )
        else:
            hops = (
                {(3, 2): always, (0, 1): lambda f: f <= 0},
                {(2, 1): always, (1, 2): lambda f: f <= 1},
                {(1, 0): always, (2, 3): lambda f: f <= 2},
            )
        cores = len(first)
        return [
            (a * cores + c, b * cores + c)
            for c in range(cores)
            for (a, b), wanted in hops[stage].items()
            if wanted(first[c])
        ]

    def step(self, term=None, first=None, spread=None):
        k = self.slot
        self.slot += 1
        self.collect(k - self.lanes)
        middle, last = k - self.lanes, k - 2 * self.lanes
        if term is not None:
            self.chunks[k] = (term, first, spread)
        ends, pair = term, self.pairs.get(middle)
        if last in self.totals:
            total = self.totals[last]
            ends = total if term is None else jnp.where(self.inner, total, term)
        if ends is not None and pair is not None:
            ends, pair = lax.optimization_barrier((ends, pair))
        axes, ends_in, pair_in = ("sent", "col"), None, None
        if ends is not None:
            perm = self.pairs_of(k, 0) + self.pairs_of(last, 2)
            ends_in = lax.ppermute(ends, axes, perm)
        if pair is not None:
            pair_in = lax.ppermute(pair, axes, self.pairs_of(middle, 1))
        self.arrived[k] = (ends, ends_in, pair_in)

    def collect(self, k):
        if k not in self.arrived:
            return
        ends, ends_in, pair_in = self.arrived.pop(k)
        middle, last = k - self.lanes, k - 2 * self.lanes
        following = self.arrived.get(k + 1, (None,))[0] if self.lanes > 1 else None
        tied = [v for v in (following, ends_in, pair_in) if v is not None]
        tied = list(lax.optimization_barrier(tuple(tied)))
        if following is not None:
            del tied[0]
        if ends_in is not None:
            ends_in = tied.pop(0)
        if pair_in is not None:
            self.totals[middle] = self.pairs[middle] + tied.pop(0)
        if k in self.chunks:
            self.pairs[k] = self.chunks[k][0] + ends_in
        if last in self.totals:
            old, first, _ = self.chunks[last]
            alone = (self.sent_index == 3) & (self.col_index >= [f == 3 for f in first].index(True)) \
                if 3 in first else None
            outer = ends_in if alone is None else jnp.where(alone, ends_in + old, ends_in)
            self.finals[last] = jnp.where(self.inner, ends, outer)


def pieces(x):
    high = x.astype(jnp.bfloat16)
    rest = x - high.astype(jnp.float32)
    middle = rest.astype(jnp.bfloat16)
    return high, middle, (rest - middle.astype(jnp.float32)).astype(jnp.bfloat16)


def whiten_kernel(scale, gram_ref, merged_ref, out_ref, work):
    size = gram_ref.shape[0]
    tile = (8, 128)
    work[:, :size] = gram_ref[...]
    rows = lax.broadcasted_iota(jnp.int32, (size, size), 0)
    work[:, size:] = (rows == lax.broadcasted_iota(jnp.int32, (size, size), 1)).astype(jnp.float32)
    sublane = lax.broadcasted_iota(jnp.int32, tile, 0)
    for panel in range(0, size, PANEL):
        end = panel + PANEL
        start = panel // 128 * 128
        stop = size + start + 128
        for block in range(panel, end, 8):
            lanes = range(start, stop, 128)
            cols = [
                [
                    jnp.broadcast_to(
                        work[t : t + 8, start : start + 128][:, block - start + k][:, None], tile
                    )
                    for k in range(8)
                ]
                for t in range(block, end, 8)
            ]
            low = [
                [jnp.broadcast_to(cols[0][k][i : i + 1], tile) for k in range(i + 1)]
                for i in range(8)
            ]
            inverse = []
            for k in range(8):
                pivot = low[k][k]
                root = lax.rsqrt(pivot)
                root = root * (1.5 - 0.5 * pivot * root * root)
                inverse.append(root)
                for i in range(k + 1, 8):
                    low[i][k] = low[i][k] * root
                for i in range(k + 1, 8):
                    for m in range(k + 1, i + 1):
                        low[i][m] = low[i][m] - low[i][k] * low[m][k]
            for t in range(1, len(cols)):
                for k in range(8):
                    value = cols[t][k]
                    for m in range(k):
                        value = value - low[k][m] * cols[t][m]
                    cols[t][k] = value * inverse[k]
            for lane in lanes:
                here = slice(lane, lane + 128)
                old = work[block : block + 8, here]
                done, new = [], old
                for k in range(8):
                    value = jnp.broadcast_to(old[k : k + 1], tile)
                    for m in range(k):
                        value = value - low[k][m] * done[m]
                    done.append(value * inverse[k])
                    new = jnp.where(sublane == k, done[k], new)
                work[block : block + 8, here] = new
                for t in range(1, len(cols)):
                    at = slice(block + 8 * t, block + 8 * t + 8)
                    value = work[at, here]
                    for k in range(8):
                        value = value - cols[t][k] * done[k]
                    work[at, here] = value
        if end < size:
            first = end // 128 * 128
            upper = pieces(work[panel:end, first:size])
            right = pieces(work[panel:end, first:stop])
            a = jnp.concatenate([upper[i] for i in (0, 0, 1, 1, 0, 2)])
            b = jnp.concatenate([right[i] for i in (0, 1, 0, 1, 2, 0)])
            update = lax.dot_general(
                a, b, (((0,), (0,)), ((), ())), preferred_element_type=jnp.float32
            )
            work[end:, first:stop] -= update[end - first :]
    a = pieces(merged_ref[...])
    b = pieces(work[:, size:] * scale)
    total = 0.0
    for i, j in ((1, 1), (0, 2), (2, 0), (0, 1), (1, 0), (0, 0)):
        total += lax.dot_general(
            a[i], b[j], (((1,), (1,)), ((), ())), preferred_element_type=jnp.float32
        )
    out_ref[...] = total


def whiten(gram, merged, scale):
    size = gram.shape[0]
    return pl.pallas_call(
        functools.partial(whiten_kernel, scale),
        out_shape=jax.ShapeDtypeStruct(merged.shape, jnp.float32),
        in_specs=[pl.BlockSpec(memory_space=pltpu.VMEM)] * 2,
        out_specs=pl.BlockSpec(memory_space=pltpu.VMEM),
        scratch_shapes=[pltpu.VMEM((size, 2 * size), jnp.float32)],
        compiler_params=pltpu.CompilerParams(vmem_limit_bytes=32 * 2**20),
        name="whiten",
    )(gram, merged)


def shards(sketched, widths, inv_factor, shared):
    view_count, row_count, col_half = sketched.shape
    factor_rows = inv_factor.shape[1]
    sent_size = lax.axis_size("sent")
    view_size = lax.axis_size("view")
    core_count = lax.axis_size("col")
    total_rows = row_count * sent_size
    scale = 1.0 / math.sqrt(total_rows)
    high = lax.Precision.HIGH
    highest = lax.Precision.HIGHEST
    col_index = lax.axis_index("col")
    sent_index = lax.axis_index("sent")
    col_pos = col_index * col_half + jnp.arange(col_half)
    keep_cols = (col_pos[None, :] < widths[:, None]).astype(jnp.float32)[:, :, None]
    row_pos = sent_index * factor_rows + jnp.arange(factor_rows)
    keep_rows = (row_pos[None, :] < widths[:, None]).astype(jnp.float32)[:, :, None]
    use_line = sent_size == 4 and core_count == 2 and col_half % CHUNK == 0

    chunk = CHUNK if use_line else col_half
    per_view = col_half // chunk
    slots = [(j, q) for j in range(view_count) for q in range(per_view)]
    firsts = [
        [(c * col_half + q * chunk) // factor_rows for c in range(core_count)] for _, q in slots
    ]

    def keep_of(j, q):
        return keep_cols[j, q * chunk : (q + 1) * chunk]

    down = (((0,), (0,)), ((), ()))
    def first_half(proj, j):
        half_part = jnp.dot(inv_factor[j], jnp.concatenate(proj), precision=high)
        if use_line:
            perm = [
                (s * 2 + c, s * 2 + 1 - c)
                for s in range(sent_size)
                for c in range(2)
                if (s + 1) * factor_rows > col_half
            ]
            half = half_part + lax.ppermute(half_part, ("sent", "col"), perm)
        else:
            half = lax.psum(half_part, "col")
        return half * keep_rows[j]

    def cut(whole):
        return [whole[q * chunk : (q + 1) * chunk] for q in range(per_view)]

    def term_of(features):
        return scale * lax.dot_general(features, shared, down, preferred_element_type=jnp.float32)

    terms = []
    for j in range(view_count):
        terms += cut(term_of(sketched[j]))

    def back_terms(proj, j):
        return cut(
            lax.dot_general(
                inv_factor[j], first_half(proj, j), down, precision=high,
                preferred_element_type=jnp.float32,
            )
        )

    if use_line:
        line = Line(LANES, sent_index, col_index)
        for term, first in zip(terms, firsts):
            line.step(term, first, True)
        done = 0
        while done < len(slots):
            while done + per_view - 1 not in line.finals:
                line.step()
            proj = [line.finals[done + q] * keep_of(*slots[done + q]) for q in range(per_view)]
            for q, term in enumerate(back_terms(proj, slots[done][0])):
                line.step(term, firsts[q], False)
            done += per_view
        begin = line.slot - len(slots)
        for _ in range(3 * LANES):
            line.step()
        sums = [line.finals[begin + k] for k in range(len(slots))]
    else:
        sums = []
        for j in range(view_count):
            proj = [lax.psum(terms[j], "sent") * keep_of(j, 0)]
            sums += [lax.psum(t, "sent") for t in back_terms(proj, j)]
    loads = [total * keep_of(*slot) for total, slot in zip(sums, slots)]
    loadings = jnp.concatenate(loads).reshape(view_count, col_half, -1)
    contrib = 0.0
    for j in range(view_count):
        whole = jnp.concatenate(loads[j * per_view : (j + 1) * per_view]).astype(jnp.bfloat16)
        contrib += jnp.dot(sketched[j], whole, preferred_element_type=jnp.float32)

    if view_size == 4 and core_count == 2:
        part_rows = row_count // 2
        near = lambda bit: [(v, v ^ bit) for v in range(view_size)]
        swap = [(0, 1), (1, 0)]
        mine = lax.dynamic_slice_in_dim(contrib, col_index * part_rows, part_rows)
        other = lax.dynamic_slice_in_dim(contrib, (1 - col_index) * part_rows, part_rows)
        mine = mine + lax.ppermute(other, "col", swap)
        upper, lower_part = mine[: part_rows // 2], mine[part_rows // 2 :]
        upper = upper + lax.ppermute(upper, "view", near(1))
        lower_part = lower_part + lax.ppermute(lower_part, "view", near(2))
        upper = upper + lax.ppermute(upper, "view", near(2))
        lower_part = lower_part + lax.ppermute(lower_part, "view", near(1))
        mine = jnp.concatenate([upper, lower_part])
        other = lax.ppermute(mine, "col", swap)
        merged = jnp.concatenate(
            [jnp.where(col_index == 0, mine, other), jnp.where(col_index == 0, other, mine)]
        )
        width = mine.shape[1] // 2
        gram = lax.dot_general(mine, mine, (((0,), (0,)), ((), ())), precision=highest)
        left, right = gram[:, :width], gram[:, width:]
        gram = jnp.where(col_index == 0, left, right)
        gram = gram + lax.ppermute(jnp.where(col_index == 0, right, left), "col", swap)
    else:
        merged = lax.psum(contrib, ("view", "col"))
        gram = lax.dot_general(merged, merged, (((0,), (0,)), ((), ())), precision=highest)
        width = gram.shape[1] // core_count
        gram = lax.dynamic_slice_in_dim(gram, col_index * width, width, axis=1)

    if sent_size & (sent_size - 1) == 0:
        bit = 1
        while bit < sent_size:
            gram = gram + lax.ppermute(gram, "sent", [(s, s ^ bit) for s in range(sent_size)])
            bit *= 2
    else:
        gram = lax.psum(gram, "sent")
    if core_count == 2:
        other = lax.ppermute(gram, "col", [(0, 1), (1, 0)])
        gram = jnp.concatenate(
            [jnp.where(col_index == 0, gram, other), jnp.where(col_index == 0, other, gram)],
            axis=1,
        )
    else:
        gram = lax.all_gather(gram, "col", axis=1, tiled=True)
    updated = whiten(gram, merged, math.sqrt(total_rows))
    return (loadings, updated)


def solution(mesh):
    return jax.shard_map(
        shards,
        mesh=mesh,
        in_specs=(P("view", "sent", "col"), P("view"), P("view", "sent", "col"), P("sent", None)),
        out_specs=(P("view", "col", None), P("sent", None)),
        check_vma=False,
    )
```

```python
import functools
import math

import jax
import jax.numpy as jnp
from jax import lax
from jax.experimental import pallas as pl
from jax.experimental.pallas import tpu as pltpu
from jax.sharding import PartitionSpec as P

CHUNK = 256
LANES = 2
PANEL = 32


class Line:
    def __init__(self, lanes, sent_index, col_index):
        self.lanes, self.sent_index, self.col_index = lanes, sent_index, col_index
        self.inner = (sent_index == 1) | (sent_index == 2)
        self.slot, self.chunks, self.pairs, self.totals, self.finals = 0, {}, {}, {}, {}
        self.arrived = {}

    def pairs_of(self, k, stage):
        if k not in self.chunks:
            return []
        _, first, spread = self.chunks[k]
        always = lambda f: True
        if spread:
            hops = (
                {(0, 1): always, (3, 2): lambda f: f < 3},
                {(1, 2): always, (2, 1): lambda f: f <= 1},
                {(2, 3): always, (1, 0): lambda f: f <= 0},
            )
        else:
            hops = (
                {(3, 2): always, (0, 1): lambda f: f <= 0},
                {(2, 1): always, (1, 2): lambda f: f <= 1},
                {(1, 0): always, (2, 3): lambda f: f <= 2},
            )
        cores = len(first)
        return [
            (a * cores + c, b * cores + c)
            for c in range(cores)
            for (a, b), wanted in hops[stage].items()
            if wanted(first[c])
        ]

    def step(self, term=None, first=None, spread=None):
        k = self.slot
        self.slot += 1
        self.collect(k - self.lanes)
        middle, last = k - self.lanes, k - 2 * self.lanes
        if term is not None:
            self.chunks[k] = (term, first, spread)
        ends, pair = term, self.pairs.get(middle)
        if last in self.totals:
            total = self.totals[last]
            ends = total if term is None else jnp.where(self.inner, total, term)
        if ends is not None and pair is not None:
            ends, pair = lax.optimization_barrier((ends, pair))
        axes, ends_in, pair_in = ("sent", "col"), None, None
        if ends is not None:
            perm = self.pairs_of(k, 0) + self.pairs_of(last, 2)
            ends_in = lax.ppermute(ends, axes, perm)
        if pair is not None:
            pair_in = lax.ppermute(pair, axes, self.pairs_of(middle, 1))
        self.arrived[k] = (ends, ends_in, pair_in)

    def collect(self, k):
        if k not in self.arrived:
            return
        ends, ends_in, pair_in = self.arrived.pop(k)
        middle, last = k - self.lanes, k - 2 * self.lanes
        following = self.arrived.get(k + 1, (None,))[0] if self.lanes > 1 else None
        tied = [v for v in (following, ends_in, pair_in) if v is not None]
        tied = list(lax.optimization_barrier(tuple(tied)))
        if following is not None:
            del tied[0]
        if ends_in is not None:
            ends_in = tied.pop(0)
        if pair_in is not None:
            self.totals[middle] = self.pairs[middle] + tied.pop(0)
        if k in self.chunks:
            self.pairs[k] = self.chunks[k][0] + ends_in
        if last in self.totals:
            old, first, _ = self.chunks[last]
            alone = (self.sent_index == 3) & (self.col_index >= [f == 3 for f in first].index(True)) \
                if 3 in first else None
            outer = ends_in if alone is None else jnp.where(alone, ends_in + old, ends_in)
            self.finals[last] = jnp.where(self.inner, ends, outer)


def pieces(x):
    high = x.astype(jnp.bfloat16)
    rest = x - high.astype(jnp.float32)
    middle = rest.astype(jnp.bfloat16)
    return high, middle, (rest - middle.astype(jnp.float32)).astype(jnp.bfloat16)


def whiten_kernel(scale, gram_ref, merged_ref, out_ref, work):
    size = gram_ref.shape[0]
    tile = (8, 128)
    work[:, :size] = gram_ref[...]
    rows = lax.broadcasted_iota(jnp.int32, (size, size), 0)
    work[:, size:] = (rows == lax.broadcasted_iota(jnp.int32, (size, size), 1)).astype(jnp.float32)
    sublane = lax.broadcasted_iota(jnp.int32, tile, 0)
    for panel in range(0, size, PANEL):
        end = panel + PANEL
        start = panel // 128 * 128
        stop = size + start + 128
        for block in range(panel, end, 8):
            lanes = range(start, stop, 128)
            cols = [
                [
                    jnp.broadcast_to(
                        work[t : t + 8, start : start + 128][:, block - start + k][:, None], tile
                    )
                    for k in range(8)
                ]
                for t in range(block, end, 8)
            ]
            low = [
                [jnp.broadcast_to(cols[0][k][i : i + 1], tile) for k in range(i + 1)]
                for i in range(8)
            ]
            inverse = []
            for k in range(8):
                pivot = low[k][k]
                root = lax.rsqrt(pivot)
                root = root * (1.5 - 0.5 * pivot * root * root)
                inverse.append(root)
                for i in range(k + 1, 8):
                    low[i][k] = low[i][k] * root
                for i in range(k + 1, 8):
                    for m in range(k + 1, i + 1):
                        low[i][m] = low[i][m] - low[i][k] * low[m][k]
            for t in range(1, len(cols)):
                for k in range(8):
                    value = cols[t][k]
                    for m in range(k):
                        value = value - low[k][m] * cols[t][m]
                    cols[t][k] = value * inverse[k]
            for lane in lanes:
                here = slice(lane, lane + 128)
                old = work[block : block + 8, here]
                done, new = [], old
                for k in range(8):
                    value = jnp.broadcast_to(old[k : k + 1], tile)
                    for m in range(k):
                        value = value - low[k][m] * done[m]
                    done.append(value * inverse[k])
                    new = jnp.where(sublane == k, done[k], new)
                work[block : block + 8, here] = new
                for t in range(1, len(cols)):
                    at = slice(block + 8 * t, block + 8 * t + 8)
                    value = work[at, here]
                    for k in range(8):
                        value = value - cols[t][k] * done[k]
                    work[at, here] = value
        if end < size:
            first = end // 128 * 128
            upper = pieces(work[panel:end, first:size])
            right = pieces(work[panel:end, first:stop])
            a = jnp.concatenate([upper[i] for i in (0, 0, 1, 1, 0, 2)])
            b = jnp.concatenate([right[i] for i in (0, 1, 0, 1, 2, 0)])
            update = lax.dot_general(
                a, b, (((0,), (0,)), ((), ())), preferred_element_type=jnp.float32
            )
            work[end:, first:stop] -= update[end - first :]
    a = pieces(merged_ref[...])
    b = pieces(work[:, size:] * scale)
    total = 0.0
    for i, j in ((1, 1), (0, 2), (2, 0), (0, 1), (1, 0), (0, 0)):
        total += lax.dot_general(
            a[i], b[j], (((1,), (1,)), ((), ())), preferred_element_type=jnp.float32
        )
    out_ref[...] = total


def whiten(gram, merged, scale):
    size = gram.shape[0]
    return pl.pallas_call(
        functools.partial(whiten_kernel, scale),
        out_shape=jax.ShapeDtypeStruct(merged.shape, jnp.float32),
        in_specs=[pl.BlockSpec(memory_space=pltpu.VMEM)] * 2,
        out_specs=pl.BlockSpec(memory_space=pltpu.VMEM),
        scratch_shapes=[pltpu.VMEM((size, 2 * size), jnp.float32)],
        compiler_params=pltpu.CompilerParams(vmem_limit_bytes=32 * 2**20),
        name="whiten",
    )(gram, merged)


def shards(sketched, widths, inv_factor, shared):
    view_count, row_count, col_half = sketched.shape
    factor_rows = inv_factor.shape[1]
    sent_size = lax.axis_size("sent")
    view_size = lax.axis_size("view")
    core_count = lax.axis_size("col")
    total_rows = row_count * sent_size
    scale = 1.0 / math.sqrt(total_rows)
    high = lax.Precision.HIGH
    highest = lax.Precision.HIGHEST
    col_index = lax.axis_index("col")
    sent_index = lax.axis_index("sent")
    col_pos = col_index * col_half + jnp.arange(col_half)
    keep_cols = (col_pos[None, :] < widths[:, None]).astype(jnp.float32)[:, :, None]
    row_pos = sent_index * factor_rows + jnp.arange(factor_rows)
    keep_rows = (row_pos[None, :] < widths[:, None]).astype(jnp.float32)[:, :, None]
    use_line = sent_size == 4 and core_count == 2 and col_half % (2 * CHUNK) == 0

    chunk = CHUNK if use_line else col_half
    per_view = col_half // chunk
    order = [q + h for q in range(per_view // 2) for h in (0, per_view // 2)] or [0]
    back_order = sorted(range(per_view), key=order.__getitem__)
    slots = [(j, q) for j in range(view_count) for q in order]
    firsts = [
        [(c * col_half + q * chunk) // factor_rows for c in range(core_count)] for _, q in slots
    ]

    def keep_of(j, q):
        return keep_cols[j, q * chunk : (q + 1) * chunk]

    down = (((0,), (0,)), ((), ()))
    def first_half(proj, j):
        proj = jnp.concatenate([proj[at] for at in back_order])
        half_part = jnp.dot(inv_factor[j], proj, precision=high)
        if use_line:
            perm = [
                (s * 2 + c, s * 2 + 1 - c)
                for s in range(sent_size)
                for c in range(2)
                if (s + 1) * factor_rows > col_half
            ]
            half = half_part + lax.ppermute(half_part, ("sent", "col"), perm)
        else:
            half = lax.psum(half_part, "col")
        return half * keep_rows[j]

    def cut(whole):
        return [whole[q * chunk : (q + 1) * chunk] for q in order]

    def term_of(features):
        return scale * lax.dot_general(features, shared, down, preferred_element_type=jnp.float32)

    terms = []
    for j in range(view_count):
        terms += cut(term_of(sketched[j]))

    def back_terms(proj, j):
        return cut(
            lax.dot_general(
                inv_factor[j], first_half(proj, j), down, precision=high,
                preferred_element_type=jnp.float32,
            )
        )

    if use_line:
        line = Line(LANES, sent_index, col_index)
        for term, first in zip(terms, firsts):
            line.step(term, first, True)
        done = 0
        while done < len(slots):
            while done + per_view - 1 not in line.finals:
                line.step()
            proj = [line.finals[done + q] * keep_of(*slots[done + q]) for q in range(per_view)]
            for q, term in enumerate(back_terms(proj, slots[done][0])):
                line.step(term, firsts[q], False)
            done += per_view
        begin = line.slot - len(slots)
        for _ in range(3 * LANES):
            line.step()
        sums = [line.finals[begin + k] for k in range(len(slots))]
    else:
        sums = []
        for j in range(view_count):
            proj = [lax.psum(terms[j], "sent") * keep_of(j, 0)]
            sums += [lax.psum(t, "sent") for t in back_terms(proj, j)]
    loads = [total * keep_of(*slot) for total, slot in zip(sums, slots)]
    loads = [loads[j * per_view + at] for j in range(view_count) for at in back_order]
    loadings = jnp.concatenate(loads).reshape(view_count, col_half, -1)
    contrib = 0.0
    for j in range(view_count):
        whole = jnp.concatenate(loads[j * per_view : (j + 1) * per_view]).astype(jnp.bfloat16)
        contrib += jnp.dot(sketched[j], whole, preferred_element_type=jnp.float32)

    if view_size == 4 and core_count == 2:
        part_rows = row_count // 2
        near = lambda bit: [(v, v ^ bit) for v in range(view_size)]
        swap = [(0, 1), (1, 0)]
        mine = lax.dynamic_slice_in_dim(contrib, col_index * part_rows, part_rows)
        other = lax.dynamic_slice_in_dim(contrib, (1 - col_index) * part_rows, part_rows)
        mine = mine + lax.ppermute(other, "col", swap)
        upper, lower_part = mine[: part_rows // 2], mine[part_rows // 2 :]
        upper = upper + lax.ppermute(upper, "view", near(1))
        lower_part = lower_part + lax.ppermute(lower_part, "view", near(2))
        upper = upper + lax.ppermute(upper, "view", near(2))
        lower_part = lower_part + lax.ppermute(lower_part, "view", near(1))
        mine = jnp.concatenate([upper, lower_part])
        other = lax.ppermute(mine, "col", swap)
        merged = jnp.concatenate(
            [jnp.where(col_index == 0, mine, other), jnp.where(col_index == 0, other, mine)]
        )
        width = mine.shape[1] // 2
        gram = lax.dot_general(mine, mine, (((0,), (0,)), ((), ())), precision=highest)
        left, right = gram[:, :width], gram[:, width:]
        gram = jnp.where(col_index == 0, left, right)
        gram = gram + lax.ppermute(jnp.where(col_index == 0, right, left), "col", swap)
    else:
        merged = lax.psum(contrib, ("view", "col"))
        gram = lax.dot_general(merged, merged, (((0,), (0,)), ((), ())), precision=highest)
        width = gram.shape[1] // core_count
        gram = lax.dynamic_slice_in_dim(gram, col_index * width, width, axis=1)

    if sent_size & (sent_size - 1) == 0:
        bit = 1
        while bit < sent_size:
            gram = gram + lax.ppermute(gram, "sent", [(s, s ^ bit) for s in range(sent_size)])
            bit *= 2
    else:
        gram = lax.psum(gram, "sent")
    if core_count == 2:
        other = lax.ppermute(gram, "col", [(0, 1), (1, 0)])
        gram = jnp.concatenate(
            [jnp.where(col_index == 0, gram, other), jnp.where(col_index == 0, other, gram)],
            axis=1,
        )
    else:
        gram = lax.all_gather(gram, "col", axis=1, tiled=True)
    updated = whiten(gram, merged, math.sqrt(total_rows))
    return (loadings, updated)


def solution(mesh):
    return jax.shard_map(
        shards,
        mesh=mesh,
        in_specs=(P("view", "sent", "col"), P("view"), P("view", "sent", "col"), P("sent", None)),
        out_specs=(P("view", "col", None), P("sent", None)),
        check_vma=False,
    )
```

```python
import functools
import math

import jax
import jax.numpy as jnp
from jax import lax
from jax.experimental import pallas as pl
from jax.experimental.pallas import tpu as pltpu
from jax.sharding import PartitionSpec as P

CHUNK = 256
LANES = 2
PANEL = 32


class Line:
    def __init__(self, lanes, sent_index, col_index):
        self.lanes, self.sent_index, self.col_index = lanes, sent_index, col_index
        self.inner = (sent_index == 1) | (sent_index == 2)
        self.slot, self.chunks, self.pairs, self.totals, self.finals = 0, {}, {}, {}, {}
        self.arrived = {}

    def pairs_of(self, k, stage):
        if k not in self.chunks:
            return []
        _, first, spread = self.chunks[k]
        always = lambda f: True
        if spread:
            hops = (
                {(0, 1): always, (3, 2): lambda f: f < 3},
                {(1, 2): always, (2, 1): lambda f: f <= 1},
                {(2, 3): always, (1, 0): lambda f: f <= 0},
            )
        else:
            hops = (
                {(3, 2): always, (0, 1): lambda f: f <= 0},
                {(2, 1): always, (1, 2): lambda f: f <= 1},
                {(1, 0): always, (2, 3): lambda f: f <= 2},
            )
        cores = len(first)
        return [
            (a * cores + c, b * cores + c)
            for c in range(cores)
            for (a, b), wanted in hops[stage].items()
            if wanted(first[c])
        ]

    def step(self, term=None, first=None, spread=None):
        k = self.slot
        self.slot += 1
        self.collect(k - self.lanes)
        middle, last = k - self.lanes, k - 2 * self.lanes
        if term is not None:
            self.chunks[k] = (term, first, spread)
        ends, pair = term, self.pairs.get(middle)
        if last in self.totals:
            total = self.totals[last]
            ends = total if term is None else jnp.where(self.inner, total, term)
        if ends is not None and pair is not None:
            ends, pair = lax.optimization_barrier((ends, pair))
        axes, ends_in, pair_in = ("sent", "col"), None, None
        if ends is not None:
            perm = self.pairs_of(k, 0) + self.pairs_of(last, 2)
            ends_in = lax.ppermute(ends, axes, perm)
        if pair is not None:
            pair_in = lax.ppermute(pair, axes, self.pairs_of(middle, 1))
        self.arrived[k] = (ends, ends_in, pair_in)

    def collect(self, k):
        if k not in self.arrived:
            return
        ends, ends_in, pair_in = self.arrived.pop(k)
        middle, last = k - self.lanes, k - 2 * self.lanes
        following = self.arrived.get(k + 1, (None,))[0] if self.lanes > 1 else None
        tied = [v for v in (following, ends_in, pair_in) if v is not None]
        tied = list(lax.optimization_barrier(tuple(tied)))
        if following is not None:
            del tied[0]
        if ends_in is not None:
            ends_in = tied.pop(0)
        if pair_in is not None:
            self.totals[middle] = self.pairs[middle] + tied.pop(0)
        if k in self.chunks:
            self.pairs[k] = self.chunks[k][0] + ends_in
        if last in self.totals:
            old, first, _ = self.chunks[last]
            alone = (self.sent_index == 3) & (self.col_index >= [f == 3 for f in first].index(True)) \
                if 3 in first else None
            outer = ends_in if alone is None else jnp.where(alone, ends_in + old, ends_in)
            self.finals[last] = jnp.where(self.inner, ends, outer)


def pieces(x):
    high = x.astype(jnp.bfloat16)
    rest = x - high.astype(jnp.float32)
    middle = rest.astype(jnp.bfloat16)
    return high, middle, (rest - middle.astype(jnp.float32)).astype(jnp.bfloat16)


def whiten_kernel(scale, gram_ref, merged_ref, out_ref, work):
    size = gram_ref.shape[0]
    tile = (8, 128)
    work[:, :size] = gram_ref[...]
    rows = lax.broadcasted_iota(jnp.int32, (size, size), 0)
    work[:, size:] = (rows == lax.broadcasted_iota(jnp.int32, (size, size), 1)).astype(jnp.float32)
    sublane = lax.broadcasted_iota(jnp.int32, tile, 0)
    for panel in range(0, size, PANEL):
        end = panel + PANEL
        start = panel // 128 * 128
        stop = size + start + 128
        for block in range(panel, end, 8):
            lanes = range(start, stop, 128)
            cols = [
                [
                    jnp.broadcast_to(
                        work[t : t + 8, start : start + 128][:, block - start + k][:, None], tile
                    )
                    for k in range(8)
                ]
                for t in range(block, end, 8)
            ]
            low = [
                [jnp.broadcast_to(cols[0][k][i : i + 1], tile) for k in range(i + 1)]
                for i in range(8)
            ]
            inverse = []
            for k in range(8):
                pivot = low[k][k]
                root = lax.rsqrt(pivot)
                root = root * (1.5 - 0.5 * pivot * root * root)
                inverse.append(root)
                for i in range(k + 1, 8):
                    low[i][k] = low[i][k] * root
                for i in range(k + 1, 8):
                    for m in range(k + 1, i + 1):
                        low[i][m] = low[i][m] - low[i][k] * low[m][k]
            for t in range(1, len(cols)):
                for k in range(8):
                    value = cols[t][k]
                    for m in range(k):
                        value = value - low[k][m] * cols[t][m]
                    cols[t][k] = value * inverse[k]
            for lane in lanes:
                here = slice(lane, lane + 128)
                old = work[block : block + 8, here]
                done, new = [], old
                for k in range(8):
                    value = jnp.broadcast_to(old[k : k + 1], tile)
                    for m in range(k):
                        value = value - low[k][m] * done[m]
                    done.append(value * inverse[k])
                    new = jnp.where(sublane == k, done[k], new)
                work[block : block + 8, here] = new
                for t in range(1, len(cols)):
                    at = slice(block + 8 * t, block + 8 * t + 8)
                    value = work[at, here]
                    for k in range(8):
                        value = value - cols[t][k] * done[k]
                    work[at, here] = value
        if end < size:
            first = end // 128 * 128
            upper = pieces(work[panel:end, first:size])
            right = pieces(work[panel:end, first:stop])
            a = jnp.concatenate([upper[i] for i in (0, 0, 1, 1, 0, 2)])
            b = jnp.concatenate([right[i] for i in (0, 1, 0, 1, 2, 0)])
            update = lax.dot_general(
                a, b, (((0,), (0,)), ((), ())), preferred_element_type=jnp.float32
            )
            work[end:, first:stop] -= update[end - first :]
    a = pieces(merged_ref[...])
    b = pieces(work[:, size:] * scale)
    total = 0.0
    for i, j in ((1, 1), (0, 2), (2, 0), (0, 1), (1, 0), (0, 0)):
        total += lax.dot_general(
            a[i], b[j], (((1,), (1,)), ((), ())), preferred_element_type=jnp.float32
        )
    out_ref[...] = total


def whiten(gram, merged, scale):
    size = gram.shape[0]
    return pl.pallas_call(
        functools.partial(whiten_kernel, scale),
        out_shape=jax.ShapeDtypeStruct(merged.shape, jnp.float32),
        in_specs=[pl.BlockSpec(memory_space=pltpu.VMEM)] * 2,
        out_specs=pl.BlockSpec(memory_space=pltpu.VMEM),
        scratch_shapes=[pltpu.VMEM((size, 2 * size), jnp.float32)],
        compiler_params=pltpu.CompilerParams(vmem_limit_bytes=32 * 2**20),
        name="whiten",
    )(gram, merged)


def shards(sketched, widths, inv_factor, shared):
    view_count, row_count, col_half = sketched.shape
    factor_rows = inv_factor.shape[1]
    sent_size = lax.axis_size("sent")
    view_size = lax.axis_size("view")
    core_count = lax.axis_size("col")
    total_rows = row_count * sent_size
    scale = 1.0 / math.sqrt(total_rows)
    high = lax.Precision.HIGH
    highest = lax.Precision.HIGHEST
    col_index = lax.axis_index("col")
    sent_index = lax.axis_index("sent")
    col_pos = col_index * col_half + jnp.arange(col_half)
    keep_cols = (col_pos[None, :] < widths[:, None]).astype(jnp.float32)[:, :, None]
    row_pos = sent_index * factor_rows + jnp.arange(factor_rows)
    keep_rows = (row_pos[None, :] < widths[:, None]).astype(jnp.float32)[:, :, None]
    use_line = sent_size == 4 and core_count == 2 and col_half % (2 * CHUNK) == 0

    chunk = CHUNK if use_line else col_half
    per_view = col_half // chunk
    order = [q + h for q in range(per_view // 2) for h in (per_view // 2, 0)] or [0]
    back_order = sorted(range(per_view), key=order.__getitem__)
    slots = [(j, q) for j in range(view_count) for q in order]
    firsts = [
        [(c * col_half + q * chunk) // factor_rows for c in range(core_count)] for _, q in slots
    ]

    def keep_of(j, q):
        return keep_cols[j, q * chunk : (q + 1) * chunk]

    down = (((0,), (0,)), ((), ()))
    def first_half(proj, j):
        proj = jnp.concatenate([proj[at] for at in back_order])
        half_part = jnp.dot(inv_factor[j], proj, precision=high)
        if use_line:
            perm = [
                (s * 2 + c, s * 2 + 1 - c)
                for s in range(sent_size)
                for c in range(2)
                if (s + 1) * factor_rows > col_half
            ]
            half = half_part + lax.ppermute(half_part, ("sent", "col"), perm)
        else:
            half = lax.psum(half_part, "col")
        return half * keep_rows[j]

    def cut(whole):
        return [whole[q * chunk : (q + 1) * chunk] for q in order]

    def term_of(features):
        return scale * lax.dot_general(features, shared, down, preferred_element_type=jnp.float32)

    terms = []
    for j in range(view_count):
        terms += cut(term_of(sketched[j]))

    def back_terms(proj, j):
        return cut(
            lax.dot_general(
                inv_factor[j], first_half(proj, j), down, precision=high,
                preferred_element_type=jnp.float32,
            )
        )

    if use_line:
        line = Line(LANES, sent_index, col_index)
        for term, first in zip(terms, firsts):
            line.step(term, first, True)
        done = 0
        while done < len(slots):
            while done + per_view - 1 not in line.finals:
                line.step()
            proj = [line.finals[done + q] * keep_of(*slots[done + q]) for q in range(per_view)]
            for q, term in enumerate(back_terms(proj, slots[done][0])):
                line.step(term, firsts[q], False)
            done += per_view
        begin = line.slot - len(slots)
        for _ in range(3 * LANES):
            line.step()
        sums = [line.finals[begin + k] for k in range(len(slots))]
    else:
        sums = []
        for j in range(view_count):
            proj = [lax.psum(terms[j], "sent") * keep_of(j, 0)]
            sums += [lax.psum(t, "sent") for t in back_terms(proj, j)]
    loads = [total * keep_of(*slot) for total, slot in zip(sums, slots)]
    loads = [loads[j * per_view + at] for j in range(view_count) for at in back_order]
    loadings = jnp.concatenate(loads).reshape(view_count, col_half, -1)
    contrib = 0.0
    for j in range(view_count):
        whole = jnp.concatenate(loads[j * per_view : (j + 1) * per_view]).astype(jnp.bfloat16)
        contrib += jnp.dot(sketched[j], whole, preferred_element_type=jnp.float32)

    if view_size == 4 and core_count == 2:
        part_rows = row_count // 2
        near = lambda bit: [(v, v ^ bit) for v in range(view_size)]
        swap = [(0, 1), (1, 0)]
        mine = lax.dynamic_slice_in_dim(contrib, col_index * part_rows, part_rows)
        other = lax.dynamic_slice_in_dim(contrib, (1 - col_index) * part_rows, part_rows)
        mine = mine + lax.ppermute(other, "col", swap)
        upper, lower_part = mine[: part_rows // 2], mine[part_rows // 2 :]
        upper = upper + lax.ppermute(upper, "view", near(1))
        lower_part = lower_part + lax.ppermute(lower_part, "view", near(2))
        upper = upper + lax.ppermute(upper, "view", near(2))
        lower_part = lower_part + lax.ppermute(lower_part, "view", near(1))
        mine = jnp.concatenate([upper, lower_part])
        other = lax.ppermute(mine, "col", swap)
        merged = jnp.concatenate(
            [jnp.where(col_index == 0, mine, other), jnp.where(col_index == 0, other, mine)]
        )
        width = mine.shape[1] // 2
        gram = lax.dot_general(mine, mine, (((0,), (0,)), ((), ())), precision=highest)
        left, right = gram[:, :width], gram[:, width:]
        gram = jnp.where(col_index == 0, left, right)
        gram = gram + lax.ppermute(jnp.where(col_index == 0, right, left), "col", swap)
    else:
        merged = lax.psum(contrib, ("view", "col"))
        gram = lax.dot_general(merged, merged, (((0,), (0,)), ((), ())), precision=highest)
        width = gram.shape[1] // core_count
        gram = lax.dynamic_slice_in_dim(gram, col_index * width, width, axis=1)

    if sent_size & (sent_size - 1) == 0:
        bit = 1
        while bit < sent_size:
            gram = gram + lax.ppermute(gram, "sent", [(s, s ^ bit) for s in range(sent_size)])
            bit *= 2
    else:
        gram = lax.psum(gram, "sent")
    if core_count == 2:
        other = lax.ppermute(gram, "col", [(0, 1), (1, 0)])
        gram = jnp.concatenate(
            [jnp.where(col_index == 0, gram, other), jnp.where(col_index == 0, other, gram)],
            axis=1,
        )
    else:
        gram = lax.all_gather(gram, "col", axis=1, tiled=True)
    updated = whiten(gram, merged, math.sqrt(total_rows))
    return (loadings, updated)


def solution(mesh):
    return jax.shard_map(
        shards,
        mesh=mesh,
        in_specs=(P("view", "sent", "col"), P("view"), P("view", "sent", "col"), P("sent", None)),
        out_specs=(P("view", "col", None), P("sent", None)),
        check_vma=False,
    )
```

```python
import functools
import math

import jax
import jax.numpy as jnp
from jax import lax
from jax.experimental import pallas as pl
from jax.experimental.pallas import tpu as pltpu
from jax.sharding import PartitionSpec as P

CHUNK = 256
LANES = 2
PANEL = 32


class Line:
    def __init__(self, lanes, sent_index, col_index):
        self.lanes, self.sent_index, self.col_index = lanes, sent_index, col_index
        self.inner = (sent_index == 1) | (sent_index == 2)
        self.slot, self.chunks, self.pairs, self.totals, self.finals = 0, {}, {}, {}, {}
        self.arrived = {}

    def pairs_of(self, k, stage):
        if k not in self.chunks:
            return []
        _, first, spread = self.chunks[k]
        always = lambda f: True
        if spread:
            hops = (
                {(0, 1): always, (3, 2): lambda f: f < 3},
                {(1, 2): always, (2, 1): lambda f: f <= 1},
                {(2, 3): always, (1, 0): lambda f: f <= 0},
            )
        else:
            hops = (
                {(3, 2): always, (0, 1): lambda f: f <= 0},
                {(2, 1): always, (1, 2): lambda f: f <= 1},
                {(1, 0): always, (2, 3): lambda f: f <= 2},
            )
        cores = len(first)
        return [
            (a * cores + c, b * cores + c)
            for c in range(cores)
            for (a, b), wanted in hops[stage].items()
            if wanted(first[c])
        ]

    def step(self, term=None, first=None, spread=None):
        k = self.slot
        self.slot += 1
        self.collect(k - self.lanes)
        middle, last = k - self.lanes, k - 2 * self.lanes
        if term is not None:
            self.chunks[k] = (term, first, spread)
        ends, pair = term, self.pairs.get(middle)
        if last in self.totals:
            total = self.totals[last]
            ends = total if term is None else jnp.where(self.inner, total, term)
        if ends is not None and pair is not None:
            ends, pair = lax.optimization_barrier((ends, pair))
        axes, ends_in, pair_in = ("sent", "col"), None, None
        if ends is not None:
            perm = self.pairs_of(k, 0) + self.pairs_of(last, 2)
            ends_in = lax.ppermute(ends, axes, perm)
        if pair is not None:
            pair_in = lax.ppermute(pair, axes, self.pairs_of(middle, 1))
        self.arrived[k] = (ends, ends_in, pair_in)

    def collect(self, k):
        if k not in self.arrived:
            return
        ends, ends_in, pair_in = self.arrived.pop(k)
        middle, last = k - self.lanes, k - 2 * self.lanes
        following = self.arrived.get(k + 1, (None,))[0] if self.lanes > 1 else None
        tied = [v for v in (following, ends_in, pair_in) if v is not None]
        tied = list(lax.optimization_barrier(tuple(tied)))
        if following is not None:
            del tied[0]
        if ends_in is not None:
            ends_in = tied.pop(0)
        if pair_in is not None:
            self.totals[middle] = self.pairs[middle] + tied.pop(0)
        if k in self.chunks:
            self.pairs[k] = self.chunks[k][0] + ends_in
        if last in self.totals:
            old, first, _ = self.chunks[last]
            alone = (self.sent_index == 3) & (self.col_index >= [f == 3 for f in first].index(True)) \
                if 3 in first else None
            outer = ends_in if alone is None else jnp.where(alone, ends_in + old, ends_in)
            self.finals[last] = jnp.where(self.inner, ends, outer)


def pieces(x):
    high = x.astype(jnp.bfloat16)
    rest = x - high.astype(jnp.float32)
    middle = rest.astype(jnp.bfloat16)
    return high, middle, (rest - middle.astype(jnp.float32)).astype(jnp.bfloat16)


def whiten_kernel(scale, gram_ref, merged_ref, out_ref, work):
    size = gram_ref.shape[0]
    tile = (8, 128)
    work[:, :size] = gram_ref[...]
    rows = lax.broadcasted_iota(jnp.int32, (size, size), 0)
    work[:, size:] = (rows == lax.broadcasted_iota(jnp.int32, (size, size), 1)).astype(jnp.float32)
    sublane = lax.broadcasted_iota(jnp.int32, tile, 0)
    for panel in range(0, size, PANEL):
        end = panel + PANEL
        start = panel // 128 * 128
        stop = size + start + 128
        for block in range(panel, end, 8):
            lanes = range(start, stop, 128)
            cols = [
                [
                    jnp.broadcast_to(
                        work[t : t + 8, start : start + 128][:, block - start + k][:, None], tile
                    )
                    for k in range(8)
                ]
                for t in range(block, end, 8)
            ]
            low = [
                [jnp.broadcast_to(cols[0][k][i : i + 1], tile) for k in range(i + 1)]
                for i in range(8)
            ]
            inverse = []
            for k in range(8):
                pivot = low[k][k]
                root = lax.rsqrt(pivot)
                root = root * (1.5 - 0.5 * pivot * root * root)
                inverse.append(root)
                for i in range(k + 1, 8):
                    low[i][k] = low[i][k] * root
                for i in range(k + 1, 8):
                    for m in range(k + 1, i + 1):
                        low[i][m] = low[i][m] - low[i][k] * low[m][k]
            for t in range(1, len(cols)):
                for k in range(8):
                    value = cols[t][k]
                    for m in range(k):
                        value = value - low[k][m] * cols[t][m]
                    cols[t][k] = value * inverse[k]
            for lane in lanes:
                here = slice(lane, lane + 128)
                old = work[block : block + 8, here]
                done, new = [], old
                for k in range(8):
                    value = jnp.broadcast_to(old[k : k + 1], tile)
                    for m in range(k):
                        value = value - low[k][m] * done[m]
                    done.append(value * inverse[k])
                    new = jnp.where(sublane == k, done[k], new)
                work[block : block + 8, here] = new
                for t in range(1, len(cols)):
                    at = slice(block + 8 * t, block + 8 * t + 8)
                    value = work[at, here]
                    for k in range(8):
                        value = value - cols[t][k] * done[k]
                    work[at, here] = value
        if end < size:
            first = end // 128 * 128
            upper = pieces(work[panel:end, first:size])
            right = pieces(work[panel:end, first:stop])
            a = jnp.concatenate([upper[i] for i in (0, 0, 1, 1, 0, 2)])
            b = jnp.concatenate([right[i] for i in (0, 1, 0, 1, 2, 0)])
            update = lax.dot_general(
                a, b, (((0,), (0,)), ((), ())), preferred_element_type=jnp.float32
            )
            work[end:, first:stop] -= update[end - first :]
    a = pieces(merged_ref[...])
    b = pieces(work[:, size:] * scale)
    total = 0.0
    for i, j in ((1, 1), (0, 2), (2, 0), (0, 1), (1, 0), (0, 0)):
        total += lax.dot_general(
            a[i], b[j], (((1,), (1,)), ((), ())), preferred_element_type=jnp.float32
        )
    out_ref[...] = total


def whiten(gram, merged, scale):
    size = gram.shape[0]
    return pl.pallas_call(
        functools.partial(whiten_kernel, scale),
        out_shape=jax.ShapeDtypeStruct(merged.shape, jnp.float32),
        in_specs=[pl.BlockSpec(memory_space=pltpu.VMEM)] * 2,
        out_specs=pl.BlockSpec(memory_space=pltpu.VMEM),
        scratch_shapes=[pltpu.VMEM((size, 2 * size), jnp.float32)],
        compiler_params=pltpu.CompilerParams(vmem_limit_bytes=32 * 2**20),
        name="whiten",
    )(gram, merged)


def shards(sketched, widths, inv_factor, shared):
    view_count, row_count, col_half = sketched.shape
    factor_rows = inv_factor.shape[1]
    sent_size = lax.axis_size("sent")
    view_size = lax.axis_size("view")
    core_count = lax.axis_size("col")
    total_rows = row_count * sent_size
    scale = 1.0 / math.sqrt(total_rows)
    high = lax.Precision.HIGH
    highest = lax.Precision.HIGHEST
    col_index = lax.axis_index("col")
    sent_index = lax.axis_index("sent")
    col_pos = col_index * col_half + jnp.arange(col_half)
    keep_cols = (col_pos[None, :] < widths[:, None]).astype(jnp.float32)[:, :, None]
    row_pos = sent_index * factor_rows + jnp.arange(factor_rows)
    keep_rows = (row_pos[None, :] < widths[:, None]).astype(jnp.float32)[:, :, None]
    use_line = sent_size == 4 and core_count == 2 and col_half % (2 * CHUNK) == 0

    chunk = CHUNK if use_line else col_half
    per_view = col_half // chunk
    order = [q + h for q in range(per_view // 2) for h in (per_view // 2, 0)] or [0]
    back_order = sorted(range(per_view), key=order.__getitem__)
    slots = [(j, q) for j in range(view_count) for q in order]
    firsts = [
        [(c * col_half + q * chunk) // factor_rows for c in range(core_count)] for _, q in slots
    ]

    def keep_of(j, q):
        return keep_cols[j, q * chunk : (q + 1) * chunk]

    down = (((0,), (0,)), ((), ()))
    def first_half(proj, j):
        proj = jnp.concatenate([proj[at] for at in back_order])
        half_part = jnp.dot(inv_factor[j], proj, precision=high)
        if use_line:
            perm = [
                (s * 2 + c, s * 2 + 1 - c)
                for s in range(sent_size)
                for c in range(2)
                if (s + 1) * factor_rows > col_half
            ]
            half = half_part + lax.ppermute(half_part, ("sent", "col"), perm)
        else:
            half = lax.psum(half_part, "col")
        return half * keep_rows[j]

    def cut(whole):
        return [whole[q * chunk : (q + 1) * chunk] for q in order]

    def term_of(features):
        return scale * lax.dot_general(features, shared, down, preferred_element_type=jnp.float32)

    terms = []
    for j in range(view_count):
        terms += cut(term_of(sketched[j]))

    def back_terms(proj, j):
        return cut(
            lax.dot_general(
                inv_factor[j], first_half(proj, j), down, precision=high,
                preferred_element_type=jnp.float32,
            )
        )

    if use_line:
        line = Line(LANES, sent_index, col_index)
        count, cut_at = len(slots), len(slots) - per_view // 2
        plan = [(True, k) for k in range(cut_at)]
        for k in range(count):
            if k < count - cut_at:
                plan += [(True, cut_at + k)]
            plan += [(False, k)]
        backs, begun = [], {}
        for spread, k in plan:
            if not spread and k == len(backs):
                while any(begun[k + q] not in line.finals for q in range(per_view)):
                    line.step()
                proj = [line.finals[begun[k + q]] * keep_of(*slots[k + q]) for q in range(per_view)]
                backs += back_terms(proj, slots[k][0])
            begun[k if spread else count + k] = line.slot
            line.step(terms[k] if spread else backs[k], firsts[k], spread)
        for _ in range(3 * LANES):
            line.step()
        sums = [line.finals[begun[count + k]] for k in range(count)]
    else:
        sums = []
        for j in range(view_count):
            proj = [lax.psum(terms[j], "sent") * keep_of(j, 0)]
            sums += [lax.psum(t, "sent") for t in back_terms(proj, j)]
    loads = [total * keep_of(*slot) for total, slot in zip(sums, slots)]
    loads = [loads[j * per_view + at] for j in range(view_count) for at in back_order]
    loadings = jnp.concatenate(loads).reshape(view_count, col_half, -1)
    contrib = 0.0
    for j in range(view_count):
        whole = jnp.concatenate(loads[j * per_view : (j + 1) * per_view]).astype(jnp.bfloat16)
        contrib += jnp.dot(sketched[j], whole, preferred_element_type=jnp.float32)

    if view_size == 4 and core_count == 2:
        part_rows = row_count // 2
        near = lambda bit: [(v, v ^ bit) for v in range(view_size)]
        swap = [(0, 1), (1, 0)]
        mine = lax.dynamic_slice_in_dim(contrib, col_index * part_rows, part_rows)
        other = lax.dynamic_slice_in_dim(contrib, (1 - col_index) * part_rows, part_rows)
        mine = mine + lax.ppermute(other, "col", swap)
        upper, lower_part = mine[: part_rows // 2], mine[part_rows // 2 :]
        upper = upper + lax.ppermute(upper, "view", near(1))
        lower_part = lower_part + lax.ppermute(lower_part, "view", near(2))
        upper = upper + lax.ppermute(upper, "view", near(2))
        lower_part = lower_part + lax.ppermute(lower_part, "view", near(1))
        mine = jnp.concatenate([upper, lower_part])
        other = lax.ppermute(mine, "col", swap)
        merged = jnp.concatenate(
            [jnp.where(col_index == 0, mine, other), jnp.where(col_index == 0, other, mine)]
        )
        width = mine.shape[1] // 2
        gram = lax.dot_general(mine, mine, (((0,), (0,)), ((), ())), precision=highest)
        left, right = gram[:, :width], gram[:, width:]
        gram = jnp.where(col_index == 0, left, right)
        gram = gram + lax.ppermute(jnp.where(col_index == 0, right, left), "col", swap)
    else:
        merged = lax.psum(contrib, ("view", "col"))
        gram = lax.dot_general(merged, merged, (((0,), (0,)), ((), ())), precision=highest)
        width = gram.shape[1] // core_count
        gram = lax.dynamic_slice_in_dim(gram, col_index * width, width, axis=1)

    if sent_size & (sent_size - 1) == 0:
        bit = 1
        while bit < sent_size:
            gram = gram + lax.ppermute(gram, "sent", [(s, s ^ bit) for s in range(sent_size)])
            bit *= 2
    else:
        gram = lax.psum(gram, "sent")
    if core_count == 2:
        other = lax.ppermute(gram, "col", [(0, 1), (1, 0)])
        gram = jnp.concatenate(
            [jnp.where(col_index == 0, gram, other), jnp.where(col_index == 0, other, gram)],
            axis=1,
        )
    else:
        gram = lax.all_gather(gram, "col", axis=1, tiled=True)
    updated = whiten(gram, merged, math.sqrt(total_rows))
    return (loadings, updated)


def solution(mesh):
    return jax.shard_map(
        shards,
        mesh=mesh,
        in_specs=(P("view", "sent", "col"), P("view"), P("view", "sent", "col"), P("sent", None)),
        out_specs=(P("view", "col", None), P("sent", None)),
        check_vma=False,
    )
```
